32 devices in a mesh: wide: 8 (over y, x, core), narrow: 4 (over z).
Axes of the slice: x: 2, y: 2, z: 4, core: 2. Of those that a mesh axis runs over, the one named last changes fastest.
Arguments:
- series: float32 [512, 512], P(('wide', 'narrow')), may hold values from -18 to 18
- flags: int32 [512, 512], P(('wide', 'narrow')), may hold values from 0 to 1, as said below
- lengths: int32 [512], P(('wide', 'narrow')), may hold values from 1 to 16, as said below
- lift_weight: bfloat16 [64, 1280], replicated, may hold values from -0.75 to 0.75
- mix_weight: bfloat16 [1280, 1280], replicated, may hold values from -0.15625 to 0.15625
- skip_weight: bfloat16 [64, 1280], replicated, may hold values from -0.75 to 0.75
- gain_first: float32 [1280], replicated, may hold values from 0.5 to 1.5
- joint_weight: bfloat16 [1280, 3840], replicated, may hold values from -0.15625 to 0.15625
- merge_weight: bfloat16 [1280, 1280], replicated, may hold values from -0.5 to 0.5
- gain_second: float32 [1280], replicated, may hold values from 0.5 to 1.5
- grow_weight: bfloat16 [1280, 1280], replicated, may hold values from -0.15625 to 0.15625
- shrink_weight: bfloat16 [1280, 1280], replicated, may hold values from -0.15625 to 0.15625
- head_weight: bfloat16 [1280, 128], replicated, may hold values from -0.15625 to 0.15625
- cotangent: float32 [512, 16, 128], P(('wide', 'narrow')), may hold values from -6 to 6
Outputs:
- predictions: float32 [512, 16, 128], P(('wide', 'narrow'))
- series_grad: float32 [512, 512], P(('wide', 'narrow'))
- lift_grad: float32 [64, 1280], P(None, ('wide', 'narrow'))
- mix_grad: float32 [1280, 1280], P(('wide', 'narrow'))
- skip_grad: float32 [64, 1280], P(None, ('wide', 'narrow'))
- first_grad: float32 [1280], P(('wide', 'narrow'))
- joint_grad: float32 [1280, 3840], P(('wide', 'narrow'))
- merge_grad: float32 [1280, 1280], P(('wide', 'narrow'))
- second_grad: float32 [1280], P(('wide', 'narrow'))
- grow_grad: float32 [1280, 1280], P(('wide', 'narrow'))
- shrink_grad: float32 [1280, 1280], P(None, ('wide', 'narrow'))
- head_grad: float32 [1280, 128], P(('wide', 'narrow'))
The draws below stay inside these ranges and needn't reach their ends.
Inputs may be any that keep to these rules, and one draw needn't show every extreme that they name: `lengths`: each series ends in its real patches; patch p of a series is real when p >= 16 - length. Some series of every draw has all 16. `flags`: 1 marks a missing time point. In some series of every draw every point of the first real patch is missing.
All inputs are finite; a program needn't handle non-finite values.
Results may differ from the reference program's by a relative error of at most 0.014.
Values sent between devices are 32-bit elements; how exact they have to be, the bound alone decides.
No kernel may reach another device: no remote copies, remote signals or barrier semaphores. Data moves between devices by JAX's collectives and lax.ppermute only.
A program may use at most 256 MiB of HBM per device.

```python
import math
import jax
import jax.numpy as jnp
from jax import lax

D = 1280
HEADS = 16
HEAD_DIM = 80
FF = 1280
WINDOW_STEPS = 32
AHEAD_STEPS = 128
WINDOWS_IN_TRACE = 16
TRACE_COUNT = 512


def common_lengths(key):
    shared_key = jax.random.fold_in(key, 23)
    key_draw, key_pick = jax.random.split(shared_key)
    drawn_lengths = jax.random.randint(key_draw, (TRACE_COUNT,), 1, WINDOWS_IN_TRACE + 1)
    chosen = jax.random.randint(key_pick, (), 0, TRACE_COUNT)
    return jnp.where(jnp.arange(TRACE_COUNT) == chosen, WINDOWS_IN_TRACE, drawn_lengths).astype(jnp.int32)


def draw_series(key, part):
    key = jax.random.fold_in(key, 11)
    subkeys = jax.random.split(key, 3)
    levels = jax.random.uniform(subkeys[0], (TRACE_COUNT, 1), jnp.float32, -2.0, 2.0)
    scales = jnp.exp(jax.random.uniform(subkeys[1], (TRACE_COUNT, 1), jnp.float32, math.log(0.3), math.log(4.0)))
    jitter = jnp.clip(jax.random.normal(subkeys[2], (TRACE_COUNT, WINDOWS_IN_TRACE * WINDOW_STEPS), jnp.float32), -4.0, 4.0)
    return levels + scales * jitter


def draw_lengths(key, part):
    return common_lengths(key)


def draw_flags(key, part):
    series_lengths = common_lengths(key)
    key = jax.random.fold_in(key, 37)
    key_base, key_wipe = jax.random.split(key)
    base_flags = (jax.random.randint(key_base, (TRACE_COUNT, WINDOWS_IN_TRACE * WINDOW_STEPS), 0, 8) == 0).astype(jnp.int32)
    wiped_count = max(TRACE_COUNT // 2048, 1)
    order = jax.random.permutation(key_wipe, TRACE_COUNT)
    rank_of = jnp.argsort(order)
    wiped_rows = rank_of < wiped_count
    patch_index = jnp.arange(WINDOWS_IN_TRACE * WINDOW_STEPS, dtype=jnp.int32) // WINDOW_STEPS
    first_real = (WINDOWS_IN_TRACE - series_lengths).astype(jnp.int32)
    wiped_points = wiped_rows[:, None] & (patch_index[None, :] == first_real[:, None])
    return jnp.where(wiped_points, 1, base_flags).astype(jnp.int32)


def block_levels(stream_key, dims, shards, low, largest):
    level = 1.0
    for axis_at, shards_of in shards:
        draws = jax.random.uniform(jax.random.fold_in(jax.random.fold_in(stream_key, 6), axis_at), (shards_of,), jnp.float32, low / len(shards), largest / len(shards))
        level = level * jnp.repeat(jnp.exp(draws), dims[axis_at] // shards_of).reshape((-1,) + (1,) * (len(dims) - 1 - axis_at))
    return level


def gaussian(rng, dims, scale, reach, shards=(), kind=jnp.bfloat16):
    level = block_levels(rng, dims, shards, -0.22, 0.18) if shards else 1.0
    drawn = jax.random.normal(rng, dims, jnp.float32) * scale * level
    return jnp.minimum(jnp.maximum(drawn, -reach), reach).astype(kind)


def setup_inputs(seed: int = 0) -> dict:
    streams_of = jax.random.split(jax.random.key(seed), 15)
    return {
        "series": draw_series(jax.random.fold_in(streams_of[14], 71), 0),
        "flags": draw_flags(jax.random.fold_in(streams_of[14], 71), 0),
        "lengths": draw_lengths(jax.random.fold_in(streams_of[14], 71), 0),
        "lift_weight": gaussian(streams_of[3], (2 * WINDOW_STEPS, D), (2 * WINDOW_STEPS) ** -0.5, 0.75),
        "mix_weight": gaussian(streams_of[4], (D, D), D ** -0.5, 0.15625),
        "skip_weight": gaussian(streams_of[5], (2 * WINDOW_STEPS, D), (2 * WINDOW_STEPS) ** -0.5, 0.75),
        "gain_first": jnp.clip(1.0 + 0.1 * jax.random.normal(streams_of[6], (D,), jnp.float32), 0.5, 1.5),
        "joint_weight": gaussian(streams_of[7], (D, 3 * D), D ** -0.5, 0.15625),
        "merge_weight": gaussian(streams_of[8], (D, D), (2 * D // WINDOWS_IN_TRACE) ** -0.5, 0.5),
        "gain_second": jnp.clip(1.0 + 0.1 * jax.random.normal(streams_of[9], (D,), jnp.float32), 0.5, 1.5),
        "grow_weight": gaussian(streams_of[10], (D, FF), D ** -0.5, 0.15625),
        "shrink_weight": gaussian(streams_of[11], (FF, D), FF ** -0.5, 0.15625),
        "head_weight": gaussian(streams_of[12], (D, AHEAD_STEPS), D ** -0.5, 0.15625),
        "cotangent": gaussian(streams_of[13], (TRACE_COUNT, WINDOWS_IN_TRACE, AHEAD_STEPS), 1.0, 6.0, ((0, 32),), jnp.float32),
    }


@jax.custom_vjp
def low(v):
    return lax.optimization_barrier(v.astype(jnp.bfloat16)).astype(jnp.float32)

@jax.custom_vjp
def low_back(v):
    return v

def low_keep(v):
    return (low(v), None)

def low_pass(kept, grad):
    return (grad,)

def back_keep(v):
    return (v, None)

def back_low(kept, grad):
    return (low(grad),)
low.defvjp(low_keep, low_pass)
low_back.defvjp(back_keep, back_low)
precise = lax.Precision.HIGHEST
epsilon = 1e-06
masked_value = -1000000000.0

def matmul(left_side, right_side):
    return jnp.matmul(left_side, right_side, precision=precise)

def rms_scale(values, gain_vector):
    return values * lax.rsqrt(lax.optimization_barrier(jnp.mean(values * values, axis=-1, keepdims=True)) + epsilon) * gain_vector

def rotary_tables(patches, head_dim):
    positions = jnp.arange(patches, dtype=jnp.int32).astype(jnp.float32)
    exponent = jnp.arange(head_dim // 2, dtype=jnp.int32).astype(jnp.float32) * (2.0 / head_dim)
    frequency = 10000.0 ** (-exponent)
    angles = positions[:, None] * frequency[None, :]
    angles = jnp.concatenate([angles, angles], axis=-1)[:, None, :]
    return (jnp.cos(angles), jnp.sin(angles))

def rotate(values, cosine, sine_table):
    half_width = values.shape[-1] // 2
    turned = jnp.concatenate([-values[..., half_width:], values[..., :half_width]], axis=-1)
    return values * cosine + turned * sine_table

def attention_mask(starts, patches):
    position = jnp.arange(patches, dtype=jnp.int32)
    query_pos = position[:, None]
    key_pos = position[None, :]
    allowed = (key_pos[None] <= query_pos[None]) & ((key_pos[None] >= starts[:, None, None]) | (key_pos[None] == query_pos[None]))
    return allowed[:, None, :, :]

def forward(series_part, flags_part, lengths_part, params):
    lift_weight, mix_weight, skip_weight, gain_first, joint_weight, merge_weight, gain_second, grow_weight, shrink_weight, head_weight = params
    series_count = series_part.shape[0]
    values = series_part.reshape(series_count, WINDOWS_IN_TRACE, WINDOW_STEPS)
    flag_values = flags_part.reshape(series_count, WINDOWS_IN_TRACE, WINDOW_STEPS).astype(jnp.float32)
    kept_mask = 1.0 - flag_values
    starts = (WINDOWS_IN_TRACE - lengths_part).astype(jnp.int32)
    position = jnp.arange(WINDOWS_IN_TRACE, dtype=jnp.int32)
    first_hot = (position[None, :] == starts[:, None]).astype(jnp.float32)
    observed_flags = (position[None, :] >= starts[:, None]).astype(jnp.float32)
    first_patch = lax.optimization_barrier(jnp.sum(first_hot[:, :, None] * values, axis=1))
    first_kept = lax.optimization_barrier(jnp.sum(first_hot[:, :, None] * kept_mask, axis=1))
    kept_count = jnp.maximum(lax.optimization_barrier(jnp.sum(first_kept, axis=-1)), 1.0)
    center = lax.optimization_barrier(jnp.sum(first_kept * first_patch, axis=-1)) / kept_count
    offset = first_patch - center[:, None]
    spread = lax.optimization_barrier(jnp.sum(first_kept * offset * offset, axis=-1)) / kept_count
    deviation = jnp.sqrt(jnp.maximum(spread, 1.0))
    scaled = (values - center[:, None, None]) / deviation[:, None, None] * kept_mask
    tokens = low(jnp.concatenate([scaled, flag_values], axis=-1))
    hidden_pre = low_back(matmul(tokens, lift_weight))
    hidden_act = low(jax.nn.silu(hidden_pre))
    embedded = low_back(matmul(hidden_act, mix_weight) + matmul(tokens, skip_weight))
    normed_one = low(rms_scale(embedded, gain_first))
    joint_out = low_back(matmul(normed_one, joint_weight))
    cosine, sine_table = rotary_tables(WINDOWS_IN_TRACE, HEAD_DIM)
    shape_heads = (series_count, WINDOWS_IN_TRACE, HEADS, HEAD_DIM)
    query_rot = low(rotate(joint_out[..., :D].reshape(shape_heads), cosine, sine_table))
    key_rot = low(rotate(joint_out[..., D:2 * D].reshape(shape_heads), cosine, sine_table))
    value_heads = low(joint_out[..., 2 * D:].reshape(shape_heads))
    scores = low_back(jnp.einsum('bqhe,bkhe->bhqk', query_rot, key_rot, precision=precise)) * HEAD_DIM ** (-0.5)
    masked = jnp.where(attention_mask(starts, WINDOWS_IN_TRACE), scores, masked_value)
    row_max = lax.optimization_barrier(jnp.max(masked, axis=-1, keepdims=True))
    raised = jnp.exp(masked - row_max)
    probs_low = low(raised / lax.optimization_barrier(jnp.sum(raised, axis=-1, keepdims=True)))
    mixed_heads = low(low_back(jnp.einsum('bhqk,bkhe->bqhe', probs_low, value_heads, precision=precise)))
    attended = low_back(matmul(mixed_heads.reshape(series_count, WINDOWS_IN_TRACE, D), merge_weight))
    resid_one = embedded + attended
    normed_two = low(rms_scale(resid_one, gain_second))
    upper_pre = low_back(matmul(normed_two, grow_weight))
    active = low(jax.nn.silu(upper_pre))
    resid_two = resid_one + low_back(matmul(active, shrink_weight))
    head_out = low_back(matmul(low(resid_two), head_weight))
    return observed_flags[:, :, None] * (head_out * deviation[:, None, None] + center[:, None, None])

def reference(series, flags, lengths, lift_weight, mix_weight, skip_weight, gain_first, joint_weight, merge_weight, gain_second, grow_weight, shrink_weight, head_weight, cotangent):
    weights = tuple((weight.astype(jnp.float32) for weight in (lift_weight, mix_weight, skip_weight, gain_first, joint_weight, merge_weight, gain_second, grow_weight, shrink_weight, head_weight)))
    group_size = math.gcd(TRACE_COUNT, 256)
    step_count = TRACE_COUNT // group_size

    def lone_batch(running, inputs):
        part_series, part_flags, part_lengths, part_cot = inputs

        def apply_layer(values, *params):
            return forward(values, part_flags, part_lengths, params)
        outputs, pullback = jax.vjp(apply_layer, part_series, *weights)
        gradients = pullback(part_cot)
        updated = tuple((before + fresh for before, fresh in zip(running, gradients[1:])))
        return (updated, (outputs, gradients[0]))
    starting_blank = tuple((jnp.zeros(weight.shape, jnp.float32) for weight in weights))
    source_block = (series.reshape(step_count, group_size, WINDOWS_IN_TRACE * WINDOW_STEPS), flags.reshape(step_count, group_size, WINDOWS_IN_TRACE * WINDOW_STEPS), lengths.reshape(step_count, group_size), cotangent.reshape(step_count, group_size, WINDOWS_IN_TRACE, AHEAD_STEPS))
    overall_sums_array, (predicted_block, trace_block) = lax.scan(lone_batch, starting_blank, source_block)
    return (predicted_block.reshape(TRACE_COUNT, WINDOWS_IN_TRACE, AHEAD_STEPS), trace_block.reshape(TRACE_COUNT, WINDOWS_IN_TRACE * WINDOW_STEPS), overall_sums_array[0], overall_sums_array[1], overall_sums_array[2], overall_sums_array[3], overall_sums_array[4], overall_sums_array[5], overall_sums_array[6], overall_sums_array[7], overall_sums_array[8], overall_sums_array[9])
```

```python
import functools
import math

import jax
import jax.numpy as jnp
from jax import lax
from jax.experimental import pallas as pl
from jax.experimental.pallas import tpu as pltpu
from jax.sharding import PartitionSpec as P

HEADS = 16


epsilon = 1e-06
masked_value = -1000000000.0
AXES = ("wide", "narrow")


def product(left_side, right_side):
    return jnp.dot(left_side, right_side, preferred_element_type=jnp.float32)


def product_back(left_side, right_side):
    return lax.dot_general(
        left_side, right_side, (((1,), (1,)), ((), ())), preferred_element_type=jnp.float32
    )


def contract_rows(left_side, right_side):
    return lax.dot_general(
        left_side, right_side, (((0,), (0,)), ((), ())), preferred_element_type=jnp.float32
    )


def silu_slope(values):
    logistic = jax.nn.sigmoid(values)
    return logistic * (1.0 + values * (1.0 - logistic))


def rotary_tables(patches, head_dim):
    positions = jnp.arange(patches, dtype=jnp.int32).astype(jnp.float32)
    exponent = jnp.arange(head_dim // 2, dtype=jnp.int32).astype(jnp.float32) * (2.0 / head_dim)
    frequency = 10000.0 ** (-exponent)
    angles = positions[:, None] * frequency[None, :]
    angles = jnp.concatenate([angles, angles], axis=-1)[:, None, :]
    return (jnp.cos(angles), jnp.sin(angles))


def rotate(values, cosine, sine_table):
    half_width = values.shape[-1] // 2
    turned = jnp.concatenate([-values[..., half_width:], values[..., :half_width]], axis=-1)
    return values * cosine + turned * sine_table


def rotate_back(gradient, cosine, sine_table):
    half_width = gradient.shape[-1] // 2
    sine_part = gradient * sine_table
    turned = jnp.concatenate([sine_part[..., half_width:], -sine_part[..., :half_width]], axis=-1)
    return gradient * cosine + turned


def attention_mask(starts, patches):
    position = jnp.arange(patches, dtype=jnp.int32)
    query_pos = position[:, None]
    key_pos = position[None, :]
    allowed = (key_pos[None] <= query_pos[None]) & (
        (key_pos[None] >= starts[:, None, None]) | (key_pos[None] == query_pos[None])
    )
    return allowed[:, None, :, :]


def norm_back(inputs, scale_inv, gain_vector, upstream):
    gain_terms = upstream * inputs * scale_inv
    through = upstream * gain_vector
    inner_mean = jnp.mean(through * inputs, axis=-1, keepdims=True)
    return (gain_terms, scale_inv * through - inputs * scale_inv**3 * inner_mean)


def scatter_sum(array):
    return lax.psum_scatter(array, AXES, scatter_dimension=0, tiled=True)


class Layout:
    def __init__(self, mesh_shape):
        self.wide = mesh_shape["wide"]
        self.narrow = mesh_shape["narrow"]
        self.total = self.wide * self.narrow

    def fits(self, rows):
        return self.wide == 8 and self.narrow == 4 and rows % (16 * self.total // 4) == 0

    def flip(self, bit):
        return [(i, i ^ bit) for i in range(self.total)]

    def middle(self):
        swapped = (0, 2, 1, 3)
        return [(i, (i & ~3) | swapped[i & 3]) for i in range(self.total)]

    def position(self):
        wide = lax.axis_index("wide")
        narrow = lax.axis_index("narrow")
        return {"y": wide // 4, "x": (wide // 2) % 2, "core": wide % 2, "z": narrow % 2}


def to_other_core(layout, array):
    return lax.ppermute(array.astype(jnp.float32), AXES, layout.flip(4))


def gradient_kernel(groups_ref, *refs, pairs, group_rows, rows):
    count = len(pairs)
    inputs, (send_ref, keep_ref), scratch = refs[: 4 * count], refs[4 * count : 4 * count + 2], refs[4 * count + 2 :]
    turned, chosen, joined = scratch[0], scratch[1 : 1 + count], scratch[1 + count :]
    step = pl.program_id(0)

    @pl.when(step == 0)
    def _():
        for at in range(count):
            left_own, left_other, right_own, right_other = inputs[4 * at : 4 * at + 4]
            turned[:, :rows] = left_own[...].astype(jnp.bfloat16).T
            turned[:, rows:] = left_other[...].astype(jnp.bfloat16).T
            for slot in range(4):
                first = pl.multiple_of(groups_ref[slot] * group_rows, 32)
                chosen[at][slot * group_rows : (slot + 1) * group_rows, :] = turned[pl.ds(first, group_rows), :]
            joined[at][:rows, :] = right_own[...].astype(jnp.bfloat16)
            joined[at][rows:, :] = right_other[...].astype(jnp.bfloat16)

    def fill(out_ref, first):
        for at in range(count):
            begin, mask = pairs[at]
            left_side = chosen[at][first : first + 2 * group_rows, :]
            right_side = joined[at][...]
            if mask is not None:
                lane = lax.broadcasted_iota(jnp.int32, right_side.shape, 1)
                inside = (lane >= mask[0]) & (lane < mask[1])
                right_side = jnp.where(inside, right_side.astype(jnp.float32), 0.0).astype(jnp.bfloat16)
            width = right_side.shape[1]
            result = jnp.dot(left_side, right_side, preferred_element_type=jnp.float32)
            result = result.reshape(2, group_rows, width)
            if mask is not None and mask[0] > 0:
                out_ref[:, :, begin : begin + width] += result
            else:
                out_ref[:, :, begin : begin + width] = result

    @pl.when(step == 0)
    def _():
        fill(send_ref, 0)

    @pl.when(step == 1)
    def _():
        fill(keep_ref, 2 * group_rows)


def weight_gradient(groups, operands, pairs, group_rows):
    rows, left_width = operands[0][0].shape
    total = max(begin + ops[2].shape[1] for (begin, _), ops in zip(pairs, operands))
    flat = [array for four in operands for array in four]
    whole = lambda array: pl.BlockSpec(array.shape, lambda i, s: (0,) * array.ndim)
    out_block = pl.BlockSpec((2, group_rows, total), lambda i, s: (0, 0, 0))
    out_type = jax.ShapeDtypeStruct((2, group_rows, total), jnp.float32)
    flops = sum(2 * 2 * rows * 4 * group_rows * ops[2].shape[1] for ops in operands)
    moved = sum(array.size * array.dtype.itemsize for array in flat) + 4 * group_rows * total * 4
    return pl.pallas_call(
        functools.partial(gradient_kernel, pairs=pairs, group_rows=group_rows, rows=rows),
        grid_spec=pltpu.PrefetchScalarGridSpec(
            num_scalar_prefetch=1,
            grid=(2,),
            in_specs=[whole(array) for array in flat],
            out_specs=[out_block, out_block],
            scratch_shapes=[pltpu.VMEM((left_width, 2 * rows), jnp.bfloat16)]
            + [pltpu.VMEM((4 * group_rows, 2 * rows), jnp.bfloat16) for _ in operands]
            + [pltpu.VMEM((2 * rows, ops[2].shape[1]), jnp.bfloat16) for ops in operands],
        ),
        out_shape=[out_type, out_type],
        compiler_params=pltpu.CompilerParams(vmem_limit_bytes=60 * 1024 * 1024),
        cost_estimate=pl.CostEstimate(flops=flops, bytes_accessed=moved, transcendentals=0),
    )(groups, *flat)


def first_groups(place, axis):
    y, x, core = place["y"], place["x"], place["core"]
    if axis == "x":
        order = [(0, 1 - x), (1, 1 - x), (0, x), (1, x)]
    else:
        order = [(1 - y, 0), (1 - y, 1), (y, 0), (y, 1)]
    return jnp.stack([((a * 2 + b) * 2 + core) for a, b in order]).astype(jnp.int32)


def pick(array, axis, index):
    return lax.dynamic_index_in_dim(array, index, axis, keepdims=False)


def sum_over_chips(layout, place, send, keep, order):
    first = order[0]
    group_rows, columns = send.shape[1:]
    rows = group_rows // 4
    held = keep + lax.ppermute(send, AXES, layout.flip({"x": 8, "y": 16}[first]))
    held = held.reshape(2, 2, 2, rows, columns)
    axes = ["y" if first == "x" else "x", "half", "part"]
    for axis in order[1:]:
        if axis == "z":
            for name in ("half", "part"):
                at = axes.index(name)
                moved = lax.ppermute(pick(held, at, 1 - place["z"]), AXES, layout.flip(1))
                held = pick(held, at, place["z"]) + moved
                axes.remove(name)
                if name == "half":
                    held = lax.ppermute(held, AXES, layout.middle())
        else:
            at = axes.index(axis)
            moved = lax.ppermute(pick(held, at, 1 - place[axis]), AXES, layout.flip({"x": 8, "y": 16}[axis]))
            held = pick(held, at, place[axis]) + moved
            axes.remove(axis)
    return held


def fast_sums(layout, wanted):
    place = layout.position()
    sent = {}

    def other(array):
        if id(array) not in sent:
            sent[id(array)] = to_other_core(layout, array)
        return sent[id(array)]

    results = []
    for order, parts in wanted:
        operands = [(left, other(left), right, other(right)) for left, right, _, _ in parts]
        pairs = tuple((begin, lanes) for _, _, begin, lanes in parts)
        group_rows = parts[0][0].shape[1] // 8
        send, keep = weight_gradient(first_groups(place, order[0]), operands, pairs, group_rows)
        results.append(sum_over_chips(layout, place, send, keep, order))
    return results


def per_device(
    layout,
    series,
    flags,
    lengths,
    lift_weight,
    mix_weight,
    skip_weight,
    gain_first,
    joint_weight,
    merge_weight,
    gain_second,
    grow_weight,
    shrink_weight,
    head_weight,
    cotangent,
):
    series_count = series.shape[0]
    patches = cotangent.shape[1]
    horizon = cotangent.shape[2]
    model_width = mix_weight.shape[0]
    patch_len = lift_weight.shape[0] // 2
    head_count = HEADS
    head_dim = model_width // head_count
    row_count = series_count * patches
    values = series.reshape(series_count, patches, patch_len)
    flag_values = flags.reshape(series_count, patches, patch_len).astype(jnp.float32)
    kept_mask = 1.0 - flag_values
    starts = patches - lengths
    position = jnp.arange(patches, dtype=jnp.int32)
    first_hot = (position[None, :] == starts[:, None]).astype(jnp.float32)
    observed_flags = (position[None, :] >= starts[:, None]).astype(jnp.float32)
    first_patch = jnp.sum(first_hot[:, :, None] * values, axis=1)
    first_kept = jnp.sum(first_hot[:, :, None] * kept_mask, axis=1)
    kept_count = jnp.maximum(jnp.sum(first_kept, axis=-1), 1.0)
    center = jnp.sum(first_kept * first_patch, axis=-1) / kept_count
    offset = first_patch - center[:, None]
    spread = jnp.sum(first_kept * offset * offset, axis=-1) / kept_count
    deviation = jnp.sqrt(jnp.maximum(spread, 1.0))
    shifted = values - center[:, None, None]
    scaled = shifted / deviation[:, None, None] * kept_mask
    tokens = (
        jnp.concatenate([scaled, flag_values], axis=-1)
        .reshape(row_count, 2 * patch_len)
        .astype(jnp.bfloat16)
    )
    hidden_pre = product(tokens, lift_weight)
    hidden_act = jax.nn.silu(hidden_pre).astype(jnp.bfloat16)
    embedded = product(hidden_act, mix_weight) + product(tokens, skip_weight)
    scale_one = lax.rsqrt(jnp.mean(embedded * embedded, axis=-1, keepdims=True) + epsilon)
    normed_one = (embedded * scale_one * gain_first).astype(jnp.bfloat16)
    joint_out = product(normed_one, joint_weight)
    cosine, sine_table = rotary_tables(patches, head_dim)
    shape_heads = (series_count, patches, head_count, head_dim)
    query_rot = rotate(joint_out[:, :model_width].reshape(shape_heads), cosine, sine_table).astype(
        jnp.bfloat16
    )
    key_rot = rotate(
        joint_out[:, model_width : 2 * model_width].reshape(shape_heads), cosine, sine_table
    ).astype(jnp.bfloat16)
    value_heads = joint_out[:, 2 * model_width :].reshape(shape_heads).astype(jnp.bfloat16)
    allowed = attention_mask(starts, patches)
    score_scale = head_dim ** (-0.5)

    def score_block():
        raw_scores = (
            jnp.einsum("bqhe,bkhe->bhqk", query_rot, key_rot, preferred_element_type=jnp.float32)
            * score_scale
        )
        return jnp.where(allowed, raw_scores, masked_value)

    masked = score_block()
    row_max = jnp.max(masked, axis=-1, keepdims=True)
    raised = jnp.exp(masked - row_max)
    row_total = jnp.sum(raised, axis=-1, keepdims=True)
    probs_full = raised / row_total
    logsum = row_max + jnp.log(row_total)
    mixed_heads = (
        jnp.einsum(
            "bhqk,bkhe->bqhe",
            probs_full.astype(jnp.bfloat16),
            value_heads,
            preferred_element_type=jnp.float32,
        )
        .astype(jnp.bfloat16)
        .reshape(row_count, model_width)
    )
    resid_one = embedded + product(mixed_heads, merge_weight)
    scale_two = lax.rsqrt(jnp.mean(resid_one * resid_one, axis=-1, keepdims=True) + epsilon)
    normed_two = (resid_one * scale_two * gain_second).astype(jnp.bfloat16)
    upper_pre = product(normed_two, grow_weight)
    active = jax.nn.silu(upper_pre).astype(jnp.bfloat16)
    resid_two = resid_one + product(active, shrink_weight)
    resid_low = resid_two.astype(jnp.bfloat16)
    head_out = product(resid_low, head_weight).reshape(series_count, patches, horizon)
    predictions = observed_flags[:, :, None] * (
        head_out * deviation[:, None, None] + center[:, None, None]
    )
    outer = cotangent * observed_flags[:, :, None]
    sigma_back = jnp.sum(outer * head_out, axis=(1, 2))
    center_back = jnp.sum(outer, axis=(1, 2))
    head_back = (outer * deviation[:, None, None]).astype(jnp.bfloat16).reshape(row_count, horizon)
    resid_back = product_back(head_back, head_weight)
    branch_back = resid_back.astype(jnp.bfloat16)
    upper_back = (product_back(branch_back, shrink_weight) * silu_slope(upper_pre)).astype(
        jnp.bfloat16
    )
    normed_back = product_back(upper_back, grow_weight)
    second_terms, middle_norm = norm_back(resid_one, scale_two, gain_second, normed_back)
    second_grad = scatter_sum(jnp.sum(second_terms, axis=0))
    middle_back = resid_back + middle_norm
    merge_back = middle_back.astype(jnp.bfloat16)
    mixed_back = product_back(merge_back, merge_weight).astype(jnp.bfloat16).reshape(shape_heads)
    probs_again = jnp.exp(score_block() - logsum)
    value_back = jnp.einsum(
        "bhqk,bqhe->bkhe",
        probs_again.astype(jnp.bfloat16),
        mixed_back,
        preferred_element_type=jnp.float32,
    )
    probs_back = jnp.einsum(
        "bqhe,bkhe->bhqk", mixed_back, value_heads, preferred_element_type=jnp.float32
    )
    row_inner = jnp.sum(probs_again * probs_back, axis=-1, keepdims=True)
    scores_back = (probs_again * (probs_back - row_inner) * score_scale).astype(jnp.bfloat16)
    query_back = rotate_back(
        jnp.einsum("bhqk,bkhe->bqhe", scores_back, key_rot, preferred_element_type=jnp.float32),
        cosine,
        sine_table,
    )
    key_back = rotate_back(
        jnp.einsum("bhqk,bqhe->bkhe", scores_back, query_rot, preferred_element_type=jnp.float32),
        cosine,
        sine_table,
    )
    joint_back = jnp.concatenate(
        [
            query_back.reshape(row_count, model_width),
            key_back.reshape(row_count, model_width),
            value_back.reshape(row_count, model_width),
        ],
        axis=-1,
    ).astype(jnp.bfloat16)
    first_back = product_back(joint_back, joint_weight)
    first_terms, embed_norm = norm_back(embedded, scale_one, gain_first, first_back)
    first_grad = scatter_sum(jnp.sum(first_terms, axis=0))
    embed_low = (middle_back + embed_norm).astype(jnp.bfloat16)
    pre_back = (product_back(embed_low, mix_weight) * silu_slope(hidden_pre)).astype(jnp.bfloat16)

    if layout.fits(model_width):
        width = active.shape[1]
        half = joint_back.shape[1] // 2
        tokens_twice = jnp.concatenate([tokens, tokens], axis=1)
        across = tokens.shape[1]
        shrink_rows, grow_head, merge_grad, joint_a, joint_b, mix_small = fast_sums(
            layout,
            [
                ("xzy", [(branch_back, active, 0, None)]),
                ("yzx", [(normed_two, upper_back, 0, None), (resid_low, head_back, width, None)]),
                ("xyz", [(mixed_heads, merge_back, 0, None)]),
                ("yxz", [(normed_one, joint_back[:, :half], 0, None)]),
                ("xyz", [(normed_one, joint_back[:, half:], 0, None)]),
                (
                    "yzx",
                    [
                        (hidden_act, embed_low, 0, None),
                        (pre_back, tokens_twice, model_width, (0, across)),
                        (embed_low, tokens_twice, model_width, (across, 2 * across)),
                    ],
                ),
            ],
        )
        grow_grad, head_grad = grow_head[:, :width], grow_head[:, width:]
        joint_grad = jnp.concatenate([joint_a, joint_b], axis=1)
        mix_grad = mix_small[:, :model_width]
        lift_rows = mix_small[:, model_width : model_width + across]
        skip_rows = mix_small[:, model_width + across :]
    else:
        head_grad = scatter_sum(contract_rows(resid_low, head_back))
        shrink_rows = scatter_sum(contract_rows(branch_back, active))
        grow_grad = scatter_sum(contract_rows(normed_two, upper_back))
        merge_grad = scatter_sum(contract_rows(mixed_heads, merge_back))
        joint_grad = scatter_sum(contract_rows(normed_one, joint_back))
        mix_grad = scatter_sum(contract_rows(hidden_act, embed_low))
        lift_rows = scatter_sum(contract_rows(pre_back, tokens))
        skip_rows = scatter_sum(contract_rows(embed_low, tokens))
    token_back = product_back(pre_back, lift_weight) + product_back(embed_low, skip_weight)
    scaled_back = token_back.reshape(series_count, patches, 2 * patch_len)[:, :, :patch_len]
    kept_back = scaled_back * kept_mask
    point_back = kept_back / deviation[:, None, None]
    center_total = center_back - jnp.sum(point_back, axis=(1, 2))
    sigma_total = sigma_back - jnp.sum(kept_back * shifted, axis=(1, 2)) / (deviation * deviation)
    spread_back = jnp.where(spread > 1.0, sigma_total * 0.5 / deviation, 0.0)
    center_all = (
        center_total - spread_back * jnp.sum(first_kept * 2.0 * offset, axis=-1) / kept_count
    )
    first_point = (
        first_kept
        * (center_all[:, None] + 2.0 * offset * spread_back[:, None])
        / kept_count[:, None]
    )
    series_grad = (point_back + first_hot[:, :, None] * first_point[:, None, :]).reshape(
        series_count, patches * patch_len
    )
    return (
        predictions,
        series_grad,
        lift_rows.T,
        mix_grad,
        skip_rows.T,
        first_grad,
        joint_grad,
        merge_grad,
        second_grad,
        grow_grad,
        shrink_rows.T,
        head_grad,
    )


def solution(mesh):
    both = P(AXES)
    in_specs = (both, both, both) + (P(),) * 10 + (both,)
    out_specs = (
        P(AXES, None, None),
        P(AXES, None),
        P(None, AXES),
        P(AXES, None),
        P(None, AXES),
        P(AXES),
        P(AXES, None),
        P(AXES, None),
        P(AXES),
        P(AXES, None),
        P(None, AXES),
        P(AXES, None),
    )
    return jax.shard_map(
        functools.partial(per_device, Layout(mesh.shape)),
        mesh=mesh,
        in_specs=in_specs,
        out_specs=out_specs,
        check_vma=False,
    )
```

```python
import functools

import jax
import jax.numpy as jnp
import numpy as np
from jax import lax
from jax.experimental import pallas as pl
from jax.experimental.pallas import tpu as pltpu
from jax.sharding import PartitionSpec as P

HEADS = 16
BLOCK = 128

epsilon = 1e-06
masked_value = -1000000000.0
AXES = ("wide", "narrow")


def rotary_tables(patches, head_dim, count):
    exponent = np.arange(head_dim // 2, dtype=np.float32) * np.float32(2.0 / head_dim)
    frequency = np.float32(10000.0) ** (-exponent)
    angles = frequency[:, None] * np.arange(patches, dtype=np.float32)[None, :]
    angles = np.tile(np.concatenate([angles, angles], axis=0), (1, count))
    return jnp.asarray(np.cos(angles)), jnp.asarray(np.sin(angles))


def dot_plain(left_side, right_side):
    return jnp.dot(left_side, right_side, preferred_element_type=jnp.float32)


def dot_over(left_side, right_side, left_axis, right_axis):
    return lax.dot_general(
        left_side,
        right_side,
        (((left_axis,), (right_axis,)), ((), ())),
        preferred_element_type=jnp.float32,
    )


def dot_exact(left_side, right_side):
    return jnp.dot(
        left_side, right_side, preferred_element_type=jnp.float32, precision=lax.Precision.HIGHEST
    )


def logistic(values):
    return 1.0 / (1.0 + jnp.exp(-values))


def quotient(values, by):
    return lax.shift_right_logical(values, jnp.int32(by.bit_length() - 1))


def remainder(values, by):
    return values & (by - 1)


def iota(shape, axis):
    return lax.broadcasted_iota(jnp.int32, shape, axis)


def series_statistics(lengths_ref, series_ref, flags_ref, patch_len):
    count, points = series_ref.shape
    patches = points // patch_len
    values = series_ref[...]
    kept = 1.0 - flags_ref[...].astype(jnp.float32)
    starts = jnp.zeros((count, 1), jnp.int32)
    row = iota((count, 1), 0)
    for at in range(count):
        starts = jnp.where(row == at, patches - lengths_ref[at], starts)
    hot = (quotient(iota((count, points), 1), patch_len) == starts).astype(jnp.float32)
    hot_kept = hot * kept
    kept_count = jnp.maximum(jnp.sum(hot_kept, axis=1, keepdims=True), 1.0)
    center = jnp.sum(hot_kept * values, axis=1, keepdims=True) / kept_count
    shifted = values - center
    spread = jnp.sum(hot_kept * shifted * shifted, axis=1, keepdims=True) / kept_count
    sigma = jnp.sqrt(jnp.maximum(spread, 1.0))
    return kept, starts, hot_kept, kept_count, center, shifted, spread, sigma


def belongs(rows, count, patches, kind):
    return (quotient(iota((rows, count), 0), patches) == iota((rows, count), 1)).astype(kind)


def belongs_back(rows, count, patches, kind):
    return (quotient(iota((count, rows), 1), patches) == iota((count, rows), 0)).astype(kind)


def own_patch(rows, points, patches, patch_len):
    return quotient(iota((rows, points), 1), patch_len) == remainder(iota((rows, points), 0), patches)


def turn_half(values):
    half = values.shape[0] // 2
    return jnp.concatenate([-values[half:], values[:half]], axis=0)


def turn_half_back(values):
    half = values.shape[0] // 2
    return jnp.concatenate([values[half:], -values[:half]], axis=0)


def split_rows(place_ref, turned, other_ref, own_ref, first, units):
    core = place_ref[0]
    unit = turned.shape[0] // units
    for at in range(units // 2):
        mine = pl.multiple_of((2 * at + core) * unit, 16)
        theirs = pl.multiple_of((2 * at + 1 - core) * unit, 16)
        own_ref[at * unit : (at + 1) * unit, :] = turned[pl.ds(mine, unit), :].astype(jnp.float32)
        other_ref[first + at * unit : first + (at + 1) * unit, :] = turned[pl.ds(theirs, unit), :].astype(jnp.float32)


def put_tiles(ref, first, values):
    rows, width = values.shape
    for at in range(width // rows):
        ref[first + at * rows : first + (at + 1) * rows, :] = values[:, at * rows : (at + 1) * rows].astype(jnp.float32)


UNITS = 8


def front_kernel(
    heads,
    lengths_ref,
    place_ref,
    series_ref,
    flags_ref,
    cotangent_ref,
    gain_first_ref,
    gain_second_ref,
    cosine_ref,
    sine_ref,
    lift_hbm,
    mix_hbm,
    skip_hbm,
    joint_hbm,
    merge_hbm,
    grow_hbm,
    shrink_hbm,
    head_hbm,
    predictions_ref,
    tokens_out,
    logsum_out,
    sigma_sum_out,
    center_sum_out,
    second_out,
    embedded_hbm,
    middle_hbm,
    turned_hbm,
    early_send_hbm,
    early_own_hbm,
    shrink_send_hbm,
    shrink_own_hbm,
    grow_send_hbm,
    grow_own_hbm,
    merge_send_hbm,
    merge_own_hbm,
    lift_ref,
    mix_ref,
    skip_ref,
    joint_ref,
    merge_ref,
    grow_ref,
    shrink_ref,
    head_ref,
    embedded_ref,
    middle_ref,
    joint_turned,
    turned_ref,
    mixed_turned,
    allowed_ref,
    resid_ref,
    upper_ref,
    back_ref,
    flip_ref,
    early_send,
    early_own,
    shrink_send,
    shrink_own,
    grow_send,
    grow_own,
    merge_send,
    merge_own,
    load_sem,
    store_sem,
):
    rows, width = embedded_ref.shape
    count, points = series_ref.shape
    patches = rows // count
    patch_len = points // patches
    head_dim = width // heads
    half_rows = width // 2
    loads = [
        pltpu.make_async_copy(lift_hbm, lift_ref, load_sem.at[0]),
        pltpu.make_async_copy(skip_hbm, skip_ref, load_sem.at[1]),
        pltpu.make_async_copy(mix_hbm, mix_ref, load_sem.at[2]),
    ]
    for at in range(3):
        loads.append(
            pltpu.make_async_copy(joint_hbm.at[:, pl.ds(at * width, width)], joint_ref.at[at], load_sem.at[3 + at])
        )
    for at, (source, target) in enumerate(
        ((merge_hbm, merge_ref), (head_hbm, head_ref), (shrink_hbm, shrink_ref), (grow_hbm, grow_ref))
    ):
        loads.append(pltpu.make_async_copy(source, target, load_sem.at[6 + at]))
    for copy in loads:
        copy.start()
    stores = []

    def store(source, target):
        copy = pltpu.make_async_copy(source, target, store_sem.at[len(stores)])
        copy.start()
        stores.append(copy)

    kept, starts, _, _, center, shifted, _, sigma = series_statistics(lengths_ref, series_ref, flags_ref, patch_len)
    scaled = (shifted / sigma * kept).astype(jnp.bfloat16)
    flag_values = flags_ref[...].astype(jnp.float32).astype(jnp.bfloat16)
    spread_out = belongs(rows, count, patches, jnp.bfloat16)
    inside = own_patch(rows, points, patches, patch_len)
    lane = iota((points, 2 * patch_len), 1)
    point = remainder(iota((points, 2 * patch_len), 0), patch_len)
    fold_left = (lane == point).astype(jnp.bfloat16)
    fold_right = (lane == point + patch_len).astype(jnp.bfloat16)
    left = jnp.where(inside, dot_plain(spread_out, scaled), 0.0).astype(jnp.bfloat16)
    right = jnp.where(inside, dot_plain(spread_out, flag_values), 0.0).astype(jnp.bfloat16)
    tokens = (dot_plain(left, fold_left) + dot_plain(right, fold_right)).astype(jnp.bfloat16)
    tokens_out[...] = tokens
    wide = cotangent_ref.shape[1]
    spread_exact = belongs(rows, count, patches, jnp.float32)
    sigma_rows = dot_exact(spread_exact, jnp.broadcast_to(sigma, (count, wide)))
    center_rows = dot_exact(spread_exact, jnp.broadcast_to(center, (count, wide)))
    starts_rows = dot_exact(spread_exact, jnp.broadcast_to(starts.astype(jnp.float32), (count, wide)))
    patch_row = remainder(iota((rows, wide), 0), patches).astype(jnp.float32)
    valid = (patch_row >= starts_rows - 0.5).astype(jnp.float32)
    block = allowed_ref.shape[1]
    key_at = remainder(iota((rows, block), 0), block)
    query_at = iota((rows, block), 1)
    key_pos, query_pos = remainder(key_at, patches), remainder(query_at, patches)
    allowed_ref[...] = (
        (quotient(key_at, patches) == quotient(query_at, patches))
        & (key_pos <= query_pos)
        & ((key_pos.astype(jnp.float32) >= starts_rows[:, :1] - 0.5) | (key_pos == query_pos))
    ).astype(jnp.float32)

    loads[0].wait()
    hidden_pre = dot_plain(tokens, lift_ref[...])
    hidden_act = (hidden_pre * logistic(hidden_pre)).astype(jnp.bfloat16)
    flip_ref[...] = hidden_act.T
    split_rows(place_ref, flip_ref, early_send, early_own.at[pl.ds(half_rows, half_rows)], half_rows, UNITS)
    loads[1].wait()
    loads[2].wait()
    embedded = dot_plain(hidden_act, mix_ref[...]) + dot_plain(tokens, skip_ref[...])
    embedded_ref[...] = embedded
    store(embedded_ref, embedded_hbm)
    scale_one = lax.rsqrt(jnp.mean(embedded * embedded, axis=1, keepdims=True) + epsilon)
    normed_one = (embedded * scale_one * gain_first_ref[...]).astype(jnp.bfloat16)
    for at in range(3):
        loads[3 + at].wait()
        tile = rows
        for part in range(width // tile):
            result = dot_plain(normed_one, joint_ref[at, :, part * tile : (part + 1) * tile])
            joint_turned[at * width + part * tile : at * width + (part + 1) * tile, :] = result.T
    flip_ref[...] = normed_one.T
    split_rows(place_ref, flip_ref, early_send, early_own.at[pl.ds(0, half_rows)], 0, UNITS)
    store(early_send, early_send_hbm)
    store(early_own, early_own_hbm)

    scale = head_dim ** (-0.5)
    cosine, sine = cosine_ref[...], sine_ref[...]

    def one_head(head, _):
        begin = pl.multiple_of(head * head_dim, 16)
        query = joint_turned[pl.ds(begin, head_dim), :]
        key = joint_turned[pl.ds(width + begin, head_dim), :]
        value = joint_turned[pl.ds(2 * width + begin, head_dim), :].astype(jnp.bfloat16)
        query = (query * cosine + turn_half(query) * sine).astype(jnp.bfloat16)
        key = (key * cosine + turn_half(key) * sine).astype(jnp.bfloat16)
        turned_ref[pl.ds(begin, head_dim), :] = query
        turned_ref[pl.ds(width + begin, head_dim), :] = key
        turned_ref[pl.ds(2 * width + begin, head_dim), :] = value
        mixed, sums = [], []
        for at in range(rows // block):
            span = slice(at * block, (at + 1) * block)
            scores = dot_over(key[:, span], query[:, span], 0, 0) * scale
            scores = jnp.where(allowed_ref[span, :] > 0.5, scores, masked_value)
            top = jnp.max(scores, axis=0, keepdims=True)
            raised = jnp.exp(scores - top)
            total = jnp.sum(raised, axis=0, keepdims=True)
            sums.append(top + jnp.log(total))
            probs = (raised / total).astype(jnp.bfloat16)
            mixed.append(dot_plain(value[:, span], probs))
        logsum_out[pl.ds(head, 1), :] = jnp.concatenate(sums, axis=1)
        mixed_turned[pl.ds(begin, head_dim), :] = jnp.concatenate(mixed, axis=1).astype(jnp.bfloat16)
        return 0

    lax.fori_loop(0, heads, one_head, 0, unroll=2)
    store(turned_ref, turned_hbm)
    split_rows(place_ref, mixed_turned, merge_send, merge_own, 0, UNITS)
    store(merge_own, merge_own_hbm)
    mixed = mixed_turned[...].T
    loads[6].wait()
    resid_one = embedded_ref[...] + dot_plain(mixed, merge_ref[...])
    resid_ref[...] = resid_one
    scale_two = lax.rsqrt(jnp.mean(resid_one * resid_one, axis=1, keepdims=True) + epsilon)
    normed_two = (resid_one * scale_two * gain_second_ref[...]).astype(jnp.bfloat16)
    flip_ref[...] = normed_two.T
    split_rows(place_ref, flip_ref, grow_send, grow_own.at[pl.ds(0, half_rows)], 0, UNITS)

    outer = cotangent_ref[...] * valid
    head_back = (outer * sigma_rows).astype(jnp.bfloat16)
    loads[7].wait()
    resid_back = dot_over(head_back, head_ref[...], 1, 1)
    back_ref[...] = resid_back
    branch_back = resid_back.astype(jnp.bfloat16)
    flip_ref[...] = branch_back.T
    split_rows(place_ref, flip_ref, shrink_send, shrink_own, 0, UNITS)
    store(shrink_own, shrink_own_hbm)

    loads[9].wait()
    upper_pre = dot_plain(normed_two, grow_ref[...])
    upper_ref[...] = upper_pre
    active = (upper_pre * logistic(upper_pre)).astype(jnp.bfloat16)
    put_tiles(shrink_send, half_rows, active)
    store(shrink_send, shrink_send_hbm)
    loads[8].wait()
    upper_pre = upper_ref[...]
    gate = logistic(upper_pre)
    slope = gate * (1.0 + upper_pre * (1.0 - gate))
    upper_back = (dot_over(branch_back, shrink_ref[...], 1, 1) * slope).astype(jnp.bfloat16)
    put_tiles(grow_send, half_rows, upper_back)
    resid_low = (resid_ref[...] + dot_plain(active, shrink_ref[...])).astype(jnp.bfloat16)
    flip_ref[...] = resid_low.T
    split_rows(place_ref, flip_ref, grow_send, grow_own.at[pl.ds(half_rows, half_rows)], half_rows + width, UNITS)
    grow_send[2 * width : 2 * width + wide, :] = head_back.astype(jnp.float32).T
    store(grow_send, grow_send_hbm)
    store(grow_own, grow_own_hbm)

    normed_back = dot_over(upper_back, grow_ref[...], 1, 1)
    resid_one = resid_ref[...]
    second_out[...] = jnp.sum(normed_back * resid_one * scale_two, axis=0, keepdims=True)
    through = normed_back * gain_second_ref[...]
    inner = jnp.mean(through * resid_one, axis=1, keepdims=True)
    middle = back_ref[...] + scale_two * through - resid_one * (scale_two * scale_two * scale_two * inner)
    middle_ref[...] = middle
    store(middle_ref, middle_hbm)
    put_tiles(merge_send, half_rows, middle.astype(jnp.bfloat16))
    store(merge_send, merge_send_hbm)

    head_out = dot_plain(resid_low, head_ref[...])
    predictions_ref[...] = valid * (head_out * sigma_rows + center_rows)
    gather = belongs_back(rows, count, patches, jnp.float32)
    sigma_sum_out[...] = dot_exact(gather, outer * head_out)
    center_sum_out[...] = dot_exact(gather, outer)
    for copy in stores:
        copy.wait()


def front(place, lengths, series, flags, cotangent, tables, weights, heads):
    lift, mix, skip, gain_first, joint, merge, gain_second, grow, shrink, head = weights
    rows, horizon = cotangent.shape
    width = mix.shape[0]
    half = width // 2
    count = series.shape[0]
    f32, bf16 = jnp.float32, jnp.bfloat16
    vmem = pl.BlockSpec(memory_space=pltpu.VMEM)
    smem = pl.BlockSpec(memory_space=pltpu.SMEM)
    hbm = pl.BlockSpec(memory_space=pl.ANY)
    shape = jax.ShapeDtypeStruct
    packs = [
        (2 * half, rows),
        (2 * half, rows),
        (half + width, rows),
        (half, rows),
        (2 * width + horizon, rows),
        (2 * half, rows),
        (half + width, rows),
        (half, rows),
    ]
    outs = [
        shape((rows, horizon), f32),
        shape((rows, lift.shape[0]), bf16),
        shape((heads, rows), f32),
        shape((count, horizon), f32),
        shape((count, horizon), f32),
        shape((1, width), f32),
        shape((rows, width), f32),
        shape((rows, width), f32),
        shape((3 * width, rows), bf16),
    ] + [shape(pack, f32) for pack in packs]
    scratch = [
        pltpu.VMEM(lift.shape, bf16),
        pltpu.VMEM(mix.shape, bf16),
        pltpu.VMEM(skip.shape, bf16),
        pltpu.VMEM((3, width, width), bf16),
        pltpu.VMEM(merge.shape, bf16),
        pltpu.VMEM(grow.shape, bf16),
        pltpu.VMEM(shrink.shape, bf16),
        pltpu.VMEM(head.shape, bf16),
        pltpu.VMEM((rows, width), f32),
        pltpu.VMEM((rows, width), f32),
        pltpu.VMEM((3 * width, rows), f32),
        pltpu.VMEM((3 * width, rows), bf16),
        pltpu.VMEM((width, rows), bf16),
        pltpu.VMEM((rows, BLOCK), f32),
        pltpu.VMEM((rows, width), f32),
        pltpu.VMEM((rows, width), f32),
        pltpu.VMEM((rows, width), f32),
        pltpu.VMEM((width, rows), bf16),
    ] + [pltpu.VMEM(pack, f32) for pack in packs]
    scratch += [pltpu.SemaphoreType.DMA((10,)), pltpu.SemaphoreType.DMA((11,))]
    return pl.pallas_call(
        functools.partial(front_kernel, heads),
        out_shape=outs,
        in_specs=[smem, smem] + [vmem] * 7 + [hbm] * 8,
        out_specs=[vmem] * 6 + [hbm] * 11,
        scratch_shapes=scratch,
        compiler_params=pltpu.CompilerParams(vmem_limit_bytes=62 * 1024 * 1024),
        cost_estimate=pl.CostEstimate(flops=9_000_000_000, bytes_accessed=45_000_000, transcendentals=2_000_000),
    )(
        lengths,
        place,
        series,
        flags,
        cotangent,
        gain_first.reshape(1, width),
        gain_second.reshape(1, width),
        *tables,
        lift,
        mix,
        skip,
        joint,
        merge,
        grow,
        shrink,
        head,
    )


def back_kernel(
    heads,
    lengths_ref,
    place_ref,
    series_ref,
    flags_ref,
    gain_first_ref,
    cosine_ref,
    sine_ref,
    tokens_ref,
    logsum_ref,
    sigma_sum_ref,
    center_sum_ref,
    second_ref,
    middle_ref,
    turned_ref,
    embedded_hbm,
    lift_hbm,
    mix_hbm,
    skip_hbm,
    joint_hbm,
    merge_hbm,
    series_grad_ref,
    joint_send_hbm,
    mix_send_hbm,
    mix_own_hbm,
    vector_send_hbm,
    vector_own_hbm,
    lift_ref,
    mix_ref,
    skip_ref,
    joint_ref,
    merge_ref,
    embedded_ref,
    mixed_turned,
    joint_turned,
    first_ref,
    allowed_ref,
    flip_ref,
    joint_send,
    mix_send,
    mix_own,
    vector_send,
    vector_own,
    vector_flip,
    load_sem,
    store_sem,
):
    rows, width = embedded_ref.shape
    count, points = series_ref.shape
    patches = rows // count
    patch_len = points // patches
    head_dim = width // heads
    half_rows = width // 2
    loads = [
        pltpu.make_async_copy(source, target, load_sem.at[at])
        for at, (source, target) in enumerate(
            (
                (merge_hbm, merge_ref),
                (joint_hbm, joint_ref),
                (embedded_hbm, embedded_ref),
                (mix_hbm, mix_ref),
                (lift_hbm, lift_ref),
                (skip_hbm, skip_ref),
            )
        )
    ]
    for copy in loads:
        copy.start()
    stores = []

    def store(source, target):
        copy = pltpu.make_async_copy(source, target, store_sem.at[len(stores)])
        copy.start()
        stores.append(copy)

    kept, starts, hot_kept, kept_count, center, shifted, spread, sigma = series_statistics(
        lengths_ref, series_ref, flags_ref, patch_len
    )
    block = allowed_ref.shape[1]
    spread_exact = belongs(rows, count, patches, jnp.float32)
    starts_rows = dot_exact(spread_exact, jnp.broadcast_to(starts.astype(jnp.float32), (count, block)))
    key_at = remainder(iota((rows, block), 0), block)
    query_at = iota((rows, block), 1)
    key_pos, query_pos = remainder(key_at, patches), remainder(query_at, patches)
    allowed_ref[...] = (
        (quotient(key_at, patches) == quotient(query_at, patches))
        & (key_pos <= query_pos)
        & ((key_pos.astype(jnp.float32) >= starts_rows - 0.5) | (key_pos == query_pos))
    ).astype(jnp.float32)
    scale = head_dim ** (-0.5)
    cosine, sine = cosine_ref[...], sine_ref[...]
    loads[0].wait()
    mixed_turned[...] = dot_over(merge_ref[...], middle_ref[...].astype(jnp.bfloat16), 1, 1).astype(jnp.bfloat16)

    def unrotate(gradient):
        return gradient * cosine + turn_half_back(gradient * sine)

    def one_head(head, _):
        begin = pl.multiple_of(head * head_dim, 16)
        query = turned_ref[pl.ds(begin, head_dim), :]
        key = turned_ref[pl.ds(width + begin, head_dim), :]
        value = turned_ref[pl.ds(2 * width + begin, head_dim), :]
        upstream = mixed_turned[pl.ds(begin, head_dim), :]
        logsum = logsum_ref[pl.ds(head, 1), :]
        query_parts, key_parts, value_parts = [], [], []
        for at in range(rows // block):
            span = slice(at * block, (at + 1) * block)
            query_in, key_in, value_in, up = query[:, span], key[:, span], value[:, span], upstream[:, span]
            scores = dot_over(key_in, query_in, 0, 0) * scale
            scores = jnp.where(allowed_ref[span, :] > 0.5, scores, masked_value)
            probs = jnp.exp(scores - logsum[:, span])
            value_parts.append(dot_over(up, probs.astype(jnp.bfloat16), 1, 1))
            probs_back = dot_over(value_in, up, 0, 0)
            inner = jnp.sum(probs * probs_back, axis=0, keepdims=True)
            scores_back = (probs * (probs_back - inner) * scale).astype(jnp.bfloat16)
            query_parts.append(dot_plain(key_in, scores_back))
            key_parts.append(dot_over(query_in, scores_back, 1, 1))
        for at, parts in enumerate((query_parts, key_parts, value_parts)):
            result = jnp.concatenate(parts, axis=1)
            if at < 2:
                result = unrotate(result)
            result = result.astype(jnp.bfloat16)
            joint_turned[pl.ds(at * width + begin, head_dim), :] = result
            joint_send[pl.ds(at * width + begin, head_dim), :] = result.astype(jnp.float32)
        return 0

    lax.fori_loop(0, heads, one_head, 0, unroll=2)
    store(joint_send, joint_send_hbm)
    loads[1].wait()
    tile = rows
    for part in range(width // tile):
        span = slice(part * tile, (part + 1) * tile)
        first_ref[:, span] = dot_plain(joint_ref[span, :], joint_turned[...]).T
    loads[2].wait()
    embedded = embedded_ref[...]
    first_back = first_ref[...]
    scale_one = lax.rsqrt(jnp.mean(embedded * embedded, axis=1, keepdims=True) + epsilon)
    first_sum = jnp.sum(first_back * embedded * scale_one, axis=0, keepdims=True)
    through = first_back * gain_first_ref[...]
    inner = jnp.mean(through * embedded, axis=1, keepdims=True)
    embed_low = (
        middle_ref[...] + scale_one * through - embedded * (scale_one * scale_one * scale_one * inner)
    ).astype(jnp.bfloat16)
    put_tiles(mix_send, 0, embed_low)
    flip_ref[...] = embed_low.T
    split_rows(place_ref, flip_ref, mix_send, mix_own.at[pl.ds(0, half_rows)], width, UNITS)
    tokens = tokens_ref[...]
    loads[4].wait()
    hidden_pre = dot_plain(tokens, lift_ref[...])
    gate = logistic(hidden_pre)
    slope = gate * (1.0 + hidden_pre * (1.0 - gate))
    loads[3].wait()
    pre_back = (dot_over(embed_low, mix_ref[...], 1, 1) * slope).astype(jnp.bfloat16)
    flip_ref[...] = pre_back.T
    split_rows(place_ref, flip_ref, mix_send, mix_own.at[pl.ds(half_rows, half_rows)], width + half_rows, UNITS)
    mix_send[2 * width : 2 * width + 2 * patch_len, :] = tokens.astype(jnp.float32).T
    store(mix_send, mix_send_hbm)
    store(mix_own, mix_own_hbm)

    lanes = vector_send.shape[1]
    row = iota((lanes, width), 0)
    both = jnp.where(row == 0, second_ref[...], jnp.where(row == 1, first_sum, 0.0))
    vector_flip[...] = both.T
    core = place_ref[0]
    unit = width // UNITS
    for at in range(UNITS // 2):
        mine = pl.multiple_of((2 * at + core) * unit, 16)
        theirs = pl.multiple_of((2 * at + 1 - core) * unit, 16)
        vector_own[at * unit : (at + 1) * unit, :] = vector_flip[pl.ds(mine, unit), :]
        vector_send[at * unit : (at + 1) * unit, :] = vector_flip[pl.ds(theirs, unit), :]
    store(vector_send, vector_send_hbm)
    store(vector_own, vector_own_hbm)

    loads[5].wait()
    token_back = dot_over(pre_back, lift_ref[...], 1, 1) + dot_over(embed_low, skip_ref[...], 1, 1)
    lane = remainder(iota((2 * patch_len, points), 1), patch_len)
    unfold = (lane == iota((2 * patch_len, points), 0)).astype(jnp.float32)
    inside = own_patch(rows, points, patches, patch_len)
    spread_back_rows = jnp.where(inside, dot_exact(token_back, unfold), 0.0)
    scaled_back = dot_exact(belongs_back(rows, count, patches, jnp.float32), spread_back_rows)
    kept_back = scaled_back * kept
    point_back = kept_back / sigma
    sigma_back = jnp.sum(sigma_sum_ref[...], axis=1, keepdims=True)
    center_back = jnp.sum(center_sum_ref[...], axis=1, keepdims=True)
    center_total = center_back - jnp.sum(point_back, axis=1, keepdims=True)
    sigma_total = sigma_back - jnp.sum(kept_back * shifted, axis=1, keepdims=True) / (sigma * sigma)
    spread_grad = jnp.where(spread > 1.0, sigma_total * 0.5 / sigma, 0.0)
    offset_sum = jnp.sum(hot_kept * 2.0 * shifted, axis=1, keepdims=True)
    center_all = center_total - spread_grad * offset_sum / kept_count
    series_grad_ref[...] = point_back + hot_kept * (center_all + 2.0 * shifted * spread_grad) / kept_count
    for copy in stores:
        copy.wait()


def back(place, lengths, series, flags, tables, weights, kept_values, heads):
    lift, mix, skip, gain_first, joint, merge = weights
    tokens, logsum, sigma_sum, center_sum, second_sum, embedded, middle, turned = kept_values
    rows, width = embedded.shape
    half = width // 2
    f32, bf16 = jnp.float32, jnp.bfloat16
    vmem = pl.BlockSpec(memory_space=pltpu.VMEM)
    smem = pl.BlockSpec(memory_space=pltpu.SMEM)
    hbm = pl.BlockSpec(memory_space=pl.ANY)
    shape = jax.ShapeDtypeStruct
    packs = [
        (3 * width, rows),
        (2 * width + lift.shape[0], rows),
        (2 * half, rows),
        (half, BLOCK),
        (half, BLOCK),
    ]
    scratch = [
        pltpu.VMEM(lift.shape, bf16),
        pltpu.VMEM(mix.shape, bf16),
        pltpu.VMEM(skip.shape, bf16),
        pltpu.VMEM(joint.shape, bf16),
        pltpu.VMEM(merge.shape, bf16),
        pltpu.VMEM((rows, width), f32),
        pltpu.VMEM((width, rows), bf16),
        pltpu.VMEM((3 * width, rows), bf16),
        pltpu.VMEM((rows, width), f32),
        pltpu.VMEM((rows, BLOCK), f32),
        pltpu.VMEM((width, rows), bf16),
    ] + [pltpu.VMEM(pack, f32) for pack in packs]
    scratch += [pltpu.VMEM((width, BLOCK), f32), pltpu.SemaphoreType.DMA((6,)), pltpu.SemaphoreType.DMA((5,))]
    return pl.pallas_call(
        functools.partial(back_kernel, heads),
        out_shape=[shape(series.shape, f32)] + [shape(pack, f32) for pack in packs],
        in_specs=[smem, smem] + [vmem] * 12 + [hbm] * 6,
        out_specs=[vmem] + [hbm] * 5,
        scratch_shapes=scratch,
        compiler_params=pltpu.CompilerParams(vmem_limit_bytes=62 * 1024 * 1024),
        cost_estimate=pl.CostEstimate(flops=6_000_000_000, bytes_accessed=35_000_000, transcendentals=1_000_000),
    )(
        lengths,
        place,
        series,
        flags,
        gain_first.reshape(1, width),
        *tables,
        tokens,
        logsum,
        sigma_sum,
        center_sum,
        second_sum,
        middle,
        turned,
        embedded,
        lift,
        mix,
        skip,
        joint,
        merge,
    )


def gradient_kernel(groups_ref, *refs, terms, inputs, unit):
    arrays, (send_ref, keep_ref), scratch = refs[:inputs], refs[inputs : inputs + 2], refs[inputs + 2 :]
    step = pl.program_id(0)
    matrices = [term for term in terms if term[7] != "sum"]

    @pl.when(step == 0)
    def _():
        for at, (own, own_row, other, other_row, near, far, row, kind, width, _) in enumerate(matrices):
            left, right = scratch[2 * at], scratch[2 * at + 1]
            rows = left.shape[1] // 2
            for slot in range(4):
                first = groups_ref[slot] * unit
                mine = pl.multiple_of(own_row + first, 16)
                theirs = pl.multiple_of(other_row + first, 16)
                span = slice(slot * unit, (slot + 1) * unit)
                left[span, :rows] = arrays[own][pl.ds(mine, unit), :].astype(jnp.bfloat16)
                left[span, rows:] = arrays[other][pl.ds(theirs, unit), :].astype(jnp.bfloat16)
            for place, source in ((0, near), (rows, far)):
                if kind == "tiles":
                    for tile in range(width // rows):
                        begin = row + tile * rows
                        right[place : place + rows, tile * rows : (tile + 1) * rows] = arrays[source][
                            begin : begin + rows, :
                        ].astype(jnp.bfloat16)
                elif kind == "turned":
                    right[:, place : place + rows] = arrays[source][row : row + width, :].astype(jnp.bfloat16)
                else:
                    filled = arrays[source][row : row + width, :].astype(jnp.bfloat16)
                    blank = jnp.zeros_like(filled)
                    stacked = (filled, blank) if kind == "low" else (blank, filled)
                    right[:, place : place + rows] = jnp.concatenate(stacked, axis=0)

    def fill(out_ref, slots):
        for at, (_, _, _, _, _, _, _, kind, width, begin) in enumerate(matrices):
            left = scratch[2 * at][slots[0] * unit : (slots[-1] + 1) * unit, :]
            right = scratch[2 * at + 1][...]
            if kind == "tiles":
                result = dot_plain(left, right)
            else:
                result = dot_over(left, right, 1, 1)
            result = result.reshape(len(slots), unit, result.shape[1])
            if kind == "high":
                out_ref[:, :, begin : begin + result.shape[2]] += result
            else:
                out_ref[:, :, begin : begin + result.shape[2]] = result
        for own, _, other, _, _, _, _, kind, width, begin in terms:
            if kind == "sum":
                for place, slot in enumerate(slots):
                    first = pl.multiple_of(groups_ref[slot] * unit, 16)
                    out_ref[place, :, begin : begin + width] = (
                        arrays[own][pl.ds(first, unit), :] + arrays[other][pl.ds(first, unit), :]
                    )

    @pl.when(step == 0)
    def _():
        fill(send_ref, (0, 1))

    @pl.when(step == 1)
    def _():
        fill(keep_ref, (2, 3))


def weight_gradient(groups, arrays, terms, unit, columns):
    rows = arrays[0][0].shape[1]
    blocks = [
        pl.BlockSpec((height, array.shape[1]), lambda i, s, at=at: (at, 0), pipeline_mode=pl.Buffered(1))
        for array, height, at in arrays
    ]
    out_block = pl.BlockSpec((2, unit, columns), lambda i, s: (0, 0, 0))
    out_type = jax.ShapeDtypeStruct((2, unit, columns), jnp.float32)
    scratch = []
    for term in terms:
        kind, width = term[7], term[8]
        if kind == "sum":
            continue
        scratch.append(pltpu.VMEM((4 * unit, 2 * rows), jnp.bfloat16))
        if kind == "tiles":
            scratch.append(pltpu.VMEM((2 * rows, width), jnp.bfloat16))
        else:
            scratch.append(pltpu.VMEM((width if kind == "turned" else 2 * width, 2 * rows), jnp.bfloat16))
    moved = sum(height * array.shape[1] * 4 for array, height, _ in arrays) + 4 * unit * columns * 4
    return pl.pallas_call(
        functools.partial(gradient_kernel, terms=terms, inputs=len(arrays), unit=unit),
        grid_spec=pltpu.PrefetchScalarGridSpec(
            num_scalar_prefetch=1,
            grid=(2,),
            in_specs=blocks,
            out_specs=[out_block, out_block],
            scratch_shapes=scratch,
        ),
        out_shape=[out_type, out_type],
        compiler_params=pltpu.CompilerParams(vmem_limit_bytes=50 * 1024 * 1024),
        cost_estimate=pl.CostEstimate(
            flops=2 * 2 * rows * 4 * unit * columns, bytes_accessed=moved, transcendentals=0
        ),
    )(groups, *(array for array, _, _ in arrays))


class Layout:
    def __init__(self, mesh_shape):
        self.wide = mesh_shape["wide"]
        self.narrow = mesh_shape["narrow"]
        self.total = self.wide * self.narrow
        self.paired = self.wide == 8 and self.narrow == 4

    def flip(self, bit):
        return [(i, i ^ bit) for i in range(self.total)]

    def middle(self):
        swapped = (0, 2, 1, 3)
        return [(i, (i & ~3) | swapped[i & 3]) for i in range(self.total)]

    def position(self):
        wide = lax.axis_index("wide")
        narrow = lax.axis_index("narrow")
        return {"y": wide // 4, "x": (wide // 2) % 2, "core": wide % 2, "z": narrow % 2}


def first_groups(place, axis):
    y, x = place["y"], place["x"]
    if axis == "x":
        order = [1 - x, 2 + 1 - x, x, 2 + x]
    else:
        order = [2 * (1 - y), 2 * (1 - y) + 1, 2 * y, 2 * y + 1]
    return jnp.stack(order).astype(jnp.int32)


def pick(array, axis, index):
    return lax.dynamic_index_in_dim(array, index, axis, keepdims=False)


def sum_over_chips(layout, place, send, keep, order):
    first = order[0]
    unit, columns = send.shape[1:]
    rows = unit // 4
    held = keep + lax.ppermute(send, AXES, layout.flip({"x": 8, "y": 16}[first]))
    held = held.reshape(2, 2, 2, rows, columns)
    axes = ["y" if first == "x" else "x", "half", "part"]
    for axis in order[1:]:
        if axis == "z":
            for name in ("half", "part"):
                at = axes.index(name)
                moved = lax.ppermute(pick(held, at, 1 - place["z"]), AXES, layout.flip(1))
                held = pick(held, at, place["z"]) + moved
                axes.remove(name)
                if name == "half":
                    held = lax.ppermute(held, AXES, layout.middle())
        else:
            at = axes.index(axis)
            moved = lax.ppermute(pick(held, at, 1 - place[axis]), AXES, layout.flip({"x": 8, "y": 16}[axis]))
            held = pick(held, at, place[axis]) + moved
            axes.remove(axis)
    return held


def whole_rows(own, other):
    unit = own.shape[0] // (UNITS // 2)
    pair = jnp.stack([own.reshape(-1, unit, own.shape[1]), other.reshape(-1, unit, own.shape[1])], axis=1)
    return pair.reshape(2 * own.shape[0], own.shape[1])


def whole_tiles(tiles, rows):
    return jnp.concatenate([tiles[at : at + rows] for at in range(0, tiles.shape[0], rows)], axis=1)


def per_device(
    layout,
    series,
    flags,
    lengths,
    lift_weight,
    mix_weight,
    skip_weight,
    gain_first,
    joint_weight,
    merge_weight,
    gain_second,
    grow_weight,
    shrink_weight,
    head_weight,
    cotangent,
):
    count = series.shape[0]
    patches, horizon = cotangent.shape[1:]
    width = mix_weight.shape[0]
    hidden = shrink_weight.shape[0]
    rows = count * patches
    half = width // 2
    tables = rotary_tables(patches, width // HEADS, count)
    place = layout.position()
    core = place["core"] if layout.paired else jnp.zeros_like(place["core"])
    core = jnp.reshape(core, (1,)).astype(jnp.int32)
    weights = (
        lift_weight,
        mix_weight,
        skip_weight,
        gain_first,
        joint_weight,
        merge_weight,
        gain_second,
        grow_weight,
        shrink_weight,
        head_weight,
    )
    (
        predictions,
        tokens,
        logsum,
        sigma_sum,
        center_sum,
        second_sum,
        embedded,
        middle,
        turned,
        early_send,
        early_own,
        shrink_send,
        shrink_own,
        grow_send,
        grow_own,
        merge_send,
        merge_own,
    ) = front(core, lengths, series, flags, cotangent.reshape(rows, horizon), tables, weights, HEADS)
    series_grad, joint_send, mix_send, mix_own, vector_send, vector_own = back(
        core,
        lengths,
        series,
        flags,
        tables,
        (lift_weight, mix_weight, skip_weight, gain_first, joint_weight, merge_weight),
        (tokens, logsum, sigma_sum, center_sum, second_sum, embedded, middle, turned),
        HEADS,
    )
    across = lift_weight.shape[0]
    joint_width = joint_weight.shape[1]
    if layout.paired:
        swap = lambda array: lax.ppermute(array, AXES, layout.flip(4))
        unit = width // UNITS
        whole = lambda array: (array, array.shape[0], 0)
        shrink_got, grow_got, merge_got, early_got = swap(shrink_send), swap(grow_send), swap(merge_send), swap(early_send)
        joint_got, mix_got, vector_got = swap(joint_send), swap(mix_send), swap(vector_send)

        def piece(order, arrays, terms, columns):
            send, keep = weight_gradient(first_groups(place, order[0]), arrays, terms, unit, columns)
            return sum_over_chips(layout, place, send, keep, order)

        shrink_rows = piece(
            "xzy",
            [whole(shrink_own), whole(shrink_send), whole(shrink_got)],
            ((0, 0, 2, 0, 1, 2, half, "tiles", hidden, 0),),
            hidden,
        )
        grow_head = piece(
            "yzx",
            [whole(grow_own), whole(grow_send), whole(grow_got)],
            (
                (0, 0, 2, 0, 1, 2, half, "tiles", hidden, 0),
                (0, half, 2, half + hidden, 1, 2, width + hidden, "turned", horizon, hidden),
            ),
            hidden + horizon,
        )
        merge_grad = piece(
            "xyz",
            [whole(merge_own), whole(merge_send), whole(merge_got)],
            ((0, 0, 2, 0, 1, 2, half, "tiles", width, 0),),
            width,
        )
        span = joint_width // 2
        joint_parts = [
            piece(
                order,
                [(early_own, half, 0), (early_got, half, 0), (joint_send, span, at), (joint_got, span, at)],
                ((0, 0, 1, 0, 2, 3, 0, "turned", span, 0),),
                span,
            )
            for at, order in enumerate(("yxz", "xyz"))
        ]
        mix_small = piece(
            "yzx",
            [
                (early_own, half, 1),
                (early_got, half, 1),
                whole(mix_own),
                whole(mix_send),
                whole(mix_got),
                whole(vector_own),
                whole(vector_got),
            ],
            (
                (0, 0, 1, 0, 3, 4, 0, "tiles", width, 0),
                (2, half, 4, width + half, 3, 4, 2 * width, "low", across, width),
                (2, 0, 4, width, 3, 4, 2 * width, "high", across, width),
                (5, 0, 6, 0, 0, 0, 0, "sum", BLOCK, width + 2 * across),
            ),
            width + 2 * across + BLOCK,
        )
        grow_grad, head_grad = grow_head[:, :hidden], grow_head[:, hidden:]
        joint_grad = jnp.concatenate(joint_parts, axis=1)
        mix_grad = mix_small[:, :width]
        lift_rows = mix_small[:, width : width + across]
        skip_rows = mix_small[:, width + across : width + 2 * across]
        second_grad = mix_small[:, width + 2 * across]
        first_grad = mix_small[:, width + 2 * across + 1]
    else:
        scatter = lambda left, right: lax.psum_scatter(
            dot_plain(left.astype(jnp.bfloat16), right.astype(jnp.bfloat16)), AXES, scatter_dimension=0, tiled=True
        )
        branch_back = whole_rows(shrink_own, shrink_send[:half])
        normed_two = whole_rows(grow_own[:half], grow_send[:half])
        resid_low = whole_rows(grow_own[half:], grow_send[half + hidden : width + hidden])
        mixed = whole_rows(merge_own, merge_send[:half])
        normed_one = whole_rows(early_own[:half], early_send[:half])
        hidden_act = whole_rows(early_own[half:], early_send[half:])
        embed_low = whole_rows(mix_own[:half], mix_send[width : width + half])
        pre_back = whole_rows(mix_own[half:], mix_send[width + half : 2 * width])
        shrink_rows = scatter(branch_back, whole_tiles(shrink_send[half:], rows))
        grow_grad = scatter(normed_two, whole_tiles(grow_send[half : half + hidden], rows))
        head_grad = scatter(resid_low, grow_send[width + hidden :].T)
        merge_grad = scatter(mixed, whole_tiles(merge_send[half:], rows))
        joint_grad = scatter(normed_one, joint_send.T)
        mix_grad = scatter(hidden_act, whole_tiles(mix_send[:width], rows))
        lift_rows = scatter(pre_back, tokens)
        skip_rows = scatter(embed_low, tokens)
        sums = lax.psum_scatter(whole_rows(vector_own, vector_send), AXES, scatter_dimension=0, tiled=True)
        second_grad, first_grad = sums[:, 0], sums[:, 1]
    return (
        predictions.reshape(count, patches, horizon),
        series_grad,
        lift_rows.T,
        mix_grad,
        skip_rows.T,
        first_grad,
        joint_grad,
        merge_grad,
        second_grad,
        grow_grad,
        shrink_rows.T,
        head_grad,
    )


def solution(mesh):
    both = P(AXES)
    in_specs = (both, both, both) + (P(),) * 10 + (both,)
    out_specs = (
        P(AXES, None, None),
        P(AXES, None),
        P(None, AXES),
        P(AXES, None),
        P(None, AXES),
        P(AXES),
        P(AXES, None),
        P(AXES, None),
        P(AXES),
        P(AXES, None),
        P(None, AXES),
        P(AXES, None),
    )
    return jax.shard_map(
        functools.partial(per_device, Layout(mesh.shape)),
        mesh=mesh,
        in_specs=in_specs,
        out_specs=out_specs,
        check_vma=False,
    )
```

```python
import functools
import math

import jax
import jax.numpy as jnp
import numpy as np
from jax import lax
from jax.experimental import pallas as pl
from jax.experimental.pallas import tpu as pltpu
from jax.sharding import PartitionSpec as P

HEADS = 16
BLOCK = 128

epsilon = 1e-06
masked_value = -1000000000.0
AXES = ("wide", "narrow")


def rotary_tables(patches, head_dim, count):
    exponent = np.arange(head_dim // 2, dtype=np.float32) * np.float32(2.0 / head_dim)
    frequency = np.float32(10000.0) ** (-exponent)
    angles = frequency[:, None] * np.arange(patches, dtype=np.float32)[None, :]
    angles = np.tile(np.concatenate([angles, angles], axis=0), (1, count))
    return jnp.asarray(np.cos(angles)), jnp.asarray(np.sin(angles))


TILE_BYTES = 409600
ORDERS = {"A": "azb", "B": "azb", "C": "azb", "D1": "azb", "D2": "abz", "D3": "abz", "E": "abz"}
PROGRAM = (
    "A", "B", "K", "A", "C", "D3", "B", "E", "A", "C", "B", "D3", "A", "C", "E", "B", "A", "D3", "B", "A", "D1", "C", "E", "B", "D2", "D3", "C", "D1", "E", "D3", "D2", "C", "E", "D1", "D3", "D2", "E", "D2", "D1", "D2", "D1", "D2", "D1",
)


def dot_plain(left_side, right_side):
    return jnp.dot(left_side, right_side, preferred_element_type=jnp.float32)


def dot_over(left_side, right_side, left_axis, right_axis):
    return lax.dot_general(
        left_side,
        right_side,
        (((left_axis,), (right_axis,)), ((), ())),
        preferred_element_type=jnp.float32,
    )


def dot_exact(left_side, right_side):
    return jnp.dot(
        left_side, right_side, preferred_element_type=jnp.float32, precision=lax.Precision.HIGHEST
    )


def logistic(values):
    return 1.0 / (1.0 + jnp.exp(-values))


def quotient(values, by):
    return lax.shift_right_logical(values, jnp.int32(by.bit_length() - 1))


def remainder(values, by):
    return values & (by - 1)


def iota(shape, axis):
    return lax.broadcasted_iota(jnp.int32, shape, axis)


def series_statistics(lengths_ref, series_ref, flags_ref, patch_len):
    count, points = series_ref.shape
    patches = points // patch_len
    values = series_ref[...]
    kept = 1.0 - flags_ref[...].astype(jnp.float32)
    starts = jnp.zeros((count, 1), jnp.int32)
    row = iota((count, 1), 0)
    for at in range(count):
        starts = jnp.where(row == at, patches - lengths_ref[at], starts)
    hot = (quotient(iota((count, points), 1), patch_len) == starts).astype(jnp.float32)
    hot_kept = hot * kept
    kept_count = jnp.maximum(jnp.sum(hot_kept, axis=1, keepdims=True), 1.0)
    center = jnp.sum(hot_kept * values, axis=1, keepdims=True) / kept_count
    shifted = values - center
    spread = jnp.sum(hot_kept * shifted * shifted, axis=1, keepdims=True) / kept_count
    sigma = jnp.sqrt(jnp.maximum(spread, 1.0))
    return kept, starts, hot_kept, kept_count, center, shifted, spread, sigma


def belongs(rows, count, patches, kind):
    return (quotient(iota((rows, count), 0), patches) == iota((rows, count), 1)).astype(kind)


def belongs_back(rows, count, patches, kind):
    return (quotient(iota((count, rows), 1), patches) == iota((count, rows), 0)).astype(kind)


def own_patch(rows, points, patches, patch_len):
    return quotient(iota((rows, points), 1), patch_len) == remainder(iota((rows, points), 0), patches)


def turn_half(values):
    half = values.shape[0] // 2
    return jnp.concatenate([-values[half:], values[:half]], axis=0)


def turn_half_back(values):
    half = values.shape[0] // 2
    return jnp.concatenate([values[half:], -values[:half]], axis=0)


def split_rows(place_ref, turned, other_ref, own_ref, first, units):
    core = place_ref[0]
    unit = turned.shape[0] // units
    for at in range(units // 2):
        mine = pl.multiple_of((2 * at + core) * unit, 16)
        theirs = pl.multiple_of((2 * at + 1 - core) * unit, 16)
        own_ref[at * unit : (at + 1) * unit, :] = turned[pl.ds(mine, unit), :].astype(jnp.float32)
        other_ref[first + at * unit : first + (at + 1) * unit, :] = turned[pl.ds(theirs, unit), :].astype(jnp.float32)


def put_tiles(ref, first, values):
    rows, width = values.shape
    for at in range(width // rows):
        ref[first + at * rows : first + (at + 1) * rows, :] = values[:, at * rows : (at + 1) * rows].astype(jnp.float32)


UNITS = 8
TOKEN = jax.ShapeDtypeStruct((8, 128), jnp.float32)


def COST(microseconds):
    return pl.CostEstimate(flops=int(microseconds * 11500000000.0), bytes_accessed=0, transcendentals=0)


OWN = ("branch", "normed_two", "resid", "mixed", "normed_one", "hidden")


def stack_rows(*heights):
    places, at = {}, 0
    for name, height in heights:
        places[name] = at
        at += height
    places["end"] = at
    return places


def later_rows(width, horizon):
    half = width // 2
    return stack_rows(("normed_two", half), ("upper", width), ("resid", half), ("head", horizon))


def rest_rows(width):
    half = width // 2
    return stack_rows(
        ("mixed", half),
        ("middle", width),
        ("normed_one", half),
        ("hidden", half),
    )


def last_rows(width, patch_len, rows):
    half = width // 2
    return stack_rows(
        ("embed_tiles", width),
        ("embed", half),
        ("pre", half),
        ("tokens", 2 * patch_len),
        ("sums", 8 * width // rows),
    )


def front_kernel(
    heads,
    lengths_ref,
    place_ref,
    series_ref,
    flags_ref,
    cotangent_ref,
    gain_first_ref,
    gain_second_ref,
    cosine_ref,
    sine_ref,
    lift_hbm,
    mix_hbm,
    skip_hbm,
    joint_hbm,
    merge_hbm,
    grow_hbm,
    shrink_hbm,
    head_hbm,
    token_ref,
    predictions_ref,
    tokens_out,
    logsum_out,
    sigma_sum_out,
    center_sum_out,
    second_out,
    embedded_hbm,
    middle_hbm,
    turned_hbm,
    own_hbm,
    soon_hbm,
    later_hbm,
    rest_hbm,
    lift_ref,
    mix_ref,
    skip_ref,
    joint_ref,
    merge_ref,
    grow_ref,
    shrink_ref,
    head_ref,
    embedded_ref,
    middle_ref,
    joint_turned,
    turned_ref,
    mixed_turned,
    allowed_ref,
    resid_ref,
    upper_ref,
    back_ref,
    flip_ref,
    own,
    soon,
    later,
    rest,
    load_sem,
    store_sem,
):
    rows, width = embedded_ref.shape
    count, points = series_ref.shape
    patches = rows // count
    patch_len = points // patches
    head_dim = width // heads
    half_rows = width // 2
    wide = cotangent_ref.shape[1]
    token_ref[...] = jnp.zeros_like(token_ref)
    loads = [
        pltpu.make_async_copy(lift_hbm, lift_ref, load_sem.at[0]),
        pltpu.make_async_copy(skip_hbm, skip_ref, load_sem.at[1]),
        pltpu.make_async_copy(mix_hbm, mix_ref, load_sem.at[2]),
    ]
    for at in range(3):
        loads.append(
            pltpu.make_async_copy(joint_hbm.at[:, pl.ds(at * width, width)], joint_ref.at[at], load_sem.at[3 + at])
        )
    for at, (source, target) in enumerate(
        ((merge_hbm, merge_ref), (head_hbm, head_ref), (shrink_hbm, shrink_ref), (grow_hbm, grow_ref))
    ):
        loads.append(pltpu.make_async_copy(source, target, load_sem.at[6 + at]))
    for copy in loads:
        copy.start()
    stores = []

    def store(source, target, first=0, count=None):
        span = pl.ds(first, source.shape[0] - first if count is None else count)
        copy = pltpu.make_async_copy(source.at[span], target.at[span], store_sem.at[len(stores)])
        copy.start()
        stores.append(copy)

    def split(turned, name, pack, at):
        first = OWN.index(name) * half_rows
        split_rows(place_ref, turned, pack, own.at[pl.ds(first, half_rows)], at, UNITS)
        store(own, own_hbm, first, half_rows)

    places = later_rows(width, wide) | rest_rows(width)

    kept, starts, _, _, center, shifted, _, sigma = series_statistics(lengths_ref, series_ref, flags_ref, patch_len)
    scaled = (shifted / sigma * kept).astype(jnp.bfloat16)
    flag_values = flags_ref[...].astype(jnp.float32).astype(jnp.bfloat16)
    spread_out = belongs(rows, count, patches, jnp.bfloat16)
    inside = own_patch(rows, points, patches, patch_len)
    lane = iota((points, 2 * patch_len), 1)
    point = remainder(iota((points, 2 * patch_len), 0), patch_len)
    fold_left = (lane == point).astype(jnp.bfloat16)
    fold_right = (lane == point + patch_len).astype(jnp.bfloat16)
    left = jnp.where(inside, dot_plain(spread_out, scaled), 0.0).astype(jnp.bfloat16)
    right = jnp.where(inside, dot_plain(spread_out, flag_values), 0.0).astype(jnp.bfloat16)
    tokens = (dot_plain(left, fold_left) + dot_plain(right, fold_right)).astype(jnp.bfloat16)
    tokens_out[...] = tokens
    spread_exact = belongs(rows, count, patches, jnp.float32)
    sigma_rows = dot_exact(spread_exact, jnp.broadcast_to(sigma, (count, wide)))
    center_rows = dot_exact(spread_exact, jnp.broadcast_to(center, (count, wide)))
    starts_rows = dot_exact(spread_exact, jnp.broadcast_to(starts.astype(jnp.float32), (count, wide)))
    patch_row = remainder(iota((rows, wide), 0), patches).astype(jnp.float32)
    valid = (patch_row >= starts_rows - 0.5).astype(jnp.float32)
    block = allowed_ref.shape[1]
    key_at = remainder(iota((rows, block), 0), block)
    query_at = iota((rows, block), 1)
    key_pos, query_pos = remainder(key_at, patches), remainder(query_at, patches)
    allowed_ref[...] = (
        (quotient(key_at, patches) == quotient(query_at, patches))
        & (key_pos <= query_pos)
        & ((key_pos.astype(jnp.float32) >= starts_rows[:, :1] - 0.5) | (key_pos == query_pos))
    ).astype(jnp.float32)

    loads[0].wait()
    hidden_pre = dot_plain(tokens, lift_ref[...])
    hidden_act = (hidden_pre * logistic(hidden_pre)).astype(jnp.bfloat16)
    flip_ref[...] = hidden_act.T
    split(flip_ref, "hidden", rest, places["hidden"])
    store(rest, rest_hbm, places["hidden"], half_rows)
    loads[1].wait()
    loads[2].wait()
    embedded = dot_plain(hidden_act, mix_ref[...]) + dot_plain(tokens, skip_ref[...])
    embedded_ref[...] = embedded
    store(embedded_ref, embedded_hbm)
    scale_one = lax.rsqrt(jnp.mean(embedded * embedded, axis=1, keepdims=True) + epsilon)
    normed_one = (embedded * scale_one * gain_first_ref[...][None, :]).astype(jnp.bfloat16)
    for at in range(3):
        loads[3 + at].wait()
        tile = rows
        for part in range(width // tile):
            result = dot_plain(normed_one, joint_ref[at, :, part * tile : (part + 1) * tile])
            joint_turned[at * width + part * tile : at * width + (part + 1) * tile, :] = result.T
    flip_ref[...] = normed_one.T
    split(flip_ref, "normed_one", rest, places["normed_one"])
    store(rest, rest_hbm, places["normed_one"], half_rows)

    scale = head_dim ** (-0.5)
    cosine, sine = cosine_ref[...], sine_ref[...]

    def one_head(head, _):
        begin = pl.multiple_of(head * head_dim, 16)
        query = joint_turned[pl.ds(begin, head_dim), :]
        key = joint_turned[pl.ds(width + begin, head_dim), :]
        value = joint_turned[pl.ds(2 * width + begin, head_dim), :].astype(jnp.bfloat16)
        query = (query * cosine + turn_half(query) * sine).astype(jnp.bfloat16)
        key = (key * cosine + turn_half(key) * sine).astype(jnp.bfloat16)
        turned_ref[pl.ds(begin, head_dim), :] = query
        turned_ref[pl.ds(width + begin, head_dim), :] = key
        turned_ref[pl.ds(2 * width + begin, head_dim), :] = value
        mixed, sums = [], []
        for at in range(rows // block):
            span = slice(at * block, (at + 1) * block)
            scores = dot_over(key[:, span], query[:, span], 0, 0) * scale
            scores = jnp.where(allowed_ref[span, :] > 0.5, scores, masked_value)
            top = jnp.max(scores, axis=0, keepdims=True)
            raised = jnp.exp(scores - top)
            total = jnp.sum(raised, axis=0, keepdims=True)
            sums.append(top + jnp.log(total))
            probs = (raised / total).astype(jnp.bfloat16)
            mixed.append(dot_plain(value[:, span], probs))
        logsum_out[pl.ds(head, 1), :] = jnp.concatenate(sums, axis=1)
        mixed_turned[pl.ds(begin, head_dim), :] = jnp.concatenate(mixed, axis=1).astype(jnp.bfloat16)
        return 0

    lax.fori_loop(0, heads, one_head, 0, unroll=2)
    store(turned_ref, turned_hbm)
    split(mixed_turned, "mixed", rest, places["mixed"])
    store(rest, rest_hbm, places["mixed"], half_rows)
    mixed = mixed_turned[...].T
    loads[6].wait()
    resid_one = embedded_ref[...] + dot_plain(mixed, merge_ref[...])
    resid_ref[...] = resid_one
    scale_two = lax.rsqrt(jnp.mean(resid_one * resid_one, axis=1, keepdims=True) + epsilon)
    normed_two = (resid_one * scale_two * gain_second_ref[...][None, :]).astype(jnp.bfloat16)
    flip_ref[...] = normed_two.T
    split(flip_ref, "normed_two", later, places["normed_two"])
    store(later, later_hbm, places["normed_two"], half_rows)

    outer = cotangent_ref[...] * valid
    head_back = (outer * sigma_rows).astype(jnp.bfloat16)
    loads[7].wait()
    resid_back = dot_over(head_back, head_ref[...], 1, 1)
    back_ref[...] = resid_back
    branch_back = resid_back.astype(jnp.bfloat16)
    flip_ref[...] = branch_back.T
    split(flip_ref, "branch", soon, 0)

    loads[9].wait()
    upper_pre = dot_plain(normed_two, grow_ref[...])
    upper_ref[...] = upper_pre
    active = (upper_pre * logistic(upper_pre)).astype(jnp.bfloat16)
    put_tiles(soon, half_rows, active)
    store(soon, soon_hbm)
    loads[8].wait()
    upper_pre = upper_ref[...]
    gate = logistic(upper_pre)
    slope = gate * (1.0 + upper_pre * (1.0 - gate))
    upper_back = (dot_over(branch_back, shrink_ref[...], 1, 1) * slope).astype(jnp.bfloat16)
    put_tiles(later, places["upper"], upper_back)
    store(later, later_hbm, places["upper"], width)
    resid_low = (resid_ref[...] + dot_plain(active, shrink_ref[...])).astype(jnp.bfloat16)
    flip_ref[...] = resid_low.T
    split(flip_ref, "resid", later, places["resid"])
    store(later, later_hbm, places["resid"], half_rows)
    later[places["head"] : places["head"] + wide, :] = head_back.astype(jnp.float32).T
    store(later, later_hbm, places["head"], wide)

    normed_back = dot_over(upper_back, grow_ref[...], 1, 1)
    resid_one = resid_ref[...]
    second_out[...] = jnp.sum(normed_back * resid_one * scale_two, axis=0, keepdims=True)
    through = normed_back * gain_second_ref[...][None, :]
    inner = jnp.mean(through * resid_one, axis=1, keepdims=True)
    middle = back_ref[...] + scale_two * through - resid_one * (scale_two * scale_two * scale_two * inner)
    middle_ref[...] = middle
    store(middle_ref, middle_hbm)
    put_tiles(rest, places["middle"], middle.astype(jnp.bfloat16))
    store(rest, rest_hbm, places["middle"], width)

    head_out = dot_plain(resid_low, head_ref[...])
    predictions_ref[...] = valid * (head_out * sigma_rows + center_rows)
    gather = belongs_back(rows, count, patches, jnp.float32)
    sigma_sum_out[...] = dot_exact(gather, outer * head_out)
    center_sum_out[...] = dot_exact(gather, outer)
    for copy in stores:
        copy.wait()


def front(place, lengths, series, flags, cotangent, tables, weights, heads):
    lift, mix, skip, gain_first, joint, merge, gain_second, grow, shrink, head = weights
    rows, horizon = cotangent.shape
    width = mix.shape[0]
    half = width // 2
    count = series.shape[0]
    f32, bf16 = jnp.float32, jnp.bfloat16
    vmem = pl.BlockSpec(memory_space=pltpu.VMEM)
    smem = pl.BlockSpec(memory_space=pltpu.SMEM)
    hbm = pl.BlockSpec(memory_space=pl.ANY)
    shape = jax.ShapeDtypeStruct
    packs = [
        (len(OWN) * half, rows),
        (half + width, rows),
        (later_rows(width, horizon)["end"], rows),
        (rest_rows(width)["end"], rows),
    ]
    outs = [
        TOKEN,
        shape((rows, horizon), f32),
        shape((rows, lift.shape[0]), bf16),
        shape((heads, rows), f32),
        shape((count, horizon), f32),
        shape((count, horizon), f32),
        shape((1, width), f32),
        shape((rows, width), f32),
        shape((rows, width), f32),
        shape((3 * width, rows), bf16),
    ] + [shape(pack, f32) for pack in packs]
    scratch = [
        pltpu.VMEM(lift.shape, bf16),
        pltpu.VMEM(mix.shape, bf16),
        pltpu.VMEM(skip.shape, bf16),
        pltpu.VMEM((3, width, width), bf16),
        pltpu.VMEM(merge.shape, bf16),
        pltpu.VMEM(grow.shape, bf16),
        pltpu.VMEM(shrink.shape, bf16),
        pltpu.VMEM(head.shape, bf16),
        pltpu.VMEM((rows, width), f32),
        pltpu.VMEM((rows, width), f32),
        pltpu.VMEM((3 * width, rows), f32),
        pltpu.VMEM((3 * width, rows), bf16),
        pltpu.VMEM((width, rows), bf16),
        pltpu.VMEM((rows, BLOCK), f32),
        pltpu.VMEM((rows, width), f32),
        pltpu.VMEM((rows, width), f32),
        pltpu.VMEM((rows, width), f32),
        pltpu.VMEM((width, rows), bf16),
    ] + [pltpu.VMEM(pack, f32) for pack in packs]
    scratch += [pltpu.SemaphoreType.DMA((10,)), pltpu.SemaphoreType.DMA((18,))]
    return pl.pallas_call(
        functools.partial(front_kernel, heads),
        out_shape=outs,
        in_specs=[smem, smem] + [vmem] * 7 + [hbm] * 8,
        out_specs=[vmem] * 7 + [hbm] * 7,
        scratch_shapes=scratch,
        compiler_params=pltpu.CompilerParams(vmem_limit_bytes=62 * 1024 * 1024),
        cost_estimate=COST(22.0),
    )(
        lengths,
        place,
        series,
        flags,
        cotangent,
        gain_first,
        gain_second,
        *tables,
        lift,
        mix,
        skip,
        joint,
        merge,
        grow,
        shrink,
        head,
    )


def back_kernel(
    heads,
    lengths_ref,
    place_ref,
    series_ref,
    flags_ref,
    gain_first_ref,
    cosine_ref,
    sine_ref,
    tokens_ref,
    logsum_ref,
    sigma_sum_ref,
    center_sum_ref,
    second_ref,
    middle_ref,
    turned_ref,
    embedded_hbm,
    lift_hbm,
    mix_hbm,
    skip_hbm,
    joint_hbm,
    merge_hbm,
    token_in,
    token_ref,
    series_grad_ref,
    joint_hbm_out,
    last_hbm,
    own_hbm,
    lift_ref,
    mix_ref,
    skip_ref,
    joint_ref,
    merge_ref,
    embedded_ref,
    mixed_turned,
    joint_turned,
    first_ref,
    allowed_ref,
    flip_ref,
    joint_pack,
    last,
    own,
    load_sem,
    store_sem,
):
    rows, width = embedded_ref.shape
    count, points = series_ref.shape
    patches = rows // count
    patch_len = points // patches
    head_dim = width // heads
    half_rows = width // 2
    del token_in
    token_ref[...] = jnp.zeros_like(token_ref)
    loads = [
        pltpu.make_async_copy(source, target, load_sem.at[at])
        for at, (source, target) in enumerate(
            (
                (merge_hbm, merge_ref),
                (joint_hbm, joint_ref),
                (embedded_hbm, embedded_ref),
                (mix_hbm, mix_ref),
                (lift_hbm, lift_ref),
                (skip_hbm, skip_ref),
            )
        )
    ]
    for copy in loads:
        copy.start()
    stores = []

    def store(source, target, first=0, count=None):
        span = pl.ds(first, source.shape[0] - first if count is None else count)
        copy = pltpu.make_async_copy(source.at[span], target.at[span], store_sem.at[len(stores)])
        copy.start()
        stores.append(copy)

    places = last_rows(width, patch_len, rows)

    kept, starts, hot_kept, kept_count, center, shifted, spread, sigma = series_statistics(
        lengths_ref, series_ref, flags_ref, patch_len
    )
    block = allowed_ref.shape[1]
    spread_exact = belongs(rows, count, patches, jnp.float32)
    starts_rows = dot_exact(spread_exact, jnp.broadcast_to(starts.astype(jnp.float32), (count, block)))
    key_at = remainder(iota((rows, block), 0), block)
    query_at = iota((rows, block), 1)
    key_pos, query_pos = remainder(key_at, patches), remainder(query_at, patches)
    allowed_ref[...] = (
        (quotient(key_at, patches) == quotient(query_at, patches))
        & (key_pos <= query_pos)
        & ((key_pos.astype(jnp.float32) >= starts_rows - 0.5) | (key_pos == query_pos))
    ).astype(jnp.float32)
    scale = head_dim ** (-0.5)
    cosine, sine = cosine_ref[...], sine_ref[...]
    loads[0].wait()
    mixed_turned[...] = dot_over(merge_ref[...], middle_ref[...].astype(jnp.bfloat16), 1, 1).astype(jnp.bfloat16)

    def unrotate(gradient):
        return gradient * cosine + turn_half_back(gradient * sine)

    def one_head(head, _):
        begin = pl.multiple_of(head * head_dim, 16)
        query = turned_ref[pl.ds(begin, head_dim), :]
        key = turned_ref[pl.ds(width + begin, head_dim), :]
        value = turned_ref[pl.ds(2 * width + begin, head_dim), :]
        upstream = mixed_turned[pl.ds(begin, head_dim), :]
        logsum = logsum_ref[pl.ds(head, 1), :]
        query_parts, key_parts, value_parts = [], [], []
        for at in range(rows // block):
            span = slice(at * block, (at + 1) * block)
            query_in, key_in, value_in, up = query[:, span], key[:, span], value[:, span], upstream[:, span]
            scores = dot_over(key_in, query_in, 0, 0) * scale
            scores = jnp.where(allowed_ref[span, :] > 0.5, scores, masked_value)
            probs = jnp.exp(scores - logsum[:, span])
            value_parts.append(dot_over(up, probs.astype(jnp.bfloat16), 1, 1))
            probs_back = dot_over(value_in, up, 0, 0)
            inner = jnp.sum(probs * probs_back, axis=0, keepdims=True)
            scores_back = (probs * (probs_back - inner) * scale).astype(jnp.bfloat16)
            query_parts.append(dot_plain(key_in, scores_back))
            key_parts.append(dot_over(query_in, scores_back, 1, 1))
        for at, parts in enumerate((query_parts, key_parts, value_parts)):
            result = jnp.concatenate(parts, axis=1)
            if at < 2:
                result = unrotate(result)
            result = result.astype(jnp.bfloat16)
            joint_turned[pl.ds(at * width + begin, head_dim), :] = result
            joint_pack[pl.ds(at * width + begin, head_dim), :] = result.astype(jnp.float32)
        return 0

    lax.fori_loop(0, heads, one_head, 0, unroll=2)
    store(joint_pack, joint_hbm_out)
    loads[1].wait()
    tile = rows
    for part in range(width // tile):
        span = slice(part * tile, (part + 1) * tile)
        first_ref[:, span] = dot_plain(joint_ref[span, :], joint_turned[...]).T
    loads[2].wait()
    embedded = embedded_ref[...]
    first_back = first_ref[...]
    scale_one = lax.rsqrt(jnp.mean(embedded * embedded, axis=1, keepdims=True) + epsilon)
    first_sum = jnp.sum(first_back * embedded * scale_one, axis=0, keepdims=True)
    through = first_back * gain_first_ref[...][None, :]
    inner = jnp.mean(through * embedded, axis=1, keepdims=True)
    embed_low = (
        middle_ref[...] + scale_one * through - embedded * (scale_one * scale_one * scale_one * inner)
    ).astype(jnp.bfloat16)
    put_tiles(last, places["embed_tiles"], embed_low)
    flip_ref[...] = embed_low.T
    split_rows(place_ref, flip_ref, last, own.at[pl.ds(0, half_rows)], places["embed"], UNITS)
    store(last, last_hbm, places["embed_tiles"], width + half_rows)
    tokens = tokens_ref[...]
    loads[4].wait()
    hidden_pre = dot_plain(tokens, lift_ref[...])
    gate = logistic(hidden_pre)
    slope = gate * (1.0 + hidden_pre * (1.0 - gate))
    loads[3].wait()
    pre_back = (dot_over(embed_low, mix_ref[...], 1, 1) * slope).astype(jnp.bfloat16)
    flip_ref[...] = pre_back.T
    split_rows(place_ref, flip_ref, last, own.at[pl.ds(half_rows, half_rows)], places["pre"], UNITS)
    store(own, own_hbm)
    last[places["tokens"] : places["sums"], :] = tokens.astype(jnp.float32).T
    row = iota((8, width), 0)
    sums = jnp.where(row == 0, second_ref[...], jnp.where(row == 1, first_sum, 0.0))
    for at in range(width // rows):
        first = places["sums"] + 8 * at
        last[first : first + 8, :] = sums[:, at * rows : (at + 1) * rows]
    store(last, last_hbm, places["pre"])

    loads[5].wait()
    token_back = dot_over(pre_back, lift_ref[...], 1, 1) + dot_over(embed_low, skip_ref[...], 1, 1)
    lane = remainder(iota((2 * patch_len, points), 1), patch_len)
    unfold = (lane == iota((2 * patch_len, points), 0)).astype(jnp.float32)
    inside = own_patch(rows, points, patches, patch_len)
    spread_back_rows = jnp.where(inside, dot_exact(token_back, unfold), 0.0)
    scaled_back = dot_exact(belongs_back(rows, count, patches, jnp.float32), spread_back_rows)
    kept_back = scaled_back * kept
    point_back = kept_back / sigma
    sigma_back = jnp.sum(sigma_sum_ref[...], axis=1, keepdims=True)
    center_back = jnp.sum(center_sum_ref[...], axis=1, keepdims=True)
    center_total = center_back - jnp.sum(point_back, axis=1, keepdims=True)
    sigma_total = sigma_back - jnp.sum(kept_back * shifted, axis=1, keepdims=True) / (sigma * sigma)
    spread_grad = jnp.where(spread > 1.0, sigma_total * 0.5 / sigma, 0.0)
    offset_sum = jnp.sum(hot_kept * 2.0 * shifted, axis=1, keepdims=True)
    center_all = center_total - spread_grad * offset_sum / kept_count
    series_grad_ref[...] = point_back + hot_kept * (center_all + 2.0 * shifted * spread_grad) / kept_count
    for copy in stores:
        copy.wait()


def back(token, place, lengths, series, flags, tables, weights, kept_values, heads):
    lift, mix, skip, gain_first, joint, merge = weights
    tokens, logsum, sigma_sum, center_sum, second_sum, embedded, middle, turned = kept_values
    rows, width = embedded.shape
    half = width // 2
    f32, bf16 = jnp.float32, jnp.bfloat16
    vmem = pl.BlockSpec(memory_space=pltpu.VMEM)
    smem = pl.BlockSpec(memory_space=pltpu.SMEM)
    hbm = pl.BlockSpec(memory_space=pl.ANY)
    shape = jax.ShapeDtypeStruct
    packs = [(3 * width, rows), (last_rows(width, lift.shape[0] // 2, rows)["end"], rows), (2 * half, rows)]
    scratch = [
        pltpu.VMEM(lift.shape, bf16),
        pltpu.VMEM(mix.shape, bf16),
        pltpu.VMEM(skip.shape, bf16),
        pltpu.VMEM(joint.shape, bf16),
        pltpu.VMEM(merge.shape, bf16),
        pltpu.VMEM((rows, width), f32),
        pltpu.VMEM((width, rows), bf16),
        pltpu.VMEM((3 * width, rows), bf16),
        pltpu.VMEM((rows, width), f32),
        pltpu.VMEM((rows, BLOCK), f32),
        pltpu.VMEM((width, rows), bf16),
    ] + [pltpu.VMEM(pack, f32) for pack in packs]
    scratch += [pltpu.SemaphoreType.DMA((6,)), pltpu.SemaphoreType.DMA((4,))]
    return pl.pallas_call(
        functools.partial(back_kernel, heads),
        out_shape=[TOKEN, shape(series.shape, f32)] + [shape(pack, f32) for pack in packs],
        in_specs=[smem, smem] + [vmem] * 12 + [hbm] * 7,
        out_specs=[vmem] * 2 + [hbm] * 3,
        scratch_shapes=scratch,
        compiler_params=pltpu.CompilerParams(vmem_limit_bytes=62 * 1024 * 1024),
        cost_estimate=COST(22.0),
    )(
        lengths,
        place,
        series,
        flags,
        gain_first,
        *tables,
        tokens,
        logsum,
        sigma_sum,
        center_sum,
        second_sum,
        middle,
        turned,
        embedded,
        lift,
        mix,
        skip,
        joint,
        merge,
        token,
    )


def gradient_kernel(place_ref, *refs, terms, arrays, unit, axis, columns):
    sources = refs[:arrays]
    token_ref, send_hbm, keep_hbm = refs[arrays + 1 : arrays + 4]
    result_ref, left_raw, left_ref, right_raw, load_sem, store_sem = refs[arrays + 4 :]
    token_ref[...] = jnp.zeros_like(token_ref)
    if axis == "z":
        height, mine = unit // 2, place_ref[3] & 1
        starts = [group * unit + half * height for half in (1 - mine, mine) for group in range(4)]
    else:
        height, mine, core = unit, place_ref[1], place_ref[0]
        stride, across = 1 + core, 2 - core
        starts = [(stride * side + across * other) * unit for side in (1 - mine, mine) for other in (0, 1)]
    total = 4 * unit
    rows = left_raw.shape[2]
    loads = []

    def load(source, first, target):
        copy = pltpu.make_async_copy(sources[source].at[pl.ds(first, target.shape[0])], target, load_sem.at[len(loads)])
        copy.start()
        loads.append(copy)
        return copy

    lefts, rights = [], []
    for at, (own, own_row, other, other_row, near, far, row, kind, width, _) in enumerate(terms):
        if kind != "sum":
            lefts.append((load(own, own_row, left_raw.at[2 * at]), load(other, other_row, left_raw.at[2 * at + 1])))
        else:
            lefts.append(())
        tiles = []
        place = sum(term[8] for term in terms[:at]) * 2
        for tile in range(0, width, rows):
            size = min(rows, width - tile)
            spots = [right_raw.at[pl.ds(place + 2 * tile + side * size, size)] for side in (0, 1)]
            tiles.append((tile, size, spots, [load(side, row + tile, spot) for side, spot in zip((near, far), spots)]))
        rights.append(tiles)
    stores = []

    def store(begin, width):
        for half, target in enumerate((send_hbm, keep_hbm)):
            copy = pltpu.make_async_copy(
                result_ref.at[pl.ds(half * total // 2, total // 2), pl.ds(begin, width)],
                target.at[:, pl.ds(begin, width)],
                store_sem.at[len(stores)],
            )
            copy.start()
            stores.append(copy)

    for at, (_, _, _, _, _, _, _, kind, _, begin) in enumerate(terms):
        for copy in lefts[at]:
            copy.wait()
        if kind == "sum":
            for _, _, _, copies in rights[at]:
                for copy in copies:
                    copy.wait()
            place = sum(term[8] for term in terms[:at]) * 2
            height_in = terms[at][8]
            both = right_raw[place : place + height_in, :] + right_raw[place + height_in : place + 2 * height_in, :]
            lanes = jnp.concatenate([both[part : part + 8, :] for part in range(0, height_in, 8)], axis=1)
            tall = jnp.concatenate([lanes, jnp.zeros((BLOCK - 8, lanes.shape[1]), jnp.float32)], axis=0).T
            unit_rows = tall.reshape(UNITS // 2, 2, unit, BLOCK)
            mine_rows = jnp.where(place_ref[0] == 0, unit_rows[:, 0], unit_rows[:, 1]).reshape(total, BLOCK)
            left_raw[0, :, :BLOCK] = mine_rows
            for slot, first in enumerate(starts):
                result_ref[slot * height : (slot + 1) * height, begin : begin + BLOCK] = left_raw[
                    0, pl.ds(pl.multiple_of(first, 16), height), :BLOCK
                ]
            store(begin, BLOCK)
            continue
        for slot, first in enumerate(starts):
            first = pl.multiple_of(first, 16)
            span = slice(slot * height, (slot + 1) * height)
            for side in (0, 1):
                left_ref[span, side * rows : (side + 1) * rows] = left_raw[2 * at + side, pl.ds(first, height), :].astype(
                    jnp.bfloat16
                )
        left = left_ref[...]
        for tile, size, spots, copies in rights[at]:
            for copy in copies:
                copy.wait()
            near, far = (spot[...].astype(jnp.bfloat16) for spot in spots)
            if kind == "tiles":
                result = dot_plain(left, jnp.concatenate([near, far], axis=0))
            else:
                right = jnp.concatenate([near, far], axis=1)
                if kind != "turned":
                    blank = jnp.zeros_like(right)
                    right = jnp.concatenate((right, blank) if kind == "low" else (blank, right), axis=0)
                result = dot_over(left, right, 1, 1)
            span = slice(begin + tile, begin + tile + result.shape[1])
            if kind == "high":
                result_ref[:, span] += result
            else:
                result_ref[:, span] = result
            if kind != "low":
                store(begin + tile, result.shape[1])
    for copy in stores:
        copy.wait()


def weight_gradient(token, place, axis, arrays, terms, unit, columns):
    rows = arrays[0].shape[1]
    total = 4 * unit
    hbm = pl.BlockSpec(memory_space=pl.ANY)
    vmem = pl.BlockSpec(memory_space=pltpu.VMEM)
    out_type = jax.ShapeDtypeStruct((total // 2, columns), jnp.float32)
    widths = sum(term[8] for term in terms)
    copies = sum(2 + 2 * (-(-term[8] // rows)) for term in terms)
    return pl.pallas_call(
        functools.partial(
            gradient_kernel, terms=terms, arrays=len(arrays), unit=unit, axis=axis, columns=columns
        ),
        in_specs=[pl.BlockSpec(memory_space=pltpu.SMEM)] + [hbm] * (len(arrays) + 1),
        out_specs=[vmem, hbm, hbm],
        scratch_shapes=[
            pltpu.VMEM((total, columns), jnp.float32),
            pltpu.VMEM((2 * len(terms), total, rows), jnp.float32),
            pltpu.VMEM((total, 2 * rows), jnp.bfloat16),
            pltpu.VMEM((2 * widths, rows), jnp.float32),
            pltpu.SemaphoreType.DMA((copies,)),
            pltpu.SemaphoreType.DMA((copies,)),
        ],
        out_shape=[TOKEN, out_type, out_type],
        compiler_params=pltpu.CompilerParams(vmem_limit_bytes=16 * 1024 * 1024),
        cost_estimate=COST(4.0),
    )(place, *arrays, token)


def part_kernel(place_ref, *refs, inputs, parts):
    token_ref, outputs = refs[inputs + 1], refs[inputs + 2 :]
    step = pl.program_id(0)

    @pl.when(jnp.logical_and(step == 0, pl.program_id(1) == 0))
    def _():
        token_ref[...] = jnp.zeros_like(token_ref)

    for at in range(parts):

        @pl.when(step == at)
        def _(at=at):
            total = refs[0][...]
            for ref in refs[1:inputs]:
                total = total + ref[...]
            outputs[at][...] = total


def add_parts(token, place, arrays, parts, which):
    before, _, after, columns = arrays[0].shape
    tiles = 1
    while after % (2 * tiles) == 0 and (after // (2 * tiles)) % 8 == 0 and before * after * columns * 4 // tiles > TILE_BYTES:
        tiles *= 2
    height = after // tiles

    def index_in(step, tile, place_ref):
        mine = place_ref[which] & (parts - 1)
        chosen = mine ^ ((step + 1) & (parts - 1))
        return (0, chosen, tile, 0)

    def index_out(step, tile, place_ref, at):
        return (0, jnp.where(step == at, tile, jnp.where(step < at, 0, tiles - 1)), 0)

    block_in = pl.BlockSpec((before, None, height, columns), index_in)
    blocks_out = [
        pl.BlockSpec((before, height, columns), functools.partial(index_out, at=at)) for at in range(parts)
    ]
    result = jax.ShapeDtypeStruct((before, after, columns), jnp.float32)
    return pl.pallas_call(
        functools.partial(part_kernel, inputs=len(arrays), parts=parts),
        grid_spec=pltpu.PrefetchScalarGridSpec(
            num_scalar_prefetch=1,
            grid=(parts, tiles),
            in_specs=[block_in] * len(arrays) + [pl.BlockSpec(memory_space=pl.ANY)],
            out_specs=[pl.BlockSpec(TOKEN.shape, lambda i, t, s: (0, 0))] + blocks_out,
        ),
        out_shape=[TOKEN] + [result] * parts,
        compiler_params=pltpu.CompilerParams(vmem_limit_bytes=8 * 1024 * 1024),
        cost_estimate=COST(1.5),
    )(place, *arrays, token)


class Layout:
    def __init__(self, mesh_shape):
        self.wide = mesh_shape["wide"]
        self.narrow = mesh_shape["narrow"]
        self.total = self.wide * self.narrow
        self.paired = self.wide == 8 and self.narrow == 4

    def flip(self, bit):
        return [(i, i ^ bit) for i in range(self.total)]

    def middle(self):
        swapped = (0, 2, 1, 3)
        return [(i, (i & ~3) | swapped[i & 3]) for i in range(self.total)]

    def across(self, first):
        return [(i, i ^ (8 if (i & 4 == 0) == first else 16)) for i in range(self.total)]

    def position(self):
        wide = lax.axis_index("wide")
        core, x, y = wide % 2, wide // 2 % 2, wide // 4 % 2
        places = (core, jnp.where(core == 0, x, y), jnp.where(core == 0, y, x), lax.axis_index("narrow"))
        if not self.paired:
            places = tuple(jnp.zeros_like(place) for place in places)
        return jnp.stack(places).astype(jnp.int32)


class Piece:
    def __init__(self, layout, place, order, arrays, terms, unit, columns):
        self.layout, self.place, self.order = layout, place, order
        self.arrays, self.terms, self.unit, self.columns = arrays, terms, unit, columns
        self.plan = []
        for axis in order:
            self.plan += ["half", "middle", "part"] if axis == "z" else [axis]
        self.axes = ["b", "a", "half", "part"]
        self.held = None
        self.result = None

    def move(self, array, step):
        layout = self.layout
        pairs = layout.across(step == "a") if step in ("a", "b") else layout.flip(1)
        return lax.ppermute(array, AXES, pairs)

    def advance(self, token):
        rows = self.unit // 4
        if self.held is None:
            step = self.plan.pop(0)
            token, send, keep = weight_gradient(
                token, self.place, self.order[0], self.arrays, self.terms, self.unit, self.columns
            )
            self.axes.remove({"a": "a", "z": "half"}.get(step, step))
            self.held = [keep, self.move(send, step)]
            return token
        dims = [2] * len(self.axes)
        if not self.plan:
            shaped = [array.reshape(1, 1, rows, self.columns) for array in self.held]
            token, whole = add_parts(token, self.place, shaped, 1, 0)
            self.result = whole.reshape(rows, self.columns)
            return token
        step = self.plan.pop(0)
        if step == "middle":
            size = math.prod(dims) * rows
            shaped = [array.reshape(1, 1, size, self.columns) for array in self.held]
            token, whole = add_parts(token, self.place, shaped, 1, 0)
            self.held = [lax.ppermute(whole, AXES, self.layout.middle())]
        elif step == "Y":
            at = self.axes.index("half")
            before, after = math.prod(dims[:at]), math.prod(dims[at + 2 :]) * rows
            shaped = [array.reshape(1, 1, before * 4 * after, self.columns) for array in self.held]
            token, whole = add_parts(token, self.place, shaped, 1, 0)
            whole = whole.reshape(before, 4, after, self.columns)
            got = lax.all_to_all(whole, "narrow", 1, 1, tiled=True)
            self.axes = [axis for axis in self.axes if axis not in ("half", "part")]
            self.held = [got[:, at] for at in range(4)]
        else:
            at = self.axes.index(step)
            before, after = math.prod(dims[:at]), math.prod(dims[at + 1 :]) * rows
            shaped = [array.reshape(before, 2, after, self.columns) for array in self.held]
            token, send, keep = add_parts(token, self.place, shaped, 2, {"a": 1, "b": 2}.get(step, 3))
            self.held = [keep, self.move(send, step)]
            self.axes.remove(step)
        return token


def whole_rows(own, other):
    unit = own.shape[0] // (UNITS // 2)
    pair = jnp.stack([own.reshape(-1, unit, own.shape[1]), other.reshape(-1, unit, own.shape[1])], axis=1)
    return pair.reshape(2 * own.shape[0], own.shape[1])


def whole_tiles(tiles, rows):
    return jnp.concatenate([tiles[at : at + rows] for at in range(0, tiles.shape[0], rows)], axis=1)


def per_device(
    layout,
    series,
    flags,
    lengths,
    lift_weight,
    mix_weight,
    skip_weight,
    gain_first,
    joint_weight,
    merge_weight,
    gain_second,
    grow_weight,
    shrink_weight,
    head_weight,
    cotangent,
):
    count = series.shape[0]
    patches, horizon = cotangent.shape[1:]
    width = mix_weight.shape[0]
    hidden = shrink_weight.shape[0]
    rows = count * patches
    half = width // 2
    tables = rotary_tables(patches, width // HEADS, count)
    place = layout.position()
    weights = (
        lift_weight,
        mix_weight,
        skip_weight,
        gain_first,
        joint_weight,
        merge_weight,
        gain_second,
        grow_weight,
        shrink_weight,
        head_weight,
    )
    (
        token,
        predictions,
        tokens,
        logsum,
        sigma_sum,
        center_sum,
        second_sum,
        embedded,
        middle,
        turned,
        own,
        soon,
        later,
        rest,
    ) = front(place, lengths, series, flags, cotangent.reshape(rows, horizon), tables, weights, HEADS)
    across = lift_weight.shape[0]
    joint_width = joint_weight.shape[1]

    def run_back(token):
        return back(
            token,
            place,
            lengths,
            series,
            flags,
            tables,
            (lift_weight, mix_weight, skip_weight, gain_first, joint_weight, merge_weight),
            (tokens, logsum, sigma_sum, center_sum, second_sum, embedded, middle, turned),
            HEADS,
        )

    at_own = {name: place * half for place, name in enumerate(OWN)}
    at_later = later_rows(width, horizon)
    at_rest = rest_rows(width)
    at_last = last_rows(width, across // 2, rows)
    if layout.paired:
        swap = lambda array: lax.ppermute(array, AXES, layout.flip(4))
        unit = width // UNITS
        soon_got, later_got, rest_got = swap(soon), swap(later), swap(rest)
        pieces = {}

        def piece(name, arrays, terms, columns):
            pieces[name] = Piece(layout, place, ORDERS[name], arrays, terms, unit, columns)

        piece("A", [own, soon, soon_got], ((0, at_own["branch"], 2, 0, 1, 2, half, "tiles", hidden, 0),), hidden)
        piece(
            "B",
            [own, later, later_got],
            (
                (0, at_own["normed_two"], 2, at_later["normed_two"], 1, 2, at_later["upper"], "tiles", hidden, 0),
                (0, at_own["resid"], 2, at_later["resid"], 1, 2, at_later["head"], "turned", horizon, hidden),
            ),
            hidden + horizon,
        )
        piece(
            "C",
            [own, rest, rest_got],
            ((0, at_own["mixed"], 2, at_rest["mixed"], 1, 2, at_rest["middle"], "tiles", width, 0),),
            width,
        )
        joint_names = [name for name in ORDERS if name.startswith("D")]
        for name in PROGRAM:
            if name == "K":
                token, series_grad, joint, last, last_own = run_back(token)
                joint_got, last_got = swap(joint), swap(last)
                span = joint_width // len(joint_names)
                for at, joint_name in enumerate(joint_names):
                    piece(
                        joint_name,
                        [own, rest_got, joint, joint_got],
                        ((0, at_own["normed_one"], 1, at_rest["normed_one"], 2, 3, at * span, "turned", span, 0),),
                        span,
                    )
                piece(
                    "E",
                    [own, rest_got, last, last_got, last_own],
                    (
                        (0, at_own["hidden"], 1, at_rest["hidden"], 2, 3, at_last["embed_tiles"], "tiles", width, 0),
                        (4, half, 3, at_last["pre"], 2, 3, at_last["tokens"], "low", across, width),
                        (4, 0, 3, at_last["embed"], 2, 3, at_last["tokens"], "high", across, width),
                        (0, 0, 0, 0, 2, 3, at_last["sums"], "sum", 8 * width // rows, width + 2 * across),
                    ),
                    width + 2 * across + BLOCK,
                )
            else:
                token = pieces[name].advance(token)
        shrink_rows, grow_head, merge_grad, mix_small = (pieces[name].result for name in "ABCE")
        grow_grad, head_grad = grow_head[:, :hidden], grow_head[:, hidden:]
        joint_grad = jnp.concatenate([pieces[name].result for name in joint_names], axis=1)
        mix_grad = mix_small[:, :width]
        lift_rows = mix_small[:, width : width + across]
        skip_rows = mix_small[:, width + across : width + 2 * across]
        second_grad = mix_small[:, width + 2 * across]
        first_grad = mix_small[:, width + 2 * across + 1]
    else:
        _, series_grad, joint, last, last_own = run_back(token)
        scatter = lambda left, right: lax.psum_scatter(
            dot_plain(left.astype(jnp.bfloat16), right.astype(jnp.bfloat16)), AXES, scatter_dimension=0, tiled=True
        )
        mine = lambda name: own[at_own[name] : at_own[name] + half]
        theirs = lambda name: (
            later[at_later[name] : at_later[name] + half]
            if name in at_later
            else rest[at_rest[name] : at_rest[name] + half]
        )
        tiles = lambda pack, first: whole_tiles(pack[first : first + width], rows)
        shrink_rows = scatter(whole_rows(mine("branch"), soon[:half]), tiles(soon, half))
        grow_grad = scatter(whole_rows(mine("normed_two"), theirs("normed_two")), tiles(later, at_later["upper"]))
        head_grad = scatter(
            whole_rows(mine("resid"), theirs("resid")), later[at_later["head"] : at_later["head"] + horizon].T
        )
        merge_grad = scatter(whole_rows(mine("mixed"), theirs("mixed")), tiles(rest, at_rest["middle"]))
        joint_grad = scatter(whole_rows(mine("normed_one"), theirs("normed_one")), joint.T)
        mix_grad = scatter(whole_rows(mine("hidden"), theirs("hidden")), tiles(last, at_last["embed_tiles"]))
        lift_rows = scatter(whole_rows(last_own[half:], last[at_last["pre"] : at_last["pre"] + half]), tokens)
        skip_rows = scatter(whole_rows(last_own[:half], last[at_last["embed"] : at_last["embed"] + half]), tokens)
        sums = whole_tiles(last[at_last["sums"] : at_last["end"]].reshape(-1, rows), 8)
        sums = lax.psum_scatter(sums[:2].T, AXES, scatter_dimension=0, tiled=True)
        second_grad, first_grad = sums[:, 0], sums[:, 1]
    return (
        predictions.reshape(count, patches, horizon),
        series_grad,
        lift_rows.T,
        mix_grad,
        skip_rows.T,
        first_grad,
        joint_grad,
        merge_grad,
        second_grad,
        grow_grad,
        shrink_rows.T,
        head_grad,
    )


def solution(mesh):
    both = P(AXES)
    in_specs = (both, both, both) + (P(),) * 10 + (both,)
    out_specs = (
        P(AXES, None, None),
        P(AXES, None),
        P(None, AXES),
        P(AXES, None),
        P(None, AXES),
        P(AXES),
        P(AXES, None),
        P(AXES, None),
        P(AXES),
        P(AXES, None),
        P(None, AXES),
        P(AXES, None),
    )
    return jax.shard_map(
        functools.partial(per_device, Layout(mesh.shape)),
        mesh=mesh,
        in_specs=in_specs,
        out_specs=out_specs,
        check_vma=False,
    )
```

```python
import functools

import jax
import jax.numpy as jnp
import numpy as np
from jax import lax
from jax.experimental import pallas as pl
from jax.experimental.pallas import tpu as pltpu
from jax.sharding import PartitionSpec as P

HEADS = 16
BLOCK = 128

epsilon = 1e-06
masked_value = -1000000000.0
AXES = ("wide", "narrow")


def rotary_tables(patches, head_dim, count):
    exponent = np.arange(head_dim // 2, dtype=np.float32) * np.float32(2.0 / head_dim)
    frequency = np.float32(10000.0) ** (-exponent)
    angles = frequency[:, None] * np.arange(patches, dtype=np.float32)[None, :]
    angles = np.tile(np.concatenate([angles, angles], axis=0), (1, count))
    return jnp.asarray(np.cos(angles)), jnp.asarray(np.sin(angles))


VMEM_GRADIENT = 60
VMEM_COMBINE = 24
ORDERS = {"A": "abY", "B": "zab", "C": "azb", "E": "abz", "D1": "abz", "D2": "azb"}
JOINT_TILES = {"D1": 15, "D2": 15}
PROGRAM = (
    ("F", (), 18),
    ("G", ("A", ), 12),
    ("G", ("B", ), 25),
    ("G", ("C", ), 40),
    ("K", (), 1),
    ("+", ("A", ), 3),
    ("+", ("C", ), 40),
    ("G", ("D2", ), 0),
    ("+", ("B", ), 8),
    ("+", ("A", ), 5),
    ("G", ("D1", ), 3),
    ("+", ("C", ), 8),
    ("G", ("E", ), 0),
    ("+", ("D2", ), 5),
    ("+", ("B", ), 8),
    ("+", ("D1", ), 3),
    ("+", ("A", ), 0),
    ("+", ("D2", ), 3),
    ("+", ("E", ), 5),
    ("+", ("C", ), 3),
    ("+", ("B", ), 3),
    ("+", ("D1", ), 0.3),
    ("+", ("C", ), 1),
    ("+", ("E", ), 0),
    ("+", ("B", ), 0.3),
    ("+", ("C", ), 0),
    ("+", ("D1", ), 0.3),
    ("+", ("D2", ), 40),
    ("+", ("B", ), 0.3),
    ("+", ("E", ), 2),
    ("+", ("D1", ), 5),
    ("+", ("D2", ), 0),
    ("+", ("E", ), 18),
    ("+", ("D2", ), 0),
    ("+", ("D1", ), 18),
    ("+", ("E", ), 3),
)


def dot_plain(left_side, right_side):
    return jnp.dot(left_side, right_side, preferred_element_type=jnp.float32)


def dot_over(left_side, right_side, left_axis, right_axis):
    return lax.dot_general(
        left_side,
        right_side,
        (((left_axis,), (right_axis,)), ((), ())),
        preferred_element_type=jnp.float32,
    )


def dot_exact(left_side, right_side):
    return jnp.dot(
        left_side, right_side, preferred_element_type=jnp.float32, precision=lax.Precision.HIGHEST
    )


def logistic(values):
    return 1.0 / (1.0 + jnp.exp(-values))


def quotient(values, by):
    return lax.shift_right_logical(values, jnp.int32(by.bit_length() - 1))


def remainder(values, by):
    return values & (by - 1)


def iota(shape, axis):
    return lax.broadcasted_iota(jnp.int32, shape, axis)


def series_statistics(lengths_ref, series_ref, flags_ref, patch_len):
    count, points = series_ref.shape
    patches = points // patch_len
    values = series_ref[...]
    kept = 1.0 - flags_ref[...].astype(jnp.float32)
    starts = jnp.zeros((count, 1), jnp.int32)
    row = iota((count, 1), 0)
    for at in range(count):
        starts = jnp.where(row == at, patches - lengths_ref[at], starts)
    hot = (quotient(iota((count, points), 1), patch_len) == starts).astype(jnp.float32)
    hot_kept = hot * kept
    kept_count = jnp.maximum(jnp.sum(hot_kept, axis=1, keepdims=True), 1.0)
    center = jnp.sum(hot_kept * values, axis=1, keepdims=True) / kept_count
    shifted = values - center
    spread = jnp.sum(hot_kept * shifted * shifted, axis=1, keepdims=True) / kept_count
    sigma = jnp.sqrt(jnp.maximum(spread, 1.0))
    return kept, starts, hot_kept, kept_count, center, shifted, spread, sigma


def belongs(rows, count, patches, kind):
    return (quotient(iota((rows, count), 0), patches) == iota((rows, count), 1)).astype(kind)


def belongs_back(rows, count, patches, kind):
    return (quotient(iota((count, rows), 1), patches) == iota((count, rows), 0)).astype(kind)


def own_patch(rows, points, patches, patch_len):
    return quotient(iota((rows, points), 1), patch_len) == remainder(iota((rows, points), 0), patches)


def turn_half(values):
    half = values.shape[0] // 2
    return jnp.concatenate([-values[half:], values[:half]], axis=0)


def turn_half_back(values):
    half = values.shape[0] // 2
    return jnp.concatenate([values[half:], -values[:half]], axis=0)


def split_rows(place_ref, turned, other_ref, own_ref, first, units):
    core = place_ref[0]
    unit = turned.shape[0] // units
    for at in range(units // 2):
        mine = pl.multiple_of((2 * at + core) * unit, 16)
        theirs = pl.multiple_of((2 * at + 1 - core) * unit, 16)
        own_ref[at * unit : (at + 1) * unit, :] = turned[pl.ds(mine, unit), :].astype(jnp.float32)
        other_ref[first + at * unit : first + (at + 1) * unit, :] = turned[pl.ds(theirs, unit), :].astype(jnp.float32)


def put_tiles(ref, first, values):
    rows, width = values.shape
    for at in range(width // rows):
        ref[first + at * rows : first + (at + 1) * rows, :] = values[:, at * rows : (at + 1) * rows].astype(jnp.float32)


UNITS = 8
TOKEN = jax.ShapeDtypeStruct((8, 128), jnp.float32)


def expect(microseconds):
    return pl.CostEstimate(flops=int(microseconds * 1.15e9), bytes_accessed=0, transcendentals=0)


OWN = ("branch", "normed_two", "resid", "mixed", "normed_one", "hidden")


def stack_rows(*heights):
    places, at = {}, 0
    for name, height in heights:
        places[name] = at
        at += height
    places["end"] = at
    return places


def later_rows(width, horizon):
    half = width // 2
    return stack_rows(("normed_two", half), ("upper", width), ("resid", half), ("head", horizon))


def rest_rows(width):
    half = width // 2
    return stack_rows(
        ("mixed", half),
        ("middle", width),
        ("normed_one", half),
        ("hidden", half),
    )


def last_rows(width, patch_len, rows):
    half = width // 2
    return stack_rows(
        ("embed_tiles", width),
        ("embed", half),
        ("pre", half),
        ("tokens", 2 * patch_len),
        ("sums", 8 * width // rows),
    )


def front_kernel(
    heads,
    lengths_ref,
    place_ref,
    series_ref,
    flags_ref,
    cotangent_ref,
    gain_first_ref,
    gain_second_ref,
    cosine_ref,
    sine_ref,
    lift_hbm,
    mix_hbm,
    skip_hbm,
    joint_hbm,
    merge_hbm,
    grow_hbm,
    shrink_hbm,
    head_hbm,
    token_ref,
    predictions_ref,
    tokens_out,
    logsum_out,
    sigma_sum_out,
    center_sum_out,
    second_out,
    embedded_hbm,
    middle_hbm,
    turned_hbm,
    own_hbm,
    soon_hbm,
    later_hbm,
    rest_hbm,
    lift_ref,
    mix_ref,
    skip_ref,
    joint_ref,
    merge_ref,
    grow_ref,
    shrink_ref,
    head_ref,
    embedded_ref,
    middle_ref,
    joint_turned,
    turned_ref,
    mixed_turned,
    allowed_ref,
    resid_ref,
    upper_ref,
    back_ref,
    flip_ref,
    own,
    soon,
    later,
    rest,
    load_sem,
    store_sem,
):
    rows, width = embedded_ref.shape
    count, points = series_ref.shape
    patches = rows // count
    patch_len = points // patches
    head_dim = width // heads
    half_rows = width // 2
    wide = cotangent_ref.shape[1]
    token_ref[...] = jnp.zeros_like(token_ref)
    loads = [
        pltpu.make_async_copy(lift_hbm, lift_ref, load_sem.at[0]),
        pltpu.make_async_copy(skip_hbm, skip_ref, load_sem.at[1]),
        pltpu.make_async_copy(mix_hbm, mix_ref, load_sem.at[2]),
    ]
    for at in range(3):
        loads.append(
            pltpu.make_async_copy(joint_hbm.at[:, pl.ds(at * width, width)], joint_ref.at[at], load_sem.at[3 + at])
        )
    for at, (source, target) in enumerate(
        ((merge_hbm, merge_ref), (head_hbm, head_ref), (shrink_hbm, shrink_ref), (grow_hbm, grow_ref))
    ):
        loads.append(pltpu.make_async_copy(source, target, load_sem.at[6 + at]))
    for copy in loads:
        copy.start()
    stores = []

    def store(source, target, first=0, count=None):
        span = pl.ds(first, source.shape[0] - first if count is None else count)
        copy = pltpu.make_async_copy(source.at[span], target.at[span], store_sem.at[len(stores)])
        copy.start()
        stores.append(copy)

    def split(turned, name, pack, at):
        first = OWN.index(name) * half_rows
        split_rows(place_ref, turned, pack, own.at[pl.ds(first, half_rows)], at, UNITS)
        store(own, own_hbm, first, half_rows)

    places = later_rows(width, wide) | rest_rows(width)

    kept, starts, _, _, center, shifted, _, sigma = series_statistics(lengths_ref, series_ref, flags_ref, patch_len)
    scaled = (shifted / sigma * kept).astype(jnp.bfloat16)
    flag_values = flags_ref[...].astype(jnp.float32).astype(jnp.bfloat16)
    spread_out = belongs(rows, count, patches, jnp.bfloat16)
    inside = own_patch(rows, points, patches, patch_len)
    lane = iota((points, 2 * patch_len), 1)
    point = remainder(iota((points, 2 * patch_len), 0), patch_len)
    fold_left = (lane == point).astype(jnp.bfloat16)
    fold_right = (lane == point + patch_len).astype(jnp.bfloat16)
    left = jnp.where(inside, dot_plain(spread_out, scaled), 0.0).astype(jnp.bfloat16)
    right = jnp.where(inside, dot_plain(spread_out, flag_values), 0.0).astype(jnp.bfloat16)
    tokens = (dot_plain(left, fold_left) + dot_plain(right, fold_right)).astype(jnp.bfloat16)
    tokens_out[...] = tokens
    spread_exact = belongs(rows, count, patches, jnp.float32)
    sigma_rows = dot_exact(spread_exact, jnp.broadcast_to(sigma, (count, wide)))
    center_rows = dot_exact(spread_exact, jnp.broadcast_to(center, (count, wide)))
    starts_rows = dot_exact(spread_exact, jnp.broadcast_to(starts.astype(jnp.float32), (count, wide)))
    patch_row = remainder(iota((rows, wide), 0), patches).astype(jnp.float32)
    valid = (patch_row >= starts_rows - 0.5).astype(jnp.float32)
    block = allowed_ref.shape[1]
    key_at = remainder(iota((rows, block), 0), block)
    query_at = iota((rows, block), 1)
    key_pos, query_pos = remainder(key_at, patches), remainder(query_at, patches)
    allowed_ref[...] = (
        (quotient(key_at, patches) == quotient(query_at, patches))
        & (key_pos <= query_pos)
        & ((key_pos.astype(jnp.float32) >= starts_rows[:, :1] - 0.5) | (key_pos == query_pos))
    ).astype(jnp.float32)

    loads[0].wait()
    hidden_pre = dot_plain(tokens, lift_ref[...])
    hidden_act = (hidden_pre * logistic(hidden_pre)).astype(jnp.bfloat16)
    flip_ref[...] = hidden_act.T
    split(flip_ref, "hidden", rest, places["hidden"])
    store(rest, rest_hbm, places["hidden"], half_rows)
    loads[1].wait()
    loads[2].wait()
    embedded = dot_plain(hidden_act, mix_ref[...]) + dot_plain(tokens, skip_ref[...])
    embedded_ref[...] = embedded
    store(embedded_ref, embedded_hbm)
    scale_one = lax.rsqrt(jnp.mean(embedded * embedded, axis=1, keepdims=True) + epsilon)
    normed_one = (embedded * scale_one * gain_first_ref[...][None, :]).astype(jnp.bfloat16)
    for at in range(3):
        loads[3 + at].wait()
        tile = rows
        for part in range(width // tile):
            result = dot_plain(normed_one, joint_ref[at, :, part * tile : (part + 1) * tile])
            joint_turned[at * width + part * tile : at * width + (part + 1) * tile, :] = result.T
    flip_ref[...] = normed_one.T
    split(flip_ref, "normed_one", rest, places["normed_one"])
    store(rest, rest_hbm, places["normed_one"], half_rows)

    scale = head_dim ** (-0.5)
    cosine, sine = cosine_ref[...], sine_ref[...]

    def one_head(head, _):
        begin = pl.multiple_of(head * head_dim, 16)
        query = joint_turned[pl.ds(begin, head_dim), :]
        key = joint_turned[pl.ds(width + begin, head_dim), :]
        value = joint_turned[pl.ds(2 * width + begin, head_dim), :].astype(jnp.bfloat16)
        query = (query * cosine + turn_half(query) * sine).astype(jnp.bfloat16)
        key = (key * cosine + turn_half(key) * sine).astype(jnp.bfloat16)
        turned_ref[pl.ds(begin, head_dim), :] = query
        turned_ref[pl.ds(width + begin, head_dim), :] = key
        turned_ref[pl.ds(2 * width + begin, head_dim), :] = value
        mixed, sums = [], []
        for at in range(rows // block):
            span = slice(at * block, (at + 1) * block)
            scores = dot_over(key[:, span], query[:, span], 0, 0) * scale
            scores = jnp.where(allowed_ref[span, :] > 0.5, scores, masked_value)
            top = jnp.max(scores, axis=0, keepdims=True)
            raised = jnp.exp(scores - top)
            total = jnp.sum(raised, axis=0, keepdims=True)
            sums.append(top + jnp.log(total))
            probs = (raised / total).astype(jnp.bfloat16)
            mixed.append(dot_plain(value[:, span], probs))
        logsum_out[pl.ds(head, 1), :] = jnp.concatenate(sums, axis=1)
        mixed_turned[pl.ds(begin, head_dim), :] = jnp.concatenate(mixed, axis=1).astype(jnp.bfloat16)
        return 0

    lax.fori_loop(0, heads, one_head, 0, unroll=2)
    store(turned_ref, turned_hbm)
    split(mixed_turned, "mixed", rest, places["mixed"])
    store(rest, rest_hbm, places["mixed"], half_rows)
    mixed = mixed_turned[...].T
    loads[6].wait()
    resid_one = embedded_ref[...] + dot_plain(mixed, merge_ref[...])
    resid_ref[...] = resid_one
    scale_two = lax.rsqrt(jnp.mean(resid_one * resid_one, axis=1, keepdims=True) + epsilon)
    normed_two = (resid_one * scale_two * gain_second_ref[...][None, :]).astype(jnp.bfloat16)
    flip_ref[...] = normed_two.T
    split(flip_ref, "normed_two", later, places["normed_two"])
    store(later, later_hbm, places["normed_two"], half_rows)

    outer = cotangent_ref[...] * valid
    head_back = (outer * sigma_rows).astype(jnp.bfloat16)
    loads[7].wait()
    resid_back = dot_over(head_back, head_ref[...], 1, 1)
    back_ref[...] = resid_back
    branch_back = resid_back.astype(jnp.bfloat16)
    flip_ref[...] = branch_back.T
    split(flip_ref, "branch", soon, 0)

    loads[9].wait()
    upper_pre = dot_plain(normed_two, grow_ref[...])
    upper_ref[...] = upper_pre
    active = (upper_pre * logistic(upper_pre)).astype(jnp.bfloat16)
    put_tiles(soon, half_rows, active)
    store(soon, soon_hbm)
    loads[8].wait()
    upper_pre = upper_ref[...]
    gate = logistic(upper_pre)
    slope = gate * (1.0 + upper_pre * (1.0 - gate))
    upper_back = (dot_over(branch_back, shrink_ref[...], 1, 1) * slope).astype(jnp.bfloat16)
    put_tiles(later, places["upper"], upper_back)
    store(later, later_hbm, places["upper"], width)
    resid_low = (resid_ref[...] + dot_plain(active, shrink_ref[...])).astype(jnp.bfloat16)
    flip_ref[...] = resid_low.T
    split(flip_ref, "resid", later, places["resid"])
    store(later, later_hbm, places["resid"], half_rows)
    later[places["head"] : places["head"] + wide, :] = head_back.astype(jnp.float32).T
    store(later, later_hbm, places["head"], wide)

    normed_back = dot_over(upper_back, grow_ref[...], 1, 1)
    resid_one = resid_ref[...]
    second_out[...] = jnp.sum(normed_back * resid_one * scale_two, axis=0, keepdims=True)
    through = normed_back * gain_second_ref[...][None, :]
    inner = jnp.mean(through * resid_one, axis=1, keepdims=True)
    middle = back_ref[...] + scale_two * through - resid_one * (scale_two * scale_two * scale_two * inner)
    middle_ref[...] = middle
    store(middle_ref, middle_hbm)
    put_tiles(rest, places["middle"], middle.astype(jnp.bfloat16))
    store(rest, rest_hbm, places["middle"], width)

    head_out = dot_plain(resid_low, head_ref[...])
    predictions_ref[...] = valid * (head_out * sigma_rows + center_rows)
    gather = belongs_back(rows, count, patches, jnp.float32)
    sigma_sum_out[...] = dot_exact(gather, outer * head_out)
    center_sum_out[...] = dot_exact(gather, outer)
    for copy in stores:
        copy.wait()


def front(place, lengths, series, flags, cotangent, tables, weights, heads, cost):
    lift, mix, skip, gain_first, joint, merge, gain_second, grow, shrink, head = weights
    rows, horizon = cotangent.shape
    width = mix.shape[0]
    half = width // 2
    count = series.shape[0]
    f32, bf16 = jnp.float32, jnp.bfloat16
    vmem = pl.BlockSpec(memory_space=pltpu.VMEM)
    smem = pl.BlockSpec(memory_space=pltpu.SMEM)
    hbm = pl.BlockSpec(memory_space=pl.ANY)
    shape = jax.ShapeDtypeStruct
    packs = [
        (len(OWN) * half, rows),
        (half + width, rows),
        (later_rows(width, horizon)["end"], rows),
        (rest_rows(width)["end"], rows),
    ]
    outs = [
        TOKEN,
        shape((rows, horizon), f32),
        shape((rows, lift.shape[0]), bf16),
        shape((heads, rows), f32),
        shape((count, horizon), f32),
        shape((count, horizon), f32),
        shape((1, width), f32),
        shape((rows, width), f32),
        shape((rows, width), f32),
        shape((3 * width, rows), bf16),
    ] + [shape(pack, f32) for pack in packs]
    scratch = [
        pltpu.VMEM(lift.shape, bf16),
        pltpu.VMEM(mix.shape, bf16),
        pltpu.VMEM(skip.shape, bf16),
        pltpu.VMEM((3, width, width), bf16),
        pltpu.VMEM(merge.shape, bf16),
        pltpu.VMEM(grow.shape, bf16),
        pltpu.VMEM(shrink.shape, bf16),
        pltpu.VMEM(head.shape, bf16),
        pltpu.VMEM((rows, width), f32),
        pltpu.VMEM((rows, width), f32),
        pltpu.VMEM((3 * width, rows), f32),
        pltpu.VMEM((3 * width, rows), bf16),
        pltpu.VMEM((width, rows), bf16),
        pltpu.VMEM((rows, BLOCK), f32),
        pltpu.VMEM((rows, width), f32),
        pltpu.VMEM((rows, width), f32),
        pltpu.VMEM((rows, width), f32),
        pltpu.VMEM((width, rows), bf16),
    ] + [pltpu.VMEM(pack, f32) for pack in packs]
    scratch += [pltpu.SemaphoreType.DMA((10,)), pltpu.SemaphoreType.DMA((18,))]
    return pl.pallas_call(
        functools.partial(front_kernel, heads),
        out_shape=outs,
        in_specs=[smem, smem] + [vmem] * 7 + [hbm] * 8,
        out_specs=[vmem] * 7 + [hbm] * 7,
        scratch_shapes=scratch,
        compiler_params=pltpu.CompilerParams(vmem_limit_bytes=62 * 1024 * 1024),
        cost_estimate=expect(cost),
    )(
        lengths,
        place,
        series,
        flags,
        cotangent,
        gain_first,
        gain_second,
        *tables,
        lift,
        mix,
        skip,
        joint,
        merge,
        grow,
        shrink,
        head,
    )


def back_kernel(
    heads,
    lengths_ref,
    place_ref,
    series_ref,
    flags_ref,
    gain_first_ref,
    cosine_ref,
    sine_ref,
    tokens_ref,
    logsum_ref,
    sigma_sum_ref,
    center_sum_ref,
    second_ref,
    middle_ref,
    turned_ref,
    embedded_hbm,
    lift_hbm,
    mix_hbm,
    skip_hbm,
    joint_hbm,
    merge_hbm,
    token_in,
    token_ref,
    series_grad_ref,
    joint_hbm_out,
    last_hbm,
    own_hbm,
    lift_ref,
    mix_ref,
    skip_ref,
    joint_ref,
    merge_ref,
    embedded_ref,
    mixed_turned,
    joint_turned,
    first_ref,
    allowed_ref,
    flip_ref,
    joint_pack,
    last,
    own,
    load_sem,
    store_sem,
):
    rows, width = embedded_ref.shape
    count, points = series_ref.shape
    patches = rows // count
    patch_len = points // patches
    head_dim = width // heads
    half_rows = width // 2
    del token_in
    token_ref[...] = jnp.zeros_like(token_ref)
    loads = [
        pltpu.make_async_copy(source, target, load_sem.at[at])
        for at, (source, target) in enumerate(
            (
                (merge_hbm, merge_ref),
                (joint_hbm, joint_ref),
                (embedded_hbm, embedded_ref),
                (mix_hbm, mix_ref),
                (lift_hbm, lift_ref),
                (skip_hbm, skip_ref),
            )
        )
    ]
    for copy in loads:
        copy.start()
    stores = []

    def store(source, target, first=0, count=None):
        span = pl.ds(first, source.shape[0] - first if count is None else count)
        copy = pltpu.make_async_copy(source.at[span], target.at[span], store_sem.at[len(stores)])
        copy.start()
        stores.append(copy)

    places = last_rows(width, patch_len, rows)

    kept, starts, hot_kept, kept_count, center, shifted, spread, sigma = series_statistics(
        lengths_ref, series_ref, flags_ref, patch_len
    )
    block = allowed_ref.shape[1]
    spread_exact = belongs(rows, count, patches, jnp.float32)
    starts_rows = dot_exact(spread_exact, jnp.broadcast_to(starts.astype(jnp.float32), (count, block)))
    key_at = remainder(iota((rows, block), 0), block)
    query_at = iota((rows, block), 1)
    key_pos, query_pos = remainder(key_at, patches), remainder(query_at, patches)
    allowed_ref[...] = (
        (quotient(key_at, patches) == quotient(query_at, patches))
        & (key_pos <= query_pos)
        & ((key_pos.astype(jnp.float32) >= starts_rows - 0.5) | (key_pos == query_pos))
    ).astype(jnp.float32)
    scale = head_dim ** (-0.5)
    cosine, sine = cosine_ref[...], sine_ref[...]
    loads[0].wait()
    mixed_turned[...] = dot_over(merge_ref[...], middle_ref[...].astype(jnp.bfloat16), 1, 1).astype(jnp.bfloat16)

    def unrotate(gradient):
        return gradient * cosine + turn_half_back(gradient * sine)

    def one_head(head, _):
        begin = pl.multiple_of(head * head_dim, 16)
        query = turned_ref[pl.ds(begin, head_dim), :]
        key = turned_ref[pl.ds(width + begin, head_dim), :]
        value = turned_ref[pl.ds(2 * width + begin, head_dim), :]
        upstream = mixed_turned[pl.ds(begin, head_dim), :]
        logsum = logsum_ref[pl.ds(head, 1), :]
        query_parts, key_parts, value_parts = [], [], []
        for at in range(rows // block):
            span = slice(at * block, (at + 1) * block)
            query_in, key_in, value_in, up = query[:, span], key[:, span], value[:, span], upstream[:, span]
            scores = dot_over(key_in, query_in, 0, 0) * scale
            scores = jnp.where(allowed_ref[span, :] > 0.5, scores, masked_value)
            probs = jnp.exp(scores - logsum[:, span])
            value_parts.append(dot_over(up, probs.astype(jnp.bfloat16), 1, 1))
            probs_back = dot_over(value_in, up, 0, 0)
            inner = jnp.sum(probs * probs_back, axis=0, keepdims=True)
            scores_back = (probs * (probs_back - inner) * scale).astype(jnp.bfloat16)
            query_parts.append(dot_plain(key_in, scores_back))
            key_parts.append(dot_over(query_in, scores_back, 1, 1))
        for at, parts in enumerate((query_parts, key_parts, value_parts)):
            result = jnp.concatenate(parts, axis=1)
            if at < 2:
                result = unrotate(result)
            result = result.astype(jnp.bfloat16)
            joint_turned[pl.ds(at * width + begin, head_dim), :] = result
            joint_pack[pl.ds(at * width + begin, head_dim), :] = result.astype(jnp.float32)
        return 0

    lax.fori_loop(0, heads, one_head, 0, unroll=8)
    store(joint_pack, joint_hbm_out)
    loads[1].wait()
    tile = rows
    for part in range(width // tile):
        span = slice(part * tile, (part + 1) * tile)
        first_ref[:, span] = dot_plain(joint_ref[span, :], joint_turned[...]).T
    loads[2].wait()
    embedded = embedded_ref[...]
    first_back = first_ref[...]
    scale_one = lax.rsqrt(jnp.mean(embedded * embedded, axis=1, keepdims=True) + epsilon)
    first_sum = jnp.sum(first_back * embedded * scale_one, axis=0, keepdims=True)
    through = first_back * gain_first_ref[...][None, :]
    inner = jnp.mean(through * embedded, axis=1, keepdims=True)
    embed_low = (
        middle_ref[...] + scale_one * through - embedded * (scale_one * scale_one * scale_one * inner)
    ).astype(jnp.bfloat16)
    put_tiles(last, places["embed_tiles"], embed_low)
    flip_ref[...] = embed_low.T
    split_rows(place_ref, flip_ref, last, own.at[pl.ds(0, half_rows)], places["embed"], UNITS)
    store(last, last_hbm, places["embed_tiles"], width + half_rows)
    tokens = tokens_ref[...]
    loads[4].wait()
    hidden_pre = dot_plain(tokens, lift_ref[...])
    gate = logistic(hidden_pre)
    slope = gate * (1.0 + hidden_pre * (1.0 - gate))
    loads[3].wait()
    pre_back = (dot_over(embed_low, mix_ref[...], 1, 1) * slope).astype(jnp.bfloat16)
    flip_ref[...] = pre_back.T
    split_rows(place_ref, flip_ref, last, own.at[pl.ds(half_rows, half_rows)], places["pre"], UNITS)
    store(own, own_hbm)
    last[places["tokens"] : places["sums"], :] = tokens.astype(jnp.float32).T
    row = iota((8, width), 0)
    sums = jnp.where(row == 0, second_ref[...], jnp.where(row == 1, first_sum, 0.0))
    for at in range(width // rows):
        first = places["sums"] + 8 * at
        last[first : first + 8, :] = sums[:, at * rows : (at + 1) * rows]
    store(last, last_hbm, places["pre"])

    loads[5].wait()
    token_back = dot_over(pre_back, lift_ref[...], 1, 1) + dot_over(embed_low, skip_ref[...], 1, 1)
    lane = remainder(iota((2 * patch_len, points), 1), patch_len)
    unfold = (lane == iota((2 * patch_len, points), 0)).astype(jnp.float32)
    inside = own_patch(rows, points, patches, patch_len)
    spread_back_rows = jnp.where(inside, dot_exact(token_back, unfold), 0.0)
    scaled_back = dot_exact(belongs_back(rows, count, patches, jnp.float32), spread_back_rows)
    kept_back = scaled_back * kept
    point_back = kept_back / sigma
    sigma_back = jnp.sum(sigma_sum_ref[...], axis=1, keepdims=True)
    center_back = jnp.sum(center_sum_ref[...], axis=1, keepdims=True)
    center_total = center_back - jnp.sum(point_back, axis=1, keepdims=True)
    sigma_total = sigma_back - jnp.sum(kept_back * shifted, axis=1, keepdims=True) / (sigma * sigma)
    spread_grad = jnp.where(spread > 1.0, sigma_total * 0.5 / sigma, 0.0)
    offset_sum = jnp.sum(hot_kept * 2.0 * shifted, axis=1, keepdims=True)
    center_all = center_total - spread_grad * offset_sum / kept_count
    series_grad_ref[...] = point_back + hot_kept * (center_all + 2.0 * shifted * spread_grad) / kept_count
    for copy in stores:
        copy.wait()


def back(token, place, lengths, series, flags, tables, weights, kept_values, heads, cost):
    lift, mix, skip, gain_first, joint, merge = weights
    tokens, logsum, sigma_sum, center_sum, second_sum, embedded, middle, turned = kept_values
    rows, width = embedded.shape
    half = width // 2
    f32, bf16 = jnp.float32, jnp.bfloat16
    vmem = pl.BlockSpec(memory_space=pltpu.VMEM)
    smem = pl.BlockSpec(memory_space=pltpu.SMEM)
    hbm = pl.BlockSpec(memory_space=pl.ANY)
    shape = jax.ShapeDtypeStruct
    packs = [(3 * width, rows), (last_rows(width, lift.shape[0] // 2, rows)["end"], rows), (2 * half, rows)]
    scratch = [
        pltpu.VMEM(lift.shape, bf16),
        pltpu.VMEM(mix.shape, bf16),
        pltpu.VMEM(skip.shape, bf16),
        pltpu.VMEM(joint.shape, bf16),
        pltpu.VMEM(merge.shape, bf16),
        pltpu.VMEM((rows, width), f32),
        pltpu.VMEM((width, rows), bf16),
        pltpu.VMEM((3 * width, rows), bf16),
        pltpu.VMEM((rows, width), f32),
        pltpu.VMEM((rows, BLOCK), f32),
        pltpu.VMEM((width, rows), bf16),
    ] + [pltpu.VMEM(pack, f32) for pack in packs]
    scratch += [pltpu.SemaphoreType.DMA((6,)), pltpu.SemaphoreType.DMA((4,))]
    return pl.pallas_call(
        functools.partial(back_kernel, heads),
        out_shape=[TOKEN, shape(series.shape, f32)] + [shape(pack, f32) for pack in packs],
        in_specs=[smem, smem] + [vmem] * 12 + [hbm] * 7,
        out_specs=[vmem] * 2 + [hbm] * 3,
        scratch_shapes=scratch,
        compiler_params=pltpu.CompilerParams(vmem_limit_bytes=62 * 1024 * 1024),
        cost_estimate=expect(cost),
    )(
        lengths,
        place,
        series,
        flags,
        gain_first,
        *tables,
        tokens,
        logsum,
        sigma_sum,
        center_sum,
        second_sum,
        middle,
        turned,
        embedded,
        lift,
        mix,
        skip,
        joint,
        merge,
        token,
    )


def gradient_kernel(place_ref, *refs, pieces, arrays, unit):
    sources = refs[:arrays]
    token_ref, outputs = refs[arrays + 1], refs[arrays + 2 : arrays + 2 + 2 * len(pieces)]
    result_ref, left_raw, left_ref, right_raw, load_sem, store_sem = refs[arrays + 2 + 2 * len(pieces) :]
    token_ref[...] = jnp.zeros_like(token_ref)
    total = 4 * unit
    rows = left_raw.shape[2]
    loads, stores, lefts, rights = [], [], {}, []

    def load(source, first, target):
        copy = pltpu.make_async_copy(sources[source].at[pl.ds(first, target.shape[0])], target, load_sem.at[len(loads)])
        copy.start()
        loads.append(copy)
        return copy

    place = 0
    for _, terms in pieces:
        for own, own_row, other, other_row, near, far, row, kind, width in terms:
            key = (own, own_row, other, other_row)
            if kind != "sum" and key not in lefts:
                at = len(lefts)
                copies = [load(own, own_row, left_raw.at[2 * at]), load(other, other_row, left_raw.at[2 * at + 1])]
                lefts[key] = (at, copies)
            tiles = []
            for tile in range(0, width, rows):
                size = min(rows, width - tile)
                spots = [right_raw.at[pl.ds(place + side * size, size)] for side in (0, 1)]
                place += 2 * size
                tiles.append((size, spots, [load(side, row + tile, spot) for side, spot in zip((near, far), spots)]))
            rights.append(tiles)
    waited = set()
    number = 0
    tile_at = 0
    for order, (axis, terms) in enumerate(pieces):
        core = place_ref[0]
        stride, across = 1 + core, 2 - core
        if axis == "z":
            height, mine = unit // 2, place_ref[3] & 1
            groups = [stride * a + across * b for b in (0, 1) for a in (0, 1)]
            starts = [group * unit + half * height for half in (1 - mine, mine) for group in groups]
        else:
            height, mine = unit, place_ref[1]
            starts = [(stride * side + across * other) * unit for side in (1 - mine, mine) for other in (0, 1)]
        out_tile = 0

        def store(count):
            for half in (0, 1):
                copy = pltpu.make_async_copy(
                    result_ref.at[pl.ds(tile_at, count), pl.ds(half * total // 2, total // 2)],
                    outputs[2 * order + half].at[pl.ds(out_tile, count)],
                    store_sem.at[len(stores)],
                )
                copy.start()
                stores.append(copy)

        held = None
        for own, own_row, other, other_row, _, _, _, kind, width in terms:
            tiles = rights[number]
            number += 1
            if kind == "sum":
                for _, spots, copies in tiles:
                    for copy in copies:
                        copy.wait()
                both = tiles[0][1][0][...] + tiles[0][1][1][...]
                lanes = jnp.concatenate([both[part : part + 8, :] for part in range(0, width, 8)], axis=1)
                tall = jnp.concatenate([lanes, jnp.zeros((BLOCK - 8, lanes.shape[1]), jnp.float32)], axis=0).T
                unit_rows = tall.reshape(UNITS // 2, 2, unit, BLOCK)
                spare = left_raw.at[left_raw.shape[0] - 1]
                spare[:, :BLOCK] = jnp.where(place_ref[0] == 0, unit_rows[:, 0], unit_rows[:, 1]).reshape(total, BLOCK)
                for slot, first in enumerate(starts):
                    result_ref[tile_at, slot * height : (slot + 1) * height, :] = spare[
                        pl.ds(pl.multiple_of(first, 16), height), :BLOCK
                    ]
                store(1)
                tile_at += 1
                out_tile += 1
                continue
            at, copies = lefts[(own, own_row, other, other_row)]
            if at not in waited:
                waited.add(at)
                for copy in copies:
                    copy.wait()
            if held != at:
                held = at
                for slot, first in enumerate(starts):
                    first = pl.multiple_of(first, 16)
                    span = slice(slot * height, (slot + 1) * height)
                    for side in (0, 1):
                        left_ref[order % 2, span, side * rows : (side + 1) * rows] = left_raw[
                            2 * at + side, pl.ds(first, height), :
                        ].astype(jnp.bfloat16)
            left = left_ref[order % 2]
            for size, spots, copies in tiles:
                for copy in copies:
                    copy.wait()
                near, far = (spot[...].astype(jnp.bfloat16) for spot in spots)
                if kind == "tiles":
                    result = dot_plain(left, jnp.concatenate([near, far], axis=0))
                else:
                    right = jnp.concatenate([near, far], axis=1)
                    if kind != "turned":
                        blank = jnp.zeros_like(right)
                        right = jnp.concatenate((right, blank) if kind == "low" else (blank, right), axis=0)
                    result = dot_over(left, right, 1, 1)
                count = result.shape[1] // BLOCK
                for part in range(count):
                    piece = result[:, part * BLOCK : (part + 1) * BLOCK]
                    if kind == "high":
                        result_ref[tile_at + part] += piece
                    else:
                        result_ref[tile_at + part] = piece
                if kind != "low":
                    store(count)
                    tile_at += count
                    out_tile += count
    for copy in stores:
        copy.wait()


def tiles_of(terms):
    widths = {"low": 0, "high": BLOCK, "sum": BLOCK}
    return sum(widths.get(term[7], term[8]) for term in terms) // BLOCK


def weight_gradient(token, place, arrays, pieces, unit, cost):
    rows = arrays[0].shape[1]
    total = 4 * unit
    hbm = pl.BlockSpec(memory_space=pl.ANY)
    vmem = pl.BlockSpec(memory_space=pltpu.VMEM)
    counts = [tiles_of(terms) for _, terms in pieces]
    every = [term for _, terms in pieces for term in terms]
    lefts = len({term[:4] for term in every if term[7] != "sum"})
    copies = 2 * lefts + sum(2 * (-(-term[8] // rows)) for term in every)
    shapes = [jax.ShapeDtypeStruct((count, total // 2, BLOCK), jnp.float32) for count in counts for _ in (0, 1)]
    results = pl.pallas_call(
        functools.partial(gradient_kernel, pieces=pieces, arrays=len(arrays), unit=unit),
        in_specs=[pl.BlockSpec(memory_space=pltpu.SMEM)] + [hbm] * (len(arrays) + 1),
        out_specs=[vmem] + [hbm] * len(shapes),
        scratch_shapes=[
            pltpu.VMEM((sum(counts), total, BLOCK), jnp.float32),
            pltpu.VMEM((2 * lefts + 1, total, rows), jnp.float32),
            pltpu.VMEM((2, total, 2 * rows), jnp.bfloat16),
            pltpu.VMEM((2 * sum(term[8] for term in every), rows), jnp.float32),
            pltpu.SemaphoreType.DMA((copies,)),
            pltpu.SemaphoreType.DMA((copies,)),
        ],
        out_shape=[TOKEN] + shapes,
        compiler_params=pltpu.CompilerParams(vmem_limit_bytes=VMEM_GRADIENT * 1024 * 1024),
        cost_estimate=expect(cost),
    )(place, *arrays, token)
    return results[0], [results[1 + 2 * at : 3 + 2 * at] for at in range(len(pieces))]


def combine_kernel(place_ref, *refs, inputs, parts, which, last, spread, passed):
    total = sum(inputs)
    sources = refs[:total]
    token_ref = refs[total + 1]
    results = refs[total + 2 : total + 2 + (len(inputs) if last else 1 if spread else parts)]
    scratch = refs[total + 2 + len(results) :]
    raws, sums, load_sem, store_sem = scratch[:total], scratch[total], scratch[total + 1], scratch[total + 2]
    token_ref[...] = jnp.zeros_like(token_ref)
    mine = place_ref[which] & (parts - 1)
    chosen = [step if spread else mine ^ ((step + 1) & (parts - 1)) for step in range(parts)]
    loads, stores = {}, []
    for step in range(parts):
        for at in range(total):
            copy = pltpu.make_async_copy(
                sources[at].at[:, :, chosen[step]], raws[at].at[step], load_sem.at[step * total + at]
            )
            copy.start()
            loads[step, at] = copy
    for step in range(parts):
        first = 0
        begin = 0
        for group, count in enumerate(inputs):
            for at in range(first, first + count):
                loads[step, at].wait()
            value = raws[first][step]
            for at in range(first + 1, first + count):
                if passed:
                    outside = jnp.logical_or(place_ref[3] == 0, place_ref[3] == 3)
                    value = jnp.where(outside, value, raws[at][step])
                else:
                    value = value + raws[at][step]
            tiles = value.shape[0]
            if last:
                fold = tiles // (results[group].shape[1] // BLOCK)
                tiles //= fold
                for tile in range(tiles):
                    piece = value[tile, 0]
                    for part in range(1, fold):
                        piece = piece + value[part * tiles + tile, 0]
                    results[group][:, tile * BLOCK : (tile + 1) * BLOCK] = piece
            else:
                sums[step, begin : begin + tiles] = value
                copy = pltpu.make_async_copy(
                    sums.at[step, pl.ds(begin, tiles)],
                    results[0].at[step, pl.ds(begin, tiles)] if spread else results[step].at[pl.ds(begin, tiles)],
                    store_sem.at[len(stores)],
                )
                copy.start()
                stores.append(copy)
            begin += tiles
            first += count
    for copy in stores:
        copy.wait()


def combine(token, place, groups, before, parts, which, cost, last=False, spread=False, fold=1, passed=False):
    rows = groups[0][0].shape[1]
    after = rows // (before * parts)
    flat = [array.reshape(array.shape[0], before, parts, after, BLOCK) for group in groups for array in group]
    tiles = [group[0].shape[0] for group in groups]
    hbm = pl.BlockSpec(memory_space=pl.ANY)
    vmem = pl.BlockSpec(memory_space=pltpu.VMEM)
    shape = jax.ShapeDtypeStruct
    if last:
        shapes = [shape((rows, count // fold * BLOCK), jnp.float32) for count in tiles]
    elif spread:
        shapes = [shape((parts, sum(tiles), before, after, BLOCK), jnp.float32)]
    else:
        shapes = [shape((sum(tiles), before, after, BLOCK), jnp.float32)] * parts
    results = pl.pallas_call(
        functools.partial(
            combine_kernel, inputs=tuple(len(group) for group in groups), parts=parts, which=which, last=last, spread=spread, passed=passed
        ),
        in_specs=[pl.BlockSpec(memory_space=pltpu.SMEM)] + [hbm] * (len(flat) + 1),
        out_specs=[vmem] + [vmem if last else hbm] * len(shapes),
        scratch_shapes=[pltpu.VMEM((parts, array.shape[0], before, after, BLOCK), jnp.float32) for array in flat]
        + [
            pltpu.VMEM((1,) * 5 if last else (parts, sum(tiles), before, after, BLOCK), jnp.float32),
            pltpu.SemaphoreType.DMA((parts * len(flat),)),
            pltpu.SemaphoreType.DMA((parts * len(groups),)),
        ],
        out_shape=[TOKEN] + shapes,
        compiler_params=pltpu.CompilerParams(vmem_limit_bytes=VMEM_COMBINE * 1024 * 1024),
        cost_estimate=expect(cost),
    )(place, *flat, token)
    if last or spread:
        return results[0], results[1:]
    return results[0], [result.reshape(sum(tiles), before * after, BLOCK) for result in results[1:]]


class Layout:
    def __init__(self, mesh_shape):
        self.wide = mesh_shape["wide"]
        self.narrow = mesh_shape["narrow"]
        self.total = self.wide * self.narrow
        self.paired = self.wide == 8 and self.narrow == 4

    def flip(self, bit):
        return [(i, i ^ bit) for i in range(self.total)]

    def middle(self):
        swapped = {1: 2, 2: 1}
        return [(i, (i & ~3) | swapped[i & 3] if i & 3 in swapped else i ^ 4) for i in range(self.total)]

    def across(self, first):
        return [(i, i ^ (8 if (i & 4 == 0) == first else 16)) for i in range(self.total)]

    def position(self):
        wide = lax.axis_index("wide")
        core, x, y = wide % 2, wide // 2 % 2, wide // 4 % 2
        places = (core, jnp.where(core == 0, x, y), jnp.where(core == 0, y, x), lax.axis_index("narrow"))
        if not self.paired:
            places = tuple(jnp.zeros_like(place) for place in places)
        return jnp.stack(places).astype(jnp.int32)


class Bundle:
    def __init__(self, names, plan, axes, groups, fold=1, passed=False):
        self.names, self.plan, self.axes, self.groups = names, plan, axes, groups
        self.fold, self.passed = fold, passed


def steps_of(order):
    plan = []
    for axis in order:
        plan += ["half", "middle", "part"] if axis == "z" else [axis]
    return plan


def move(layout, array, step):
    if step == "middle":
        pairs = layout.middle()
    else:
        pairs = layout.across(step == "a") if step in ("a", "b") else layout.flip(1)
    return lax.ppermute(array, AXES, pairs)


def start_bundles(layout, token, place, arrays, names, terms, unit, cost):
    plans = [steps_of(ORDERS[name]) for name in names]
    token, results = weight_gradient(
        token, place, arrays, tuple((ORDERS[name][0], terms[name]) for name in names), unit, cost
    )
    bundles = {}
    for name, plan, (send, keep) in zip(names, plans, results):
        step = plan.pop(0)
        axes = [axis for axis in ("b", "a", "half", "part") if axis != step]
        bundles[name] = Bundle([name], plan, axes, [[keep, move(layout, send, step)]])
    return token, bundles


def advance(layout, token, place, bundles, rows, cost, finished):
    plan, axes = bundles[0].plan, bundles[0].axes
    groups = [group for bundle in bundles for group in bundle.groups]
    names = [name for bundle in bundles for name in bundle.names]
    sizes = [group[0].shape[0] for group in groups]
    if not plan:
        token, results = combine(token, place, groups, 1, 1, 0, cost, last=True, fold=bundles[0].fold)
        wide = results[0] if len(results) == 1 else jnp.concatenate(results, axis=1)
        finished.append((names, wide))
        return token, None
    step, plan = plan[0], plan[1:]
    if step == "middle":
        token, (whole,) = combine(token, place, groups, 1, 1, 0, cost)
        return token, Bundle(names, plan, axes, [[whole, move(layout, whole, step)]], passed=True)
    if step == "Y":
        token, (whole,) = combine(token, place, groups, 1, 4, 0, cost, spread=True)
        got = lax.all_to_all(whole, "narrow", 0, 0, tiled=True)
        return token, Bundle(names, plan, [], [[got.reshape(4 * sum(sizes), rows, BLOCK)]], 4)
    at = axes.index(step)
    which = {"a": 1, "b": 2}.get(step, 3)
    token, (send, keep) = combine(token, place, groups, 2**at, 2, which, cost, passed=bundles[0].passed)
    return token, Bundle(names, plan, [axis for axis in axes if axis != step], [[keep, move(layout, send, step)]])


def whole_rows(own, other):
    unit = own.shape[0] // (UNITS // 2)
    pair = jnp.stack([own.reshape(-1, unit, own.shape[1]), other.reshape(-1, unit, own.shape[1])], axis=1)
    return pair.reshape(2 * own.shape[0], own.shape[1])


def whole_tiles(tiles, rows):
    return jnp.concatenate([tiles[at : at + rows] for at in range(0, tiles.shape[0], rows)], axis=1)


def per_device(
    layout,
    series,
    flags,
    lengths,
    lift_weight,
    mix_weight,
    skip_weight,
    gain_first,
    joint_weight,
    merge_weight,
    gain_second,
    grow_weight,
    shrink_weight,
    head_weight,
    cotangent,
):
    count = series.shape[0]
    patches, horizon = cotangent.shape[1:]
    width = mix_weight.shape[0]
    hidden = shrink_weight.shape[0]
    rows = count * patches
    half = width // 2
    tables = rotary_tables(patches, width // HEADS, count)
    place = layout.position()
    weights = (
        lift_weight,
        mix_weight,
        skip_weight,
        gain_first,
        joint_weight,
        merge_weight,
        gain_second,
        grow_weight,
        shrink_weight,
        head_weight,
    )
    (
        token,
        predictions,
        tokens,
        logsum,
        sigma_sum,
        center_sum,
        second_sum,
        embedded,
        middle,
        turned,
        own,
        soon,
        later,
        rest,
    ) = front(place, lengths, series, flags, cotangent.reshape(rows, horizon), tables, weights, HEADS, PROGRAM[0][2])
    across = lift_weight.shape[0]
    joint_width = joint_weight.shape[1]

    def run_back(token, cost):
        return back(
            token,
            place,
            lengths,
            series,
            flags,
            tables,
            (lift_weight, mix_weight, skip_weight, gain_first, joint_weight, merge_weight),
            (tokens, logsum, sigma_sum, center_sum, second_sum, embedded, middle, turned),
            HEADS,
            cost,
        )

    at_own = {name: place * half for place, name in enumerate(OWN)}
    at_later = later_rows(width, horizon)
    at_rest = rest_rows(width)
    at_last = last_rows(width, across // 2, rows)
    if layout.paired:
        swap = lambda array: lax.ppermute(array, AXES, layout.flip(4))
        unit = width // UNITS
        soon_got, later_got, rest_got = swap(soon), swap(later), swap(rest)
        terms = {
            "A": ((0, at_own["branch"], 2, 0, 1, 2, half, "tiles", hidden),),
            "B": (
                (0, at_own["normed_two"], 4, at_later["normed_two"], 3, 4, at_later["upper"], "tiles", hidden),
                (0, at_own["resid"], 4, at_later["resid"], 3, 4, at_later["head"], "turned", horizon),
            ),
            "C": ((0, at_own["mixed"], 6, at_rest["mixed"], 5, 6, at_rest["middle"], "tiles", width),),
            "E": (
                (0, at_own["hidden"], 6, at_rest["hidden"], 9, 10, at_last["embed_tiles"], "tiles", width),
                (11, half, 10, at_last["pre"], 9, 10, at_last["tokens"], "low", across),
                (11, 0, 10, at_last["embed"], 9, 10, at_last["tokens"], "high", across),
                (0, 0, 0, 0, 9, 10, at_last["sums"], "sum", 8 * width // rows),
            ),
        }
        joint_names = [name for name in ORDERS if name.startswith("D")]
        first = 0
        for name in joint_names:
            span = JOINT_TILES[name] * BLOCK
            terms[name] = ((0, at_own["normed_one"], 6, at_rest["normed_one"], 7, 8, first, "turned", span),)
            first += span
        arrays = [own, soon, soon_got, later, later_got, rest, rest_got]
        bundles, finished = {}, []
        for kind, names, cost in PROGRAM[1:]:
            if kind == "K":
                token, series_grad, joint, last, last_own = run_back(token, cost)
                arrays += [joint, swap(joint), last, swap(last), last_own]
            elif kind == "G":
                used = sorted({index for name in names for term in terms[name] for index in (term[0], *term[2:3], *term[4:6])})
                local = {
                    name: tuple(
                        (used.index(t[0]), t[1], used.index(t[2]), t[3], used.index(t[4]), used.index(t[5]), *t[6:])
                        for t in terms[name]
                    )
                    for name in names
                }
                token, fresh = start_bundles(
                    layout, token, place, [arrays[index] for index in used], names, local, unit, cost
                )
                bundles.update(fresh)
            else:
                token, joined = advance(
                    layout, token, place, [bundles.pop(name) for name in names], unit // 4, cost, finished
                )
                bundles["".join(names)] = joined
        columns = {}
        for names, wide in finished:
            begin = 0
            for name in names:
                span = tiles_of(terms[name]) * BLOCK
                columns[name] = wide[:, begin : begin + span]
                begin += span
        shrink_rows, merge_grad = columns["A"], columns["C"]
        grow_grad, head_grad = columns["B"][:, :hidden], columns["B"][:, hidden:]
        joint_grad = jnp.concatenate([columns[name] for name in joint_names], axis=1)
        mix_small = columns["E"]
        mix_grad = mix_small[:, :width]
        lift_rows = mix_small[:, width : width + across]
        skip_rows = mix_small[:, width + across : width + 2 * across]
        second_grad = mix_small[:, width + 2 * across]
        first_grad = mix_small[:, width + 2 * across + 1]
    else:
        _, series_grad, joint, last, last_own = run_back(token, 1.0)
        scatter = lambda left, right: lax.psum_scatter(
            dot_plain(left.astype(jnp.bfloat16), right.astype(jnp.bfloat16)), AXES, scatter_dimension=0, tiled=True
        )
        mine = lambda name: own[at_own[name] : at_own[name] + half]
        theirs = lambda name: (
            later[at_later[name] : at_later[name] + half]
            if name in at_later
            else rest[at_rest[name] : at_rest[name] + half]
        )
        tiles = lambda pack, first: whole_tiles(pack[first : first + width], rows)
        shrink_rows = scatter(whole_rows(mine("branch"), soon[:half]), tiles(soon, half))
        grow_grad = scatter(whole_rows(mine("normed_two"), theirs("normed_two")), tiles(later, at_later["upper"]))
        head_grad = scatter(
            whole_rows(mine("resid"), theirs("resid")), later[at_later["head"] : at_later["head"] + horizon].T
        )
        merge_grad = scatter(whole_rows(mine("mixed"), theirs("mixed")), tiles(rest, at_rest["middle"]))
        joint_grad = scatter(whole_rows(mine("normed_one"), theirs("normed_one")), joint.T)
        mix_grad = scatter(whole_rows(mine("hidden"), theirs("hidden")), tiles(last, at_last["embed_tiles"]))
        lift_rows = scatter(whole_rows(last_own[half:], last[at_last["pre"] : at_last["pre"] + half]), tokens)
        skip_rows = scatter(whole_rows(last_own[:half], last[at_last["embed"] : at_last["embed"] + half]), tokens)
        sums = whole_tiles(last[at_last["sums"] : at_last["end"]].reshape(-1, rows), 8)
        sums = lax.psum_scatter(sums[:2].T, AXES, scatter_dimension=0, tiled=True)
        second_grad, first_grad = sums[:, 0], sums[:, 1]
    return (
        predictions.reshape(count, patches, horizon),
        series_grad,
        lift_rows.T,
        mix_grad,
        skip_rows.T,
        first_grad,
        joint_grad,
        merge_grad,
        second_grad,
        grow_grad,
        shrink_rows.T,
        head_grad,
    )


def solution(mesh):
    both = P(AXES)
    in_specs = (both, both, both) + (P(),) * 10 + (both,)
    out_specs = (
        P(AXES, None, None),
        P(AXES, None),
        P(None, AXES),
        P(AXES, None),
        P(None, AXES),
        P(AXES),
        P(AXES, None),
        P(AXES, None),
        P(AXES),
        P(AXES, None),
        P(None, AXES),
        P(AXES, None),
    )
    return jax.shard_map(
        functools.partial(per_device, Layout(mesh.shape)),
        mesh=mesh,
        in_specs=in_specs,
        out_specs=out_specs,
        check_vma=False,
    )
```

```python
import functools

import jax
import jax.numpy as jnp
import numpy as np
from jax import lax
from jax.experimental import pallas as pl
from jax.experimental.pallas import tpu as pltpu
from jax.sharding import PartitionSpec as P

HEADS = 16
BLOCK = 128

epsilon = 1e-06
masked_value = -1000000000.0
AXES = ("wide", "narrow")


def rotary_tables(patches, head_dim, count):
    exponent = np.arange(head_dim // 2, dtype=np.float32) * np.float32(2.0 / head_dim)
    frequency = np.float32(10000.0) ** (-exponent)
    angles = frequency[:, None] * np.arange(patches, dtype=np.float32)[None, :]
    angles = np.tile(np.concatenate([angles, angles], axis=0), (1, count))
    return jnp.asarray(np.cos(angles)), jnp.asarray(np.sin(angles))


VMEM_GRADIENT = 60
VMEM_COMBINE = 24
ORDERS = {"A": "abY", "B": "zab", "C": "azb", "E": "abz", "D1": "abz", "D2": "azb"}
JOINT_TILES = {"D1": 15, "D2": 15}
PROGRAM = (
    ("F", (), 2),
    ("G", ("A", ), 18),
    ("G", ("B", ), 25),
    ("G", ("C", ), 5),
    ("K", (), 1),
    ("+", ("A", ), 40),
    ("+", ("C", ), 3),
    ("G", ("D2", ), 3),
    ("+", ("B", ), 12),
    ("+", ("A", ), 18),
    ("G", ("D1", ), 0),
    ("G", ("E", ), 0),
    ("+", ("D2", ), 3),
    ("+", ("B", ), 18),
    ("+", ("C", ), 2),
    ("+", ("A", ), 0),
    ("+", ("D1", ), 2),
    ("+", ("D2", ), 12),
    ("+", ("E", ), 0.3),
    ("+", ("C", ), 0.3),
    ("+", ("B", ), 1),
    ("+", ("D1", ), 3),
    ("+", ("C", ), 2),
    ("+", ("E", ), 0),
    ("+", ("B", ), 2),
    ("+", ("D1", ), 0),
    ("+", ("D2", ), 0.3),
    ("+", ("B", ), 2),
    ("+", ("E", ), 0),
    ("+", ("C", ), 0.3),
    ("+", ("D1", ), 0),
    ("+", ("D2", ), 2),
    ("+", ("E", ), 12),
    ("+", ("D2", ), 0.3),
    ("+", ("D1", ), 2),
    ("+", ("E", ), 12),
)


def dot_plain(left_side, right_side):
    return jnp.dot(left_side, right_side, preferred_element_type=jnp.float32)


def dot_over(left_side, right_side, left_axis, right_axis):
    return lax.dot_general(
        left_side,
        right_side,
        (((left_axis,), (right_axis,)), ((), ())),
        preferred_element_type=jnp.float32,
    )


def dot_exact(left_side, right_side):
    return jnp.dot(
        left_side, right_side, preferred_element_type=jnp.float32, precision=lax.Precision.HIGHEST
    )


def logistic(values):
    return 1.0 / (1.0 + jnp.exp(-values))


def quotient(values, by):
    return lax.shift_right_logical(values, jnp.int32(by.bit_length() - 1))


def remainder(values, by):
    return values & (by - 1)


def iota(shape, axis):
    return lax.broadcasted_iota(jnp.int32, shape, axis)


def series_statistics(lengths_ref, series_ref, flags_ref, patch_len):
    count, points = series_ref.shape
    patches = points // patch_len
    values = series_ref[...]
    kept = 1.0 - flags_ref[...].astype(jnp.float32)
    starts = jnp.zeros((count, 1), jnp.int32)
    row = iota((count, 1), 0)
    for at in range(count):
        starts = jnp.where(row == at, patches - lengths_ref[at], starts)
    hot = (quotient(iota((count, points), 1), patch_len) == starts).astype(jnp.float32)
    hot_kept = hot * kept
    kept_count = jnp.maximum(jnp.sum(hot_kept, axis=1, keepdims=True), 1.0)
    center = jnp.sum(hot_kept * values, axis=1, keepdims=True) / kept_count
    shifted = values - center
    spread = jnp.sum(hot_kept * shifted * shifted, axis=1, keepdims=True) / kept_count
    sigma = jnp.sqrt(jnp.maximum(spread, 1.0))
    return kept, starts, hot_kept, kept_count, center, shifted, spread, sigma


def belongs(rows, count, patches, kind):
    return (quotient(iota((rows, count), 0), patches) == iota((rows, count), 1)).astype(kind)


def belongs_back(rows, count, patches, kind):
    return (quotient(iota((count, rows), 1), patches) == iota((count, rows), 0)).astype(kind)


def own_patch(rows, points, patches, patch_len):
    return quotient(iota((rows, points), 1), patch_len) == remainder(iota((rows, points), 0), patches)


def turn_half(values):
    half = values.shape[0] // 2
    return jnp.concatenate([-values[half:], values[:half]], axis=0)


def turn_half_back(values):
    half = values.shape[0] // 2
    return jnp.concatenate([values[half:], -values[:half]], axis=0)


def split_rows(place_ref, turned, other_ref, own_ref, first, units):
    core = place_ref[0]
    unit = turned.shape[0] // units
    for at in range(units // 2):
        mine = pl.multiple_of((2 * at + core) * unit, 16)
        theirs = pl.multiple_of((2 * at + 1 - core) * unit, 16)
        own_ref[at * unit : (at + 1) * unit, :] = turned[pl.ds(mine, unit), :].astype(jnp.float32)
        other_ref[first + at * unit : first + (at + 1) * unit, :] = turned[pl.ds(theirs, unit), :].astype(jnp.float32)


def put_tiles(ref, first, values):
    rows, width = values.shape
    for at in range(width // rows):
        ref[first + at * rows : first + (at + 1) * rows, :] = values[:, at * rows : (at + 1) * rows].astype(jnp.float32)


UNITS = 8
TOKEN = jax.ShapeDtypeStruct((8, 128), jnp.float32)


def expect(microseconds):
    return pl.CostEstimate(flops=int(microseconds * 1.15e9), bytes_accessed=0, transcendentals=0)


OWN = ("branch", "normed_two", "resid", "mixed", "normed_one", "hidden")


def stack_rows(*heights):
    places, at = {}, 0
    for name, height in heights:
        places[name] = at
        at += height
    places["end"] = at
    return places


def later_rows(width, horizon):
    half = width // 2
    return stack_rows(("normed_two", half), ("upper", width), ("resid", half), ("head", horizon))


def rest_rows(width):
    half = width // 2
    return stack_rows(
        ("mixed", half),
        ("middle", width),
        ("normed_one", half),
        ("hidden", half),
    )


def last_rows(width, patch_len, rows):
    half = width // 2
    return stack_rows(
        ("embed_tiles", width),
        ("embed", half),
        ("pre", half),
        ("tokens", 2 * patch_len),
        ("sums", 8 * width // rows),
    )


def front_kernel(
    heads,
    lengths_ref,
    place_ref,
    series_ref,
    flags_ref,
    cotangent_ref,
    gain_first_ref,
    gain_second_ref,
    cosine_ref,
    sine_ref,
    lift_hbm,
    mix_hbm,
    skip_hbm,
    joint_hbm,
    merge_hbm,
    grow_hbm,
    shrink_hbm,
    head_hbm,
    token_ref,
    predictions_ref,
    tokens_out,
    logsum_out,
    sigma_sum_out,
    center_sum_out,
    second_out,
    embedded_hbm,
    middle_hbm,
    turned_hbm,
    own_hbm,
    soon_hbm,
    later_hbm,
    rest_hbm,
    lift_ref,
    mix_ref,
    skip_ref,
    joint_ref,
    merge_ref,
    grow_ref,
    shrink_ref,
    head_ref,
    embedded_ref,
    middle_ref,
    joint_turned,
    turned_ref,
    mixed_turned,
    allowed_ref,
    resid_ref,
    upper_ref,
    back_ref,
    flip_ref,
    own,
    soon,
    later,
    rest,
    load_sem,
    store_sem,
):
    rows, width = embedded_ref.shape
    count, points = series_ref.shape
    patches = rows // count
    patch_len = points // patches
    head_dim = width // heads
    half_rows = width // 2
    wide = cotangent_ref.shape[1]
    del token_ref
    loads = [
        pltpu.make_async_copy(lift_hbm, lift_ref, load_sem.at[0]),
        pltpu.make_async_copy(skip_hbm, skip_ref, load_sem.at[1]),
        pltpu.make_async_copy(mix_hbm, mix_ref, load_sem.at[2]),
    ]
    for at in range(3):
        loads.append(
            pltpu.make_async_copy(joint_hbm.at[:, pl.ds(at * width, width)], joint_ref.at[at], load_sem.at[3 + at])
        )
    for at, (source, target) in enumerate(
        ((merge_hbm, merge_ref), (head_hbm, head_ref), (shrink_hbm, shrink_ref), (grow_hbm, grow_ref))
    ):
        loads.append(pltpu.make_async_copy(source, target, load_sem.at[6 + at]))
    for copy in loads:
        copy.start()
    stores = []

    def store(source, target, first=0, count=None):
        span = pl.ds(first, source.shape[0] - first if count is None else count)
        copy = pltpu.make_async_copy(source.at[span], target.at[span], store_sem.at[len(stores)])
        copy.start()
        stores.append(copy)

    def split(turned, name, pack, at):
        first = OWN.index(name) * half_rows
        split_rows(place_ref, turned, pack, own.at[pl.ds(first, half_rows)], at, UNITS)
        store(own, own_hbm, first, half_rows)

    places = later_rows(width, wide) | rest_rows(width)

    kept, starts, _, _, center, shifted, _, sigma = series_statistics(lengths_ref, series_ref, flags_ref, patch_len)
    scaled = (shifted / sigma * kept).astype(jnp.bfloat16)
    flag_values = flags_ref[...].astype(jnp.float32).astype(jnp.bfloat16)
    spread_out = belongs(rows, count, patches, jnp.bfloat16)
    inside = own_patch(rows, points, patches, patch_len)
    lane = iota((points, 2 * patch_len), 1)
    point = remainder(iota((points, 2 * patch_len), 0), patch_len)
    fold_left = (lane == point).astype(jnp.bfloat16)
    fold_right = (lane == point + patch_len).astype(jnp.bfloat16)
    left = jnp.where(inside, dot_plain(spread_out, scaled), 0.0).astype(jnp.bfloat16)
    right = jnp.where(inside, dot_plain(spread_out, flag_values), 0.0).astype(jnp.bfloat16)
    tokens = (dot_plain(left, fold_left) + dot_plain(right, fold_right)).astype(jnp.bfloat16)
    tokens_out[...] = tokens
    spread_exact = belongs(rows, count, patches, jnp.float32)
    sigma_rows = dot_exact(spread_exact, jnp.broadcast_to(sigma, (count, wide)))
    center_rows = dot_exact(spread_exact, jnp.broadcast_to(center, (count, wide)))
    starts_rows = dot_exact(spread_exact, jnp.broadcast_to(starts.astype(jnp.float32), (count, wide)))
    patch_row = remainder(iota((rows, wide), 0), patches).astype(jnp.float32)
    valid = (patch_row >= starts_rows - 0.5).astype(jnp.float32)
    block = allowed_ref.shape[1]
    key_at = remainder(iota((rows, block), 0), block)
    query_at = iota((rows, block), 1)
    key_pos, query_pos = remainder(key_at, patches), remainder(query_at, patches)
    allowed_ref[...] = (
        (quotient(key_at, patches) == quotient(query_at, patches))
        & (key_pos <= query_pos)
        & ((key_pos.astype(jnp.float32) >= starts_rows[:, :1] - 0.5) | (key_pos == query_pos))
    ).astype(jnp.float32)

    loads[0].wait()
    hidden_pre = dot_plain(tokens, lift_ref[...])
    hidden_act = (hidden_pre * logistic(hidden_pre)).astype(jnp.bfloat16)
    flip_ref[...] = hidden_act.T
    split(flip_ref, "hidden", rest, places["hidden"])
    store(rest, rest_hbm, places["hidden"], half_rows)
    loads[1].wait()
    loads[2].wait()
    embedded = dot_plain(hidden_act, mix_ref[...]) + dot_plain(tokens, skip_ref[...])
    embedded_ref[...] = embedded
    store(embedded_ref, embedded_hbm)
    scale_one = lax.rsqrt(jnp.mean(embedded * embedded, axis=1, keepdims=True) + epsilon)
    normed_one = (embedded * scale_one * gain_first_ref[...][None, :]).astype(jnp.bfloat16)
    for at in range(3):
        loads[3 + at].wait()
        tile = rows
        for part in range(width // tile):
            result = dot_plain(normed_one, joint_ref[at, :, part * tile : (part + 1) * tile])
            joint_turned[at * width + part * tile : at * width + (part + 1) * tile, :] = result.T
    flip_ref[...] = normed_one.T
    split(flip_ref, "normed_one", rest, places["normed_one"])
    store(rest, rest_hbm, places["normed_one"], half_rows)

    scale = head_dim ** (-0.5)
    cosine, sine = cosine_ref[...], sine_ref[...]

    def one_head(head, _):
        begin = pl.multiple_of(head * head_dim, 16)
        query = joint_turned[pl.ds(begin, head_dim), :]
        key = joint_turned[pl.ds(width + begin, head_dim), :]
        value = joint_turned[pl.ds(2 * width + begin, head_dim), :].astype(jnp.bfloat16)
        query = (query * cosine + turn_half(query) * sine).astype(jnp.bfloat16)
        key = (key * cosine + turn_half(key) * sine).astype(jnp.bfloat16)
        turned_ref[pl.ds(begin, head_dim), :] = query
        turned_ref[pl.ds(width + begin, head_dim), :] = key
        turned_ref[pl.ds(2 * width + begin, head_dim), :] = value
        mixed, sums = [], []
        for at in range(rows // block):
            span = slice(at * block, (at + 1) * block)
            scores = dot_over(key[:, span], query[:, span], 0, 0) * scale
            scores = jnp.where(allowed_ref[span, :] > 0.5, scores, masked_value)
            top = jnp.max(scores, axis=0, keepdims=True)
            raised = jnp.exp(scores - top)
            total = jnp.sum(raised, axis=0, keepdims=True)
            sums.append(top + jnp.log(total))
            probs = (raised / total).astype(jnp.bfloat16)
            mixed.append(dot_plain(value[:, span], probs))
        logsum_out[pl.ds(head, 1), :] = jnp.concatenate(sums, axis=1)
        mixed_turned[pl.ds(begin, head_dim), :] = jnp.concatenate(mixed, axis=1).astype(jnp.bfloat16)
        return 0

    lax.fori_loop(0, heads, one_head, 0, unroll=2)
    store(turned_ref, turned_hbm)
    split(mixed_turned, "mixed", rest, places["mixed"])
    store(rest, rest_hbm, places["mixed"], half_rows)
    mixed = mixed_turned[...].T
    loads[6].wait()
    resid_one = embedded_ref[...] + dot_plain(mixed, merge_ref[...])
    resid_ref[...] = resid_one
    scale_two = lax.rsqrt(jnp.mean(resid_one * resid_one, axis=1, keepdims=True) + epsilon)
    normed_two = (resid_one * scale_two * gain_second_ref[...][None, :]).astype(jnp.bfloat16)
    flip_ref[...] = normed_two.T
    split(flip_ref, "normed_two", later, places["normed_two"])
    store(later, later_hbm, places["normed_two"], half_rows)

    outer = cotangent_ref[...] * valid
    head_back = (outer * sigma_rows).astype(jnp.bfloat16)
    loads[7].wait()
    resid_back = dot_over(head_back, head_ref[...], 1, 1)
    back_ref[...] = resid_back
    branch_back = resid_back.astype(jnp.bfloat16)
    flip_ref[...] = branch_back.T
    split(flip_ref, "branch", soon, 0)

    loads[9].wait()
    upper_pre = dot_plain(normed_two, grow_ref[...])
    upper_ref[...] = upper_pre
    active = (upper_pre * logistic(upper_pre)).astype(jnp.bfloat16)
    put_tiles(soon, half_rows, active)
    store(soon, soon_hbm)
    loads[8].wait()
    upper_pre = upper_ref[...]
    gate = logistic(upper_pre)
    slope = gate * (1.0 + upper_pre * (1.0 - gate))
    upper_back = (dot_over(branch_back, shrink_ref[...], 1, 1) * slope).astype(jnp.bfloat16)
    put_tiles(later, places["upper"], upper_back)
    store(later, later_hbm, places["upper"], width)
    resid_low = (resid_ref[...] + dot_plain(active, shrink_ref[...])).astype(jnp.bfloat16)
    flip_ref[...] = resid_low.T
    split(flip_ref, "resid", later, places["resid"])
    store(later, later_hbm, places["resid"], half_rows)
    later[places["head"] : places["head"] + wide, :] = head_back.astype(jnp.float32).T
    store(later, later_hbm, places["head"], wide)

    normed_back = dot_over(upper_back, grow_ref[...], 1, 1)
    resid_one = resid_ref[...]
    second_out[...] = jnp.sum(normed_back * resid_one * scale_two, axis=0, keepdims=True)
    through = normed_back * gain_second_ref[...][None, :]
    inner = jnp.mean(through * resid_one, axis=1, keepdims=True)
    middle = back_ref[...] + scale_two * through - resid_one * (scale_two * scale_two * scale_two * inner)
    middle_ref[...] = middle
    store(middle_ref, middle_hbm)
    put_tiles(rest, places["middle"], middle.astype(jnp.bfloat16))
    store(rest, rest_hbm, places["middle"], width)

    head_out = dot_plain(resid_low, head_ref[...])
    predictions_ref[...] = valid * (head_out * sigma_rows + center_rows)
    gather = belongs_back(rows, count, patches, jnp.float32)
    sigma_sum_out[...] = dot_exact(gather, outer * head_out)
    center_sum_out[...] = dot_exact(gather, outer)
    for copy in stores:
        copy.wait()


def front(place, lengths, series, flags, cotangent, tables, weights, heads, cost):
    lift, mix, skip, gain_first, joint, merge, gain_second, grow, shrink, head = weights
    rows, horizon = cotangent.shape
    width = mix.shape[0]
    half = width // 2
    count = series.shape[0]
    f32, bf16 = jnp.float32, jnp.bfloat16
    vmem = pl.BlockSpec(memory_space=pltpu.VMEM)
    smem = pl.BlockSpec(memory_space=pltpu.SMEM)
    hbm = pl.BlockSpec(memory_space=pl.ANY)
    shape = jax.ShapeDtypeStruct
    packs = [
        (len(OWN) * half, rows),
        (half + width, rows),
        (later_rows(width, horizon)["end"], rows),
        (rest_rows(width)["end"], rows),
    ]
    outs = [
        TOKEN,
        shape((rows, horizon), f32),
        shape((rows, lift.shape[0]), bf16),
        shape((heads, rows), f32),
        shape((count, horizon), f32),
        shape((count, horizon), f32),
        shape((1, width), f32),
        shape((rows, width), f32),
        shape((rows, width), f32),
        shape((3 * width, rows), bf16),
    ] + [shape(pack, f32) for pack in packs]
    scratch = [
        pltpu.VMEM(lift.shape, bf16),
        pltpu.VMEM(mix.shape, bf16),
        pltpu.VMEM(skip.shape, bf16),
        pltpu.VMEM((3, width, width), bf16),
        pltpu.VMEM(merge.shape, bf16),
        pltpu.VMEM(grow.shape, bf16),
        pltpu.VMEM(shrink.shape, bf16),
        pltpu.VMEM(head.shape, bf16),
        pltpu.VMEM((rows, width), f32),
        pltpu.VMEM((rows, width), f32),
        pltpu.VMEM((3 * width, rows), f32),
        pltpu.VMEM((3 * width, rows), bf16),
        pltpu.VMEM((width, rows), bf16),
        pltpu.VMEM((rows, BLOCK), f32),
        pltpu.VMEM((rows, width), f32),
        pltpu.VMEM((rows, width), f32),
        pltpu.VMEM((rows, width), f32),
        pltpu.VMEM((width, rows), bf16),
    ] + [pltpu.VMEM(pack, f32) for pack in packs]
    scratch += [pltpu.SemaphoreType.DMA((10,)), pltpu.SemaphoreType.DMA((18,))]
    return pl.pallas_call(
        functools.partial(front_kernel, heads),
        out_shape=outs,
        in_specs=[smem, smem] + [vmem] * 7 + [hbm] * 8,
        out_specs=[hbm] + [vmem] * 6 + [hbm] * 7,
        scratch_shapes=scratch,
        compiler_params=pltpu.CompilerParams(vmem_limit_bytes=62 * 1024 * 1024),
        cost_estimate=expect(cost),
    )(
        lengths,
        place,
        series,
        flags,
        cotangent,
        gain_first,
        gain_second,
        *tables,
        lift,
        mix,
        skip,
        joint,
        merge,
        grow,
        shrink,
        head,
    )


def back_kernel(
    heads,
    lengths_ref,
    place_ref,
    series_ref,
    flags_ref,
    gain_first_ref,
    cosine_ref,
    sine_ref,
    tokens_ref,
    logsum_ref,
    sigma_sum_ref,
    center_sum_ref,
    second_ref,
    middle_ref,
    turned_ref,
    embedded_hbm,
    lift_hbm,
    mix_hbm,
    skip_hbm,
    joint_hbm,
    merge_hbm,
    token_in,
    token_ref,
    series_grad_ref,
    joint_hbm_out,
    last_hbm,
    own_hbm,
    lift_ref,
    mix_ref,
    skip_ref,
    joint_ref,
    merge_ref,
    embedded_ref,
    mixed_turned,
    joint_turned,
    first_ref,
    allowed_ref,
    flip_ref,
    joint_pack,
    last,
    own,
    load_sem,
    store_sem,
):
    rows, width = embedded_ref.shape
    count, points = series_ref.shape
    patches = rows // count
    patch_len = points // patches
    head_dim = width // heads
    half_rows = width // 2
    del token_in, token_ref
    loads = [
        pltpu.make_async_copy(source, target, load_sem.at[at])
        for at, (source, target) in enumerate(
            (
                (merge_hbm, merge_ref),
                (joint_hbm, joint_ref),
                (embedded_hbm, embedded_ref),
                (mix_hbm, mix_ref),
                (lift_hbm, lift_ref),
                (skip_hbm, skip_ref),
            )
        )
    ]
    for copy in loads:
        copy.start()
    stores = []

    def store(source, target, first=0, count=None):
        span = pl.ds(first, source.shape[0] - first if count is None else count)
        copy = pltpu.make_async_copy(source.at[span], target.at[span], store_sem.at[len(stores)])
        copy.start()
        stores.append(copy)

    places = last_rows(width, patch_len, rows)

    kept, starts, hot_kept, kept_count, center, shifted, spread, sigma = series_statistics(
        lengths_ref, series_ref, flags_ref, patch_len
    )
    block = allowed_ref.shape[1]
    spread_exact = belongs(rows, count, patches, jnp.float32)
    starts_rows = dot_exact(spread_exact, jnp.broadcast_to(starts.astype(jnp.float32), (count, block)))
    key_at = remainder(iota((rows, block), 0), block)
    query_at = iota((rows, block), 1)
    key_pos, query_pos = remainder(key_at, patches), remainder(query_at, patches)
    allowed_ref[...] = (
        (quotient(key_at, patches) == quotient(query_at, patches))
        & (key_pos <= query_pos)
        & ((key_pos.astype(jnp.float32) >= starts_rows - 0.5) | (key_pos == query_pos))
    ).astype(jnp.float32)
    scale = head_dim ** (-0.5)
    cosine, sine = cosine_ref[...], sine_ref[...]
    loads[0].wait()
    mixed_turned[...] = dot_over(merge_ref[...], middle_ref[...].astype(jnp.bfloat16), 1, 1).astype(jnp.bfloat16)

    def unrotate(gradient):
        return gradient * cosine + turn_half_back(gradient * sine)

    def one_head(head, _):
        begin = pl.multiple_of(head * head_dim, 16)
        query = turned_ref[pl.ds(begin, head_dim), :]
        key = turned_ref[pl.ds(width + begin, head_dim), :]
        value = turned_ref[pl.ds(2 * width + begin, head_dim), :]
        upstream = mixed_turned[pl.ds(begin, head_dim), :]
        logsum = logsum_ref[pl.ds(head, 1), :]
        query_parts, key_parts, value_parts = [], [], []
        for at in range(rows // block):
            span = slice(at * block, (at + 1) * block)
            query_in, key_in, value_in, up = query[:, span], key[:, span], value[:, span], upstream[:, span]
            scores = dot_over(key_in, query_in, 0, 0) * scale
            scores = jnp.where(allowed_ref[span, :] > 0.5, scores, masked_value)
            probs = jnp.exp(scores - logsum[:, span])
            value_parts.append(dot_over(up, probs.astype(jnp.bfloat16), 1, 1))
            probs_back = dot_over(value_in, up, 0, 0)
            inner = jnp.sum(probs * probs_back, axis=0, keepdims=True)
            scores_back = (probs * (probs_back - inner) * scale).astype(jnp.bfloat16)
            query_parts.append(dot_plain(key_in, scores_back))
            key_parts.append(dot_over(query_in, scores_back, 1, 1))
        for at, parts in enumerate((query_parts, key_parts, value_parts)):
            result = jnp.concatenate(parts, axis=1)
            if at < 2:
                result = unrotate(result)
            result = result.astype(jnp.bfloat16)
            joint_turned[pl.ds(at * width + begin, head_dim), :] = result
            joint_pack[pl.ds(at * width + begin, head_dim), :] = result.astype(jnp.float32)
        return 0

    lax.fori_loop(0, heads, one_head, 0, unroll=8)
    store(joint_pack, joint_hbm_out)
    loads[1].wait()
    tile = rows
    for part in range(width // tile):
        span = slice(part * tile, (part + 1) * tile)
        first_ref[:, span] = dot_plain(joint_ref[span, :], joint_turned[...]).T
    loads[2].wait()
    embedded = embedded_ref[...]
    first_back = first_ref[...]
    scale_one = lax.rsqrt(jnp.mean(embedded * embedded, axis=1, keepdims=True) + epsilon)
    first_sum = jnp.sum(first_back * embedded * scale_one, axis=0, keepdims=True)
    through = first_back * gain_first_ref[...][None, :]
    inner = jnp.mean(through * embedded, axis=1, keepdims=True)
    embed_low = (
        middle_ref[...] + scale_one * through - embedded * (scale_one * scale_one * scale_one * inner)
    ).astype(jnp.bfloat16)
    put_tiles(last, places["embed_tiles"], embed_low)
    flip_ref[...] = embed_low.T
    split_rows(place_ref, flip_ref, last, own.at[pl.ds(0, half_rows)], places["embed"], UNITS)
    store(last, last_hbm, places["embed_tiles"], width + half_rows)
    tokens = tokens_ref[...]
    loads[4].wait()
    hidden_pre = dot_plain(tokens, lift_ref[...])
    gate = logistic(hidden_pre)
    slope = gate * (1.0 + hidden_pre * (1.0 - gate))
    loads[3].wait()
    pre_back = (dot_over(embed_low, mix_ref[...], 1, 1) * slope).astype(jnp.bfloat16)
    flip_ref[...] = pre_back.T
    split_rows(place_ref, flip_ref, last, own.at[pl.ds(half_rows, half_rows)], places["pre"], UNITS)
    store(own, own_hbm)
    last[places["tokens"] : places["sums"], :] = tokens.astype(jnp.float32).T
    row = iota((8, width), 0)
    sums = jnp.where(row == 0, second_ref[...], jnp.where(row == 1, first_sum, 0.0))
    for at in range(width // rows):
        first = places["sums"] + 8 * at
        last[first : first + 8, :] = sums[:, at * rows : (at + 1) * rows]
    store(last, last_hbm, places["pre"])

    loads[5].wait()
    token_back = dot_over(pre_back, lift_ref[...], 1, 1) + dot_over(embed_low, skip_ref[...], 1, 1)
    lane = remainder(iota((2 * patch_len, points), 1), patch_len)
    unfold = (lane == iota((2 * patch_len, points), 0)).astype(jnp.float32)
    inside = own_patch(rows, points, patches, patch_len)
    spread_back_rows = jnp.where(inside, dot_exact(token_back, unfold), 0.0)
    scaled_back = dot_exact(belongs_back(rows, count, patches, jnp.float32), spread_back_rows)
    kept_back = scaled_back * kept
    point_back = kept_back / sigma
    sigma_back = jnp.sum(sigma_sum_ref[...], axis=1, keepdims=True)
    center_back = jnp.sum(center_sum_ref[...], axis=1, keepdims=True)
    center_total = center_back - jnp.sum(point_back, axis=1, keepdims=True)
    sigma_total = sigma_back - jnp.sum(kept_back * shifted, axis=1, keepdims=True) / (sigma * sigma)
    spread_grad = jnp.where(spread > 1.0, sigma_total * 0.5 / sigma, 0.0)
    offset_sum = jnp.sum(hot_kept * 2.0 * shifted, axis=1, keepdims=True)
    center_all = center_total - spread_grad * offset_sum / kept_count
    series_grad_ref[...] = point_back + hot_kept * (center_all + 2.0 * shifted * spread_grad) / kept_count
    for copy in stores:
        copy.wait()


def back(token, place, lengths, series, flags, tables, weights, kept_values, heads, cost):
    lift, mix, skip, gain_first, joint, merge = weights
    tokens, logsum, sigma_sum, center_sum, second_sum, embedded, middle, turned = kept_values
    rows, width = embedded.shape
    half = width // 2
    f32, bf16 = jnp.float32, jnp.bfloat16
    vmem = pl.BlockSpec(memory_space=pltpu.VMEM)
    smem = pl.BlockSpec(memory_space=pltpu.SMEM)
    hbm = pl.BlockSpec(memory_space=pl.ANY)
    shape = jax.ShapeDtypeStruct
    packs = [(3 * width, rows), (last_rows(width, lift.shape[0] // 2, rows)["end"], rows), (2 * half, rows)]
    scratch = [
        pltpu.VMEM(lift.shape, bf16),
        pltpu.VMEM(mix.shape, bf16),
        pltpu.VMEM(skip.shape, bf16),
        pltpu.VMEM(joint.shape, bf16),
        pltpu.VMEM(merge.shape, bf16),
        pltpu.VMEM((rows, width), f32),
        pltpu.VMEM((width, rows), bf16),
        pltpu.VMEM((3 * width, rows), bf16),
        pltpu.VMEM((rows, width), f32),
        pltpu.VMEM((rows, BLOCK), f32),
        pltpu.VMEM((width, rows), bf16),
    ] + [pltpu.VMEM(pack, f32) for pack in packs]
    scratch += [pltpu.SemaphoreType.DMA((6,)), pltpu.SemaphoreType.DMA((4,))]
    return pl.pallas_call(
        functools.partial(back_kernel, heads),
        out_shape=[TOKEN, shape(series.shape, f32)] + [shape(pack, f32) for pack in packs],
        in_specs=[smem, smem] + [vmem] * 12 + [hbm] * 7,
        out_specs=[hbm, vmem] + [hbm] * 3,
        scratch_shapes=scratch,
        compiler_params=pltpu.CompilerParams(vmem_limit_bytes=62 * 1024 * 1024),
        cost_estimate=expect(cost),
    )(
        lengths,
        place,
        series,
        flags,
        gain_first,
        *tables,
        tokens,
        logsum,
        sigma_sum,
        center_sum,
        second_sum,
        middle,
        turned,
        embedded,
        lift,
        mix,
        skip,
        joint,
        merge,
        token,
    )


def gradient_kernel(place_ref, *refs, pieces, arrays, unit):
    sources = refs[:arrays]
    token_ref, outputs = refs[arrays + 1], refs[arrays + 2 : arrays + 2 + 2 * len(pieces)]
    result_ref, left_raw, left_ref, right_raw, load_sem, store_sem = refs[arrays + 2 + 2 * len(pieces) :]
    del token_ref
    total = 4 * unit
    rows = left_raw.shape[2]
    loads, stores, lefts, rights = [], [], {}, []

    def load(source, first, target):
        copy = pltpu.make_async_copy(sources[source].at[pl.ds(first, target.shape[0])], target, load_sem.at[len(loads)])
        copy.start()
        loads.append(copy)
        return copy

    place = 0
    for _, terms in pieces:
        for own, own_row, other, other_row, near, far, row, kind, width in terms:
            key = (own, own_row, other, other_row)
            if kind != "sum" and key not in lefts:
                at = len(lefts)
                copies = [load(own, own_row, left_raw.at[2 * at]), load(other, other_row, left_raw.at[2 * at + 1])]
                lefts[key] = (at, copies)
            tiles = []
            for tile in range(0, width, rows):
                size = min(rows, width - tile)
                spots = [right_raw.at[pl.ds(place + side * size, size)] for side in (0, 1)]
                place += 2 * size
                tiles.append((size, spots, [load(side, row + tile, spot) for side, spot in zip((near, far), spots)]))
            rights.append(tiles)
    waited = set()
    number = 0
    tile_at = 0
    for order, (axis, terms) in enumerate(pieces):
        core = place_ref[0]
        stride, across = 1 + core, 2 - core
        if axis == "z":
            height, mine = unit // 2, place_ref[3] & 1
            groups = [stride * a + across * b for b in (0, 1) for a in (0, 1)]
            starts = [group * unit + half * height for half in (1 - mine, mine) for group in groups]
        else:
            height, mine = unit, place_ref[1]
            starts = [(stride * side + across * other) * unit for side in (1 - mine, mine) for other in (0, 1)]
        out_tile = 0

        def store(count):
            for half in (0, 1):
                copy = pltpu.make_async_copy(
                    result_ref.at[pl.ds(tile_at, count), pl.ds(half * total // 2, total // 2)],
                    outputs[2 * order + half].at[pl.ds(out_tile, count)],
                    store_sem.at[len(stores)],
                )
                copy.start()
                stores.append(copy)

        held = None
        for own, own_row, other, other_row, _, _, _, kind, width in terms:
            tiles = rights[number]
            number += 1
            if kind == "sum":
                for _, spots, copies in tiles:
                    for copy in copies:
                        copy.wait()
                both = tiles[0][1][0][...] + tiles[0][1][1][...]
                lanes = jnp.concatenate([both[part : part + 8, :] for part in range(0, width, 8)], axis=1)
                tall = jnp.concatenate([lanes, jnp.zeros((BLOCK - 8, lanes.shape[1]), jnp.float32)], axis=0).T
                unit_rows = tall.reshape(UNITS // 2, 2, unit, BLOCK)
                spare = left_raw.at[left_raw.shape[0] - 1]
                spare[:, :BLOCK] = jnp.where(place_ref[0] == 0, unit_rows[:, 0], unit_rows[:, 1]).reshape(total, BLOCK)
                for slot, first in enumerate(starts):
                    result_ref[tile_at, slot * height : (slot + 1) * height, :] = spare[
                        pl.ds(pl.multiple_of(first, 16), height), :BLOCK
                    ]
                store(1)
                tile_at += 1
                out_tile += 1
                continue
            at, copies = lefts[(own, own_row, other, other_row)]
            if at not in waited:
                waited.add(at)
                for copy in copies:
                    copy.wait()
            if held != at:
                held = at
                for slot, first in enumerate(starts):
                    first = pl.multiple_of(first, 16)
                    span = slice(slot * height, (slot + 1) * height)
                    for side in (0, 1):
                        left_ref[order % 2, span, side * rows : (side + 1) * rows] = left_raw[
                            2 * at + side, pl.ds(first, height), :
                        ].astype(jnp.bfloat16)
            left = left_ref[order % 2]
            for size, spots, copies in tiles:
                for copy in copies:
                    copy.wait()
                near, far = (spot[...].astype(jnp.bfloat16) for spot in spots)
                if kind == "tiles":
                    result = dot_plain(left, jnp.concatenate([near, far], axis=0))
                else:
                    right = jnp.concatenate([near, far], axis=1)
                    if kind != "turned":
                        blank = jnp.zeros_like(right)
                        right = jnp.concatenate((right, blank) if kind == "low" else (blank, right), axis=0)
                    result = dot_over(left, right, 1, 1)
                count = result.shape[1] // BLOCK
                for part in range(count):
                    piece = result[:, part * BLOCK : (part + 1) * BLOCK]
                    if kind == "high":
                        result_ref[tile_at + part] += piece
                    else:
                        result_ref[tile_at + part] = piece
                if kind != "low":
                    store(count)
                    tile_at += count
                    out_tile += count
    for copy in stores:
        copy.wait()


def tiles_of(terms):
    widths = {"low": 0, "high": BLOCK, "sum": BLOCK}
    return sum(widths.get(term[7], term[8]) for term in terms) // BLOCK


def weight_gradient(token, place, arrays, pieces, unit, cost):
    rows = arrays[0].shape[1]
    total = 4 * unit
    hbm = pl.BlockSpec(memory_space=pl.ANY)
    vmem = pl.BlockSpec(memory_space=pltpu.VMEM)
    counts = [tiles_of(terms) for _, terms in pieces]
    every = [term for _, terms in pieces for term in terms]
    lefts = len({term[:4] for term in every if term[7] != "sum"})
    copies = 2 * lefts + sum(2 * (-(-term[8] // rows)) for term in every)
    shapes = [jax.ShapeDtypeStruct((count, total // 2, BLOCK), jnp.float32) for count in counts for _ in (0, 1)]
    results = pl.pallas_call(
        functools.partial(gradient_kernel, pieces=pieces, arrays=len(arrays), unit=unit),
        in_specs=[pl.BlockSpec(memory_space=pltpu.SMEM)] + [hbm] * (len(arrays) + 1),
        out_specs=[hbm] * (1 + len(shapes)),
        scratch_shapes=[
            pltpu.VMEM((sum(counts), total, BLOCK), jnp.float32),
            pltpu.VMEM((2 * lefts + 1, total, rows), jnp.float32),
            pltpu.VMEM((2, total, 2 * rows), jnp.bfloat16),
            pltpu.VMEM((2 * sum(term[8] for term in every), rows), jnp.float32),
            pltpu.SemaphoreType.DMA((copies,)),
            pltpu.SemaphoreType.DMA((copies,)),
        ],
        out_shape=[TOKEN] + shapes,
        compiler_params=pltpu.CompilerParams(vmem_limit_bytes=VMEM_GRADIENT * 1024 * 1024),
        cost_estimate=expect(cost),
    )(place, *arrays, token)
    return results[0], [results[1 + 2 * at : 3 + 2 * at] for at in range(len(pieces))]


def combine_kernel(place_ref, *refs, inputs, parts, which, last, spread, passed):
    total = sum(inputs)
    sources = refs[:total]
    token_ref = refs[total + 1]
    results = refs[total + 2 : total + 2 + (len(inputs) if last else 1 if spread else parts)]
    scratch = refs[total + 2 + len(results) :]
    raws, sums, load_sem, store_sem = scratch[:total], scratch[total], scratch[total + 1], scratch[total + 2]
    del token_ref
    mine = place_ref[which] & (parts - 1)
    chosen = [step if spread else mine ^ ((step + 1) & (parts - 1)) for step in range(parts)]
    loads, stores = {}, []
    for step in range(parts):
        for at in range(total):
            copy = pltpu.make_async_copy(
                sources[at].at[:, :, chosen[step]], raws[at].at[step], load_sem.at[step * total + at]
            )
            copy.start()
            loads[step, at] = copy
    for step in range(parts):
        first = 0
        begin = 0
        for group, count in enumerate(inputs):
            for at in range(first, first + count):
                loads[step, at].wait()
            value = raws[first][step]
            for at in range(first + 1, first + count):
                if passed:
                    outside = jnp.logical_or(place_ref[3] == 0, place_ref[3] == 3)
                    value = jnp.where(outside, value, raws[at][step])
                else:
                    value = value + raws[at][step]
            tiles = value.shape[0]
            if last:
                fold = tiles // (results[group].shape[1] // BLOCK)
                tiles //= fold
                for tile in range(tiles):
                    piece = value[tile, 0]
                    for part in range(1, fold):
                        piece = piece + value[part * tiles + tile, 0]
                    results[group][:, tile * BLOCK : (tile + 1) * BLOCK] = piece
            else:
                sums[step, begin : begin + tiles] = value
                copy = pltpu.make_async_copy(
                    sums.at[step, pl.ds(begin, tiles)],
                    results[0].at[step, pl.ds(begin, tiles)] if spread else results[step].at[pl.ds(begin, tiles)],
                    store_sem.at[len(stores)],
                )
                copy.start()
                stores.append(copy)
            begin += tiles
            first += count
    for copy in stores:
        copy.wait()


def combine(token, place, groups, before, parts, which, cost, last=False, spread=False, fold=1, passed=False):
    rows = groups[0][0].shape[1]
    after = rows // (before * parts)
    flat = [array.reshape(array.shape[0], before, parts, after, BLOCK) for group in groups for array in group]
    tiles = [group[0].shape[0] for group in groups]
    hbm = pl.BlockSpec(memory_space=pl.ANY)
    vmem = pl.BlockSpec(memory_space=pltpu.VMEM)
    shape = jax.ShapeDtypeStruct
    if last:
        shapes = [shape((rows, count // fold * BLOCK), jnp.float32) for count in tiles]
    elif spread:
        shapes = [shape((parts, sum(tiles), before, after, BLOCK), jnp.float32)]
    else:
        shapes = [shape((sum(tiles), before, after, BLOCK), jnp.float32)] * parts
    results = pl.pallas_call(
        functools.partial(
            combine_kernel, inputs=tuple(len(group) for group in groups), parts=parts, which=which, last=last, spread=spread, passed=passed
        ),
        in_specs=[pl.BlockSpec(memory_space=pltpu.SMEM)] + [hbm] * (len(flat) + 1),
        out_specs=[hbm] + [vmem if last else hbm] * len(shapes),
        scratch_shapes=[pltpu.VMEM((parts, array.shape[0], before, after, BLOCK), jnp.float32) for array in flat]
        + [
            pltpu.VMEM((1,) * 5 if last else (parts, sum(tiles), before, after, BLOCK), jnp.float32),
            pltpu.SemaphoreType.DMA((parts * len(flat),)),
            pltpu.SemaphoreType.DMA((parts * len(groups),)),
        ],
        out_shape=[TOKEN] + shapes,
        compiler_params=pltpu.CompilerParams(vmem_limit_bytes=VMEM_COMBINE * 1024 * 1024),
        cost_estimate=expect(cost),
    )(place, *flat, token)
    if last or spread:
        return results[0], results[1:]
    return results[0], [result.reshape(sum(tiles), before * after, BLOCK) for result in results[1:]]


class Layout:
    def __init__(self, mesh_shape):
        self.wide = mesh_shape["wide"]
        self.narrow = mesh_shape["narrow"]
        self.total = self.wide * self.narrow
        self.paired = self.wide == 8 and self.narrow == 4

    def flip(self, bit):
        return [(i, i ^ bit) for i in range(self.total)]

    def middle(self):
        swapped = {1: 2, 2: 1}
        return [(i, (i & ~3) | swapped[i & 3] if i & 3 in swapped else i ^ 4) for i in range(self.total)]

    def across(self, first):
        return [(i, i ^ (8 if (i & 4 == 0) == first else 16)) for i in range(self.total)]

    def position(self):
        wide = lax.axis_index("wide")
        core, x, y = wide % 2, wide // 2 % 2, wide // 4 % 2
        places = (core, jnp.where(core == 0, x, y), jnp.where(core == 0, y, x), lax.axis_index("narrow"))
        if not self.paired:
            places = tuple(jnp.zeros_like(place) for place in places)
        return jnp.stack(places).astype(jnp.int32)


class Bundle:
    def __init__(self, names, plan, axes, groups, fold=1, passed=False):
        self.names, self.plan, self.axes, self.groups = names, plan, axes, groups
        self.fold, self.passed = fold, passed


def steps_of(order):
    plan = []
    for axis in order:
        plan += ["half", "middle", "part"] if axis == "z" else [axis]
    return plan


def move(layout, array, step):
    if step == "middle":
        pairs = layout.middle()
    else:
        pairs = layout.across(step == "a") if step in ("a", "b") else layout.flip(1)
    return lax.ppermute(array, AXES, pairs)


def start_bundles(layout, token, place, arrays, names, terms, unit, cost):
    plans = [steps_of(ORDERS[name]) for name in names]
    token, results = weight_gradient(
        token, place, arrays, tuple((ORDERS[name][0], terms[name]) for name in names), unit, cost
    )
    bundles = {}
    for name, plan, (send, keep) in zip(names, plans, results):
        step = plan.pop(0)
        axes = [axis for axis in ("b", "a", "half", "part") if axis != step]
        bundles[name] = Bundle([name], plan, axes, [[keep, move(layout, send, step)]])
    return token, bundles


def advance(layout, token, place, bundles, rows, cost, finished):
    plan, axes = bundles[0].plan, bundles[0].axes
    groups = [group for bundle in bundles for group in bundle.groups]
    names = [name for bundle in bundles for name in bundle.names]
    sizes = [group[0].shape[0] for group in groups]
    if not plan:
        token, results = combine(token, place, groups, 1, 1, 0, cost, last=True, fold=bundles[0].fold)
        wide = results[0] if len(results) == 1 else jnp.concatenate(results, axis=1)
        finished.append((names, wide))
        return token, None
    step, plan = plan[0], plan[1:]
    if step == "middle":
        token, (whole,) = combine(token, place, groups, 1, 1, 0, cost)
        return token, Bundle(names, plan, axes, [[whole, move(layout, whole, step)]], passed=True)
    if step == "Y":
        token, (whole,) = combine(token, place, groups, 1, 4, 0, cost, spread=True)
        got = lax.all_to_all(whole, "narrow", 0, 0, tiled=True)
        return token, Bundle(names, plan, [], [[got.reshape(4 * sum(sizes), rows, BLOCK)]], 4)
    at = axes.index(step)
    which = {"a": 1, "b": 2}.get(step, 3)
    token, (send, keep) = combine(token, place, groups, 2**at, 2, which, cost, passed=bundles[0].passed)
    return token, Bundle(names, plan, [axis for axis in axes if axis != step], [[keep, move(layout, send, step)]])


def whole_rows(own, other):
    unit = own.shape[0] // (UNITS // 2)
    pair = jnp.stack([own.reshape(-1, unit, own.shape[1]), other.reshape(-1, unit, own.shape[1])], axis=1)
    return pair.reshape(2 * own.shape[0], own.shape[1])


def whole_tiles(tiles, rows):
    return jnp.concatenate([tiles[at : at + rows] for at in range(0, tiles.shape[0], rows)], axis=1)


def per_device(
    layout,
    series,
    flags,
    lengths,
    lift_weight,
    mix_weight,
    skip_weight,
    gain_first,
    joint_weight,
    merge_weight,
    gain_second,
    grow_weight,
    shrink_weight,
    head_weight,
    cotangent,
):
    count = series.shape[0]
    patches, horizon = cotangent.shape[1:]
    width = mix_weight.shape[0]
    hidden = shrink_weight.shape[0]
    rows = count * patches
    half = width // 2
    tables = rotary_tables(patches, width // HEADS, count)
    place = layout.position()
    weights = (
        lift_weight,
        mix_weight,
        skip_weight,
        gain_first,
        joint_weight,
        merge_weight,
        gain_second,
        grow_weight,
        shrink_weight,
        head_weight,
    )
    (
        token,
        predictions,
        tokens,
        logsum,
        sigma_sum,
        center_sum,
        second_sum,
        embedded,
        middle,
        turned,
        own,
        soon,
        later,
        rest,
    ) = front(place, lengths, series, flags, cotangent.reshape(rows, horizon), tables, weights, HEADS, PROGRAM[0][2])
    across = lift_weight.shape[0]
    joint_width = joint_weight.shape[1]

    def run_back(token, cost):
        return back(
            token,
            place,
            lengths,
            series,
            flags,
            tables,
            (lift_weight, mix_weight, skip_weight, gain_first, joint_weight, merge_weight),
            (tokens, logsum, sigma_sum, center_sum, second_sum, embedded, middle, turned),
            HEADS,
            cost,
        )

    at_own = {name: place * half for place, name in enumerate(OWN)}
    at_later = later_rows(width, horizon)
    at_rest = rest_rows(width)
    at_last = last_rows(width, across // 2, rows)
    if layout.paired:
        swap = lambda array: lax.ppermute(array, AXES, layout.flip(4))
        unit = width // UNITS
        soon_got, later_got, rest_got = swap(soon), swap(later), swap(rest)
        terms = {
            "A": ((0, at_own["branch"], 2, 0, 1, 2, half, "tiles", hidden),),
            "B": (
                (0, at_own["normed_two"], 4, at_later["normed_two"], 3, 4, at_later["upper"], "tiles", hidden),
                (0, at_own["resid"], 4, at_later["resid"], 3, 4, at_later["head"], "turned", horizon),
            ),
            "C": ((0, at_own["mixed"], 6, at_rest["mixed"], 5, 6, at_rest["middle"], "tiles", width),),
            "E": (
                (0, at_own["hidden"], 6, at_rest["hidden"], 9, 10, at_last["embed_tiles"], "tiles", width),
                (11, half, 10, at_last["pre"], 9, 10, at_last["tokens"], "low", across),
                (11, 0, 10, at_last["embed"], 9, 10, at_last["tokens"], "high", across),
                (0, 0, 0, 0, 9, 10, at_last["sums"], "sum", 8 * width // rows),
            ),
        }
        joint_names = [name for name in ORDERS if name.startswith("D")]
        first = 0
        for name in joint_names:
            span = JOINT_TILES[name] * BLOCK
            terms[name] = ((0, at_own["normed_one"], 6, at_rest["normed_one"], 7, 8, first, "turned", span),)
            first += span
        arrays = [own, soon, soon_got, later, later_got, rest, rest_got]
        bundles, finished = {}, []
        for kind, names, cost in PROGRAM[1:]:
            if kind == "K":
                token, series_grad, joint, last, last_own = run_back(token, cost)
                arrays += [joint, swap(joint), last, swap(last), last_own]
            elif kind == "G":
                used = sorted({index for name in names for term in terms[name] for index in (term[0], *term[2:3], *term[4:6])})
                local = {
                    name: tuple(
                        (used.index(t[0]), t[1], used.index(t[2]), t[3], used.index(t[4]), used.index(t[5]), *t[6:])
                        for t in terms[name]
                    )
                    for name in names
                }
                token, fresh = start_bundles(
                    layout, token, place, [arrays[index] for index in used], names, local, unit, cost
                )
                bundles.update(fresh)
            else:
                token, joined = advance(
                    layout, token, place, [bundles.pop(name) for name in names], unit // 4, cost, finished
                )
                bundles["".join(names)] = joined
        columns = {}
        for names, wide in finished:
            begin = 0
            for name in names:
                span = tiles_of(terms[name]) * BLOCK
                columns[name] = wide[:, begin : begin + span]
                begin += span
        shrink_rows, merge_grad = columns["A"], columns["C"]
        grow_grad, head_grad = columns["B"][:, :hidden], columns["B"][:, hidden:]
        joint_grad = jnp.concatenate([columns[name] for name in joint_names], axis=1)
        mix_small = columns["E"]
        mix_grad = mix_small[:, :width]
        lift_rows = mix_small[:, width : width + across]
        skip_rows = mix_small[:, width + across : width + 2 * across]
        second_grad = mix_small[:, width + 2 * across]
        first_grad = mix_small[:, width + 2 * across + 1]
    else:
        _, series_grad, joint, last, last_own = run_back(token, 1.0)
        scatter = lambda left, right: lax.psum_scatter(
            dot_plain(left.astype(jnp.bfloat16), right.astype(jnp.bfloat16)), AXES, scatter_dimension=0, tiled=True
        )
        mine = lambda name: own[at_own[name] : at_own[name] + half]
        theirs = lambda name: (
            later[at_later[name] : at_later[name] + half]
            if name in at_later
            else rest[at_rest[name] : at_rest[name] + half]
        )
        tiles = lambda pack, first: whole_tiles(pack[first : first + width], rows)
        shrink_rows = scatter(whole_rows(mine("branch"), soon[:half]), tiles(soon, half))
        grow_grad = scatter(whole_rows(mine("normed_two"), theirs("normed_two")), tiles(later, at_later["upper"]))
        head_grad = scatter(
            whole_rows(mine("resid"), theirs("resid")), later[at_later["head"] : at_later["head"] + horizon].T
        )
        merge_grad = scatter(whole_rows(mine("mixed"), theirs("mixed")), tiles(rest, at_rest["middle"]))
        joint_grad = scatter(whole_rows(mine("normed_one"), theirs("normed_one")), joint.T)
        mix_grad = scatter(whole_rows(mine("hidden"), theirs("hidden")), tiles(last, at_last["embed_tiles"]))
        lift_rows = scatter(whole_rows(last_own[half:], last[at_last["pre"] : at_last["pre"] + half]), tokens)
        skip_rows = scatter(whole_rows(last_own[:half], last[at_last["embed"] : at_last["embed"] + half]), tokens)
        sums = whole_tiles(last[at_last["sums"] : at_last["end"]].reshape(-1, rows), 8)
        sums = lax.psum_scatter(sums[:2].T, AXES, scatter_dimension=0, tiled=True)
        second_grad, first_grad = sums[:, 0], sums[:, 1]
    return (
        predictions.reshape(count, patches, horizon),
        series_grad,
        lift_rows.T,
        mix_grad,
        skip_rows.T,
        first_grad,
        joint_grad,
        merge_grad,
        second_grad,
        grow_grad,
        shrink_rows.T,
        head_grad,
    )


def solution(mesh):
    both = P(AXES)
    in_specs = (both, both, both) + (P(),) * 10 + (both,)
    out_specs = (
        P(AXES, None, None),
        P(AXES, None),
        P(None, AXES),
        P(AXES, None),
        P(None, AXES),
        P(AXES),
        P(AXES, None),
        P(AXES, None),
        P(AXES),
        P(AXES, None),
        P(None, AXES),
        P(AXES, None),
    )
    return jax.shard_map(
        functools.partial(per_device, Layout(mesh.shape)),
        mesh=mesh,
        in_specs=in_specs,
        out_specs=out_specs,
        check_vma=False,
    )
```

```python
import functools

import jax
import jax.numpy as jnp
import numpy as np
from jax import lax
from jax.experimental import pallas as pl
from jax.experimental.pallas import tpu as pltpu
from jax.sharding import PartitionSpec as P

HEADS = 16
BLOCK = 128

epsilon = 1e-06
masked_value = -1000000000.0
AXES = ("wide", "narrow")


def rotary_tables(patches, head_dim, count):
    exponent = np.arange(head_dim // 2, dtype=np.float32) * np.float32(2.0 / head_dim)
    frequency = np.float32(10000.0) ** (-exponent)
    angles = frequency[:, None] * np.arange(patches, dtype=np.float32)[None, :]
    angles = np.tile(np.concatenate([angles, angles], axis=0), (1, count))
    return jnp.asarray(np.cos(angles)), jnp.asarray(np.sin(angles))


VMEM_GRADIENT = 60
VMEM_COMBINE = 24
ORDERS = {"A": "abY", "B": "zab", "C": "azb", "E": "abz", "D1": "abz", "D2": "azb"}
JOINT_TILES = {"D1": 15, "D2": 15}
PROGRAM = (
    ("F", (), 5),
    ("G", ("A", ), 25),
    ("G", ("B", ), 18),
    ("G", ("C", ), 2),
    ("K", (), 5),
    ("+", ("A", ), 40),
    ("+", ("C", ), 0.3),
    ("G", ("D2", ), 1),
    ("+", ("B", ), 3),
    ("+", ("A", ), 18),
    ("G", ("D1", ), 1),
    ("G", ("E", ), 3),
    ("+", ("D2", ), 12),
    ("+", ("B", ), 8),
    ("+", ("C", ), 0),
    ("+", ("A", ), 2),
    ("+", ("D1", ), 8),
    ("+", ("D2", ), 1),
    ("+", ("E", ), 18),
    ("+", ("C", ), 3),
    ("+", ("B", ), 0),
    ("+", ("D1", ), 1),
    ("+", ("C", ), 1),
    ("+", ("E", ), 1),
    ("+", ("B", ), 2),
    ("+", ("D1", ), 3),
    ("+", ("D2", ), 0),
    ("+", ("B", ), 0),
    ("+", ("E", ), 2),
    ("+", ("C", ), 1),
    ("+", ("D1", ), 0),
    ("+", ("D2", ), 2),
    ("+", ("E", ), 2),
    ("+", ("D1", ), 1),
    ("+", ("D2", ), 2),
    ("+", ("E", ), 3),
)


def dot_plain(left_side, right_side):
    return jnp.dot(left_side, right_side, preferred_element_type=jnp.float32)


def dot_over(left_side, right_side, left_axis, right_axis):
    return lax.dot_general(
        left_side,
        right_side,
        (((left_axis,), (right_axis,)), ((), ())),
        preferred_element_type=jnp.float32,
    )


def dot_exact(left_side, right_side):
    return jnp.dot(
        left_side, right_side, preferred_element_type=jnp.float32, precision=lax.Precision.HIGHEST
    )


def logistic(values):
    return 1.0 / (1.0 + jnp.exp(-values))


def quotient(values, by):
    return lax.shift_right_logical(values, jnp.int32(by.bit_length() - 1))


def remainder(values, by):
    return values & (by - 1)


def iota(shape, axis):
    return lax.broadcasted_iota(jnp.int32, shape, axis)


def series_statistics(lengths_ref, series_ref, flags_ref, patch_len):
    count, points = series_ref.shape
    patches = points // patch_len
    values = series_ref[...]
    kept = 1.0 - flags_ref[...].astype(jnp.float32)
    starts = jnp.zeros((count, 1), jnp.int32)
    row = iota((count, 1), 0)
    for at in range(count):
        starts = jnp.where(row == at, patches - lengths_ref[at], starts)
    hot = (quotient(iota((count, points), 1), patch_len) == starts).astype(jnp.float32)
    hot_kept = hot * kept
    kept_count = jnp.maximum(jnp.sum(hot_kept, axis=1, keepdims=True), 1.0)
    center = jnp.sum(hot_kept * values, axis=1, keepdims=True) / kept_count
    shifted = values - center
    spread = jnp.sum(hot_kept * shifted * shifted, axis=1, keepdims=True) / kept_count
    sigma = jnp.sqrt(jnp.maximum(spread, 1.0))
    return kept, starts, hot_kept, kept_count, center, shifted, spread, sigma


def belongs(rows, count, patches, kind):
    return (quotient(iota((rows, count), 0), patches) == iota((rows, count), 1)).astype(kind)


def belongs_back(rows, count, patches, kind):
    return (quotient(iota((count, rows), 1), patches) == iota((count, rows), 0)).astype(kind)


def own_patch(rows, points, patches, patch_len):
    return quotient(iota((rows, points), 1), patch_len) == remainder(iota((rows, points), 0), patches)


def turn_half(values):
    half = values.shape[0] // 2
    return jnp.concatenate([-values[half:], values[:half]], axis=0)


def turn_half_back(values):
    half = values.shape[0] // 2
    return jnp.concatenate([values[half:], -values[:half]], axis=0)


def split_rows(place_ref, turned, other_ref, own_ref, first, units):
    core = place_ref[0]
    unit = turned.shape[0] // units
    for at in range(units // 2):
        mine = pl.multiple_of((2 * at + core) * unit, 16)
        theirs = pl.multiple_of((2 * at + 1 - core) * unit, 16)
        own_ref[at * unit : (at + 1) * unit, :] = turned[pl.ds(mine, unit), :].astype(jnp.float32)
        other_ref[first + at * unit : first + (at + 1) * unit, :] = turned[pl.ds(theirs, unit), :].astype(jnp.float32)


def put_tiles(ref, first, values):
    rows, width = values.shape
    for at in range(width // rows):
        ref[first + at * rows : first + (at + 1) * rows, :] = values[:, at * rows : (at + 1) * rows].astype(jnp.float32)


UNITS = 8
TOKEN = jax.ShapeDtypeStruct((8, 128), jnp.float32)


def expect(microseconds):
    return pl.CostEstimate(flops=int(microseconds * 1.15e9), bytes_accessed=0, transcendentals=0)


OWN = ("branch", "normed_two", "resid", "mixed", "normed_one", "hidden")


def stack_rows(*heights):
    places, at = {}, 0
    for name, height in heights:
        places[name] = at
        at += height
    places["end"] = at
    return places


def later_rows(width, horizon):
    half = width // 2
    return stack_rows(("normed_two", half), ("upper", width), ("resid", half), ("head", horizon))


def rest_rows(width):
    half = width // 2
    return stack_rows(
        ("mixed", half),
        ("middle", width),
        ("normed_one", half),
        ("hidden", half),
    )


def last_rows(width, patch_len, rows):
    half = width // 2
    return stack_rows(
        ("embed_tiles", width),
        ("embed", half),
        ("pre", half),
        ("tokens", 2 * patch_len),
        ("sums", 8 * width // rows),
    )


def front_kernel(
    heads,
    lengths_ref,
    place_ref,
    series_ref,
    flags_ref,
    cotangent_ref,
    gain_first_ref,
    gain_second_ref,
    cosine_ref,
    sine_ref,
    lift_hbm,
    mix_hbm,
    skip_hbm,
    joint_hbm,
    merge_hbm,
    grow_hbm,
    shrink_hbm,
    head_hbm,
    token_ref,
    predictions_ref,
    tokens_out,
    logsum_out,
    sigma_sum_out,
    center_sum_out,
    second_out,
    embedded_hbm,
    middle_hbm,
    turned_hbm,
    own_hbm,
    soon_hbm,
    later_hbm,
    rest_hbm,
    lift_ref,
    mix_ref,
    skip_ref,
    joint_ref,
    merge_ref,
    grow_ref,
    shrink_ref,
    head_ref,
    embedded_ref,
    middle_ref,
    joint_turned,
    turned_ref,
    mixed_turned,
    allowed_ref,
    resid_ref,
    upper_ref,
    back_ref,
    flip_ref,
    own,
    soon,
    later,
    rest,
    load_sem,
    store_sem,
):
    rows, width = embedded_ref.shape
    count, points = series_ref.shape
    patches = rows // count
    patch_len = points // patches
    head_dim = width // heads
    half_rows = width // 2
    wide = cotangent_ref.shape[1]
    del token_ref
    loads = [
        pltpu.make_async_copy(lift_hbm, lift_ref, load_sem.at[0]),
        pltpu.make_async_copy(skip_hbm, skip_ref, load_sem.at[1]),
        pltpu.make_async_copy(mix_hbm, mix_ref, load_sem.at[2]),
    ]
    for at in range(3):
        loads.append(
            pltpu.make_async_copy(joint_hbm.at[:, pl.ds(at * width, width)], joint_ref.at[at], load_sem.at[3 + at])
        )
    for at, (source, target) in enumerate(
        ((merge_hbm, merge_ref), (head_hbm, head_ref), (shrink_hbm, shrink_ref), (grow_hbm, grow_ref))
    ):
        loads.append(pltpu.make_async_copy(source, target, load_sem.at[6 + at]))
    for copy in loads:
        copy.start()
    stores = []

    def store(source, target, first=0, count=None):
        span = pl.ds(first, source.shape[0] - first if count is None else count)
        copy = pltpu.make_async_copy(source.at[span], target.at[span], store_sem.at[len(stores)])
        copy.start()
        stores.append(copy)

    def split(turned, name, pack, at):
        first = OWN.index(name) * half_rows
        split_rows(place_ref, turned, pack, own.at[pl.ds(first, half_rows)], at, UNITS)
        store(own, own_hbm, first, half_rows)

    places = later_rows(width, wide) | rest_rows(width)

    kept, starts, _, _, center, shifted, _, sigma = series_statistics(lengths_ref, series_ref, flags_ref, patch_len)
    scaled = (shifted / sigma * kept).astype(jnp.bfloat16)
    flag_values = flags_ref[...].astype(jnp.float32).astype(jnp.bfloat16)
    spread_out = belongs(rows, count, patches, jnp.bfloat16)
    inside = own_patch(rows, points, patches, patch_len)
    lane = iota((points, 2 * patch_len), 1)
    point = remainder(iota((points, 2 * patch_len), 0), patch_len)
    fold_left = (lane == point).astype(jnp.bfloat16)
    fold_right = (lane == point + patch_len).astype(jnp.bfloat16)
    left = jnp.where(inside, dot_plain(spread_out, scaled), 0.0).astype(jnp.bfloat16)
    right = jnp.where(inside, dot_plain(spread_out, flag_values), 0.0).astype(jnp.bfloat16)
    tokens = (dot_plain(left, fold_left) + dot_plain(right, fold_right)).astype(jnp.bfloat16)
    tokens_out[...] = tokens
    spread_exact = belongs(rows, count, patches, jnp.float32)
    sigma_rows = dot_exact(spread_exact, jnp.broadcast_to(sigma, (count, wide)))
    center_rows = dot_exact(spread_exact, jnp.broadcast_to(center, (count, wide)))
    starts_rows = dot_exact(spread_exact, jnp.broadcast_to(starts.astype(jnp.float32), (count, wide)))
    patch_row = remainder(iota((rows, wide), 0), patches).astype(jnp.float32)
    valid = (patch_row >= starts_rows - 0.5).astype(jnp.float32)
    block = allowed_ref.shape[1]
    key_at = remainder(iota((rows, block), 0), block)
    query_at = iota((rows, block), 1)
    key_pos, query_pos = remainder(key_at, patches), remainder(query_at, patches)
    allowed_ref[...] = (
        (quotient(key_at, patches) == quotient(query_at, patches))
        & (key_pos <= query_pos)
        & ((key_pos.astype(jnp.float32) >= starts_rows[:, :1] - 0.5) | (key_pos == query_pos))
    ).astype(jnp.float32)

    loads[0].wait()
    hidden_pre = dot_plain(tokens, lift_ref[...])
    hidden_act = (hidden_pre * logistic(hidden_pre)).astype(jnp.bfloat16)
    flip_ref[...] = hidden_act.T
    split(flip_ref, "hidden", rest, places["hidden"])
    store(rest, rest_hbm, places["hidden"], half_rows)
    loads[1].wait()
    loads[2].wait()
    embedded = dot_plain(hidden_act, mix_ref[...]) + dot_plain(tokens, skip_ref[...])
    embedded_ref[...] = embedded
    store(embedded_ref, embedded_hbm)
    scale_one = lax.rsqrt(jnp.mean(embedded * embedded, axis=1, keepdims=True) + epsilon)
    normed_one = (embedded * scale_one * gain_first_ref[...][None, :]).astype(jnp.bfloat16)
    for at in range(3):
        loads[3 + at].wait()
        tile = rows
        for part in range(width // tile):
            result = dot_plain(normed_one, joint_ref[at, :, part * tile : (part + 1) * tile])
            joint_turned[at * width + part * tile : at * width + (part + 1) * tile, :] = result.T
    flip_ref[...] = normed_one.T
    split(flip_ref, "normed_one", rest, places["normed_one"])
    store(rest, rest_hbm, places["normed_one"], half_rows)

    scale = head_dim ** (-0.5)
    cosine, sine = cosine_ref[...], sine_ref[...]

    def one_head(head, _):
        begin = pl.multiple_of(head * head_dim, 16)
        query = joint_turned[pl.ds(begin, head_dim), :]
        key = joint_turned[pl.ds(width + begin, head_dim), :]
        value = joint_turned[pl.ds(2 * width + begin, head_dim), :].astype(jnp.bfloat16)
        query = (query * cosine + turn_half(query) * sine).astype(jnp.bfloat16)
        key = (key * cosine + turn_half(key) * sine).astype(jnp.bfloat16)
        turned_ref[pl.ds(begin, head_dim), :] = query
        turned_ref[pl.ds(width + begin, head_dim), :] = key
        turned_ref[pl.ds(2 * width + begin, head_dim), :] = value
        mixed, sums = [], []
        for at in range(rows // block):
            span = slice(at * block, (at + 1) * block)
            scores = dot_over(key[:, span], query[:, span], 0, 0) * scale
            scores = jnp.where(allowed_ref[span, :] > 0.5, scores, masked_value)
            top = jnp.max(scores, axis=0, keepdims=True)
            raised = jnp.exp(scores - top)
            total = jnp.sum(raised, axis=0, keepdims=True)
            sums.append(top + jnp.log(total))
            probs = (raised / total).astype(jnp.bfloat16)
            mixed.append(dot_plain(value[:, span], probs))
        logsum_out[pl.ds(head, 1), :] = jnp.concatenate(sums, axis=1)
        mixed_turned[pl.ds(begin, head_dim), :] = jnp.concatenate(mixed, axis=1).astype(jnp.bfloat16)
        return 0

    lax.fori_loop(0, heads, one_head, 0, unroll=2)
    store(turned_ref, turned_hbm)
    split(mixed_turned, "mixed", rest, places["mixed"])
    store(rest, rest_hbm, places["mixed"], half_rows)
    mixed = mixed_turned[...].T
    loads[6].wait()
    resid_one = embedded_ref[...] + dot_plain(mixed, merge_ref[...])
    resid_ref[...] = resid_one
    scale_two = lax.rsqrt(jnp.mean(resid_one * resid_one, axis=1, keepdims=True) + epsilon)
    normed_two = (resid_one * scale_two * gain_second_ref[...][None, :]).astype(jnp.bfloat16)
    flip_ref[...] = normed_two.T
    split(flip_ref, "normed_two", later, places["normed_two"])
    store(later, later_hbm, places["normed_two"], half_rows)

    outer = cotangent_ref[...] * valid
    head_back = (outer * sigma_rows).astype(jnp.bfloat16)
    loads[7].wait()
    resid_back = dot_over(head_back, head_ref[...], 1, 1)
    back_ref[...] = resid_back
    branch_back = resid_back.astype(jnp.bfloat16)
    flip_ref[...] = branch_back.T
    split(flip_ref, "branch", soon, 0)

    loads[9].wait()
    upper_pre = dot_plain(normed_two, grow_ref[...])
    upper_ref[...] = upper_pre
    active = (upper_pre * logistic(upper_pre)).astype(jnp.bfloat16)
    put_tiles(soon, half_rows, active)
    store(soon, soon_hbm)
    loads[8].wait()
    upper_pre = upper_ref[...]
    gate = logistic(upper_pre)
    slope = gate * (1.0 + upper_pre * (1.0 - gate))
    upper_back = (dot_over(branch_back, shrink_ref[...], 1, 1) * slope).astype(jnp.bfloat16)
    put_tiles(later, places["upper"], upper_back)
    store(later, later_hbm, places["upper"], width)
    resid_low = (resid_ref[...] + dot_plain(active, shrink_ref[...])).astype(jnp.bfloat16)
    flip_ref[...] = resid_low.T
    split(flip_ref, "resid", later, places["resid"])
    store(later, later_hbm, places["resid"], half_rows)
    later[places["head"] : places["head"] + wide, :] = head_back.astype(jnp.float32).T
    store(later, later_hbm, places["head"], wide)

    normed_back = dot_over(upper_back, grow_ref[...], 1, 1)
    resid_one = resid_ref[...]
    second_out[...] = jnp.sum(normed_back * resid_one * scale_two, axis=0, keepdims=True)
    through = normed_back * gain_second_ref[...][None, :]
    inner = jnp.mean(through * resid_one, axis=1, keepdims=True)
    middle = back_ref[...] + scale_two * through - resid_one * (scale_two * scale_two * scale_two * inner)
    middle_ref[...] = middle
    store(middle_ref, middle_hbm)
    put_tiles(rest, places["middle"], middle.astype(jnp.bfloat16))
    store(rest, rest_hbm, places["middle"], width)

    head_out = dot_plain(resid_low, head_ref[...])
    predictions_ref[...] = valid * (head_out * sigma_rows + center_rows)
    gather = belongs_back(rows, count, patches, jnp.float32)
    sigma_sum_out[...] = dot_exact(gather, outer * head_out)
    center_sum_out[...] = dot_exact(gather, outer)
    for copy in stores:
        copy.wait()


def front(place, lengths, series, flags, cotangent, tables, weights, heads, cost):
    lift, mix, skip, gain_first, joint, merge, gain_second, grow, shrink, head = weights
    rows, horizon = cotangent.shape
    width = mix.shape[0]
    half = width // 2
    count = series.shape[0]
    f32, bf16 = jnp.float32, jnp.bfloat16
    vmem = pl.BlockSpec(memory_space=pltpu.VMEM)
    smem = pl.BlockSpec(memory_space=pltpu.SMEM)
    hbm = pl.BlockSpec(memory_space=pl.ANY)
    shape = jax.ShapeDtypeStruct
    packs = [
        (len(OWN) * half, rows),
        (half + width, rows),
        (later_rows(width, horizon)["end"], rows),
        (rest_rows(width)["end"], rows),
    ]
    outs = [
        TOKEN,
        shape((rows, horizon), f32),
        shape((rows, lift.shape[0]), bf16),
        shape((heads, rows), f32),
        shape((count, horizon), f32),
        shape((count, horizon), f32),
        shape((1, width), f32),
        shape((rows, width), f32),
        shape((rows, width), f32),
        shape((3 * width, rows), bf16),
    ] + [shape(pack, f32) for pack in packs]
    scratch = [
        pltpu.VMEM(lift.shape, bf16),
        pltpu.VMEM(mix.shape, bf16),
        pltpu.VMEM(skip.shape, bf16),
        pltpu.VMEM((3, width, width), bf16),
        pltpu.VMEM(merge.shape, bf16),
        pltpu.VMEM(grow.shape, bf16),
        pltpu.VMEM(shrink.shape, bf16),
        pltpu.VMEM(head.shape, bf16),
        pltpu.VMEM((rows, width), f32),
        pltpu.VMEM((rows, width), f32),
        pltpu.VMEM((3 * width, rows), f32),
        pltpu.VMEM((3 * width, rows), bf16),
        pltpu.VMEM((width, rows), bf16),
        pltpu.VMEM((rows, BLOCK), f32),
        pltpu.VMEM((rows, width), f32),
        pltpu.VMEM((rows, width), f32),
        pltpu.VMEM((rows, width), f32),
        pltpu.VMEM((width, rows), bf16),
    ] + [pltpu.VMEM(pack, f32) for pack in packs]
    scratch += [pltpu.SemaphoreType.DMA((10,)), pltpu.SemaphoreType.DMA((18,))]
    return pl.pallas_call(
        functools.partial(front_kernel, heads),
        out_shape=outs,
        in_specs=[smem, smem] + [vmem] * 7 + [hbm] * 8,
        out_specs=[hbm] + [vmem] * 6 + [hbm] * 7,
        scratch_shapes=scratch,
        compiler_params=pltpu.CompilerParams(vmem_limit_bytes=62 * 1024 * 1024),
        cost_estimate=expect(cost),
    )(
        lengths,
        place,
        series,
        flags,
        cotangent,
        gain_first,
        gain_second,
        *tables,
        lift,
        mix,
        skip,
        joint,
        merge,
        grow,
        shrink,
        head,
    )


def back_kernel(
    heads,
    lengths_ref,
    place_ref,
    series_ref,
    flags_ref,
    gain_first_ref,
    cosine_ref,
    sine_ref,
    tokens_ref,
    logsum_ref,
    sigma_sum_ref,
    center_sum_ref,
    second_ref,
    middle_hbm,
    turned_hbm,
    embedded_hbm,
    lift_hbm,
    mix_hbm,
    skip_hbm,
    joint_hbm,
    merge_hbm,
    token_in,
    token_ref,
    series_grad_ref,
    joint_hbm_out,
    last_hbm,
    own_hbm,
    lift_ref,
    mix_ref,
    skip_ref,
    joint_ref,
    merge_ref,
    embedded_ref,
    middle_ref,
    turned_ref,
    mixed_turned,
    joint_turned,
    first_ref,
    allowed_ref,
    flip_ref,
    joint_pack,
    last,
    own,
    load_sem,
    store_sem,
):
    rows, width = embedded_ref.shape
    count, points = series_ref.shape
    patches = rows // count
    patch_len = points // patches
    head_dim = width // heads
    half_rows = width // 2
    del token_in, token_ref
    loads = [
        pltpu.make_async_copy(source, target, load_sem.at[at])
        for at, (source, target) in enumerate(
            (
                (merge_hbm, merge_ref),
                (joint_hbm, joint_ref),
                (embedded_hbm, embedded_ref),
                (mix_hbm, mix_ref),
                (lift_hbm, lift_ref),
                (skip_hbm, skip_ref),
                (middle_hbm, middle_ref),
                (turned_hbm, turned_ref),
            )
        )
    ]
    for at in (6, 0, 7, 1, 2, 3, 4, 5):
        loads[at].start()
    stores = []

    def store(source, target, first=0, count=None):
        span = pl.ds(first, source.shape[0] - first if count is None else count)
        copy = pltpu.make_async_copy(source.at[span], target.at[span], store_sem.at[len(stores)])
        copy.start()
        stores.append(copy)

    places = last_rows(width, patch_len, rows)

    kept, starts, hot_kept, kept_count, center, shifted, spread, sigma = series_statistics(
        lengths_ref, series_ref, flags_ref, patch_len
    )
    block = allowed_ref.shape[1]
    spread_exact = belongs(rows, count, patches, jnp.float32)
    starts_rows = dot_exact(spread_exact, jnp.broadcast_to(starts.astype(jnp.float32), (count, block)))
    key_at = remainder(iota((rows, block), 0), block)
    query_at = iota((rows, block), 1)
    key_pos, query_pos = remainder(key_at, patches), remainder(query_at, patches)
    allowed_ref[...] = (
        (quotient(key_at, patches) == quotient(query_at, patches))
        & (key_pos <= query_pos)
        & ((key_pos.astype(jnp.float32) >= starts_rows - 0.5) | (key_pos == query_pos))
    ).astype(jnp.float32)
    scale = head_dim ** (-0.5)
    cosine, sine = cosine_ref[...], sine_ref[...]
    loads[0].wait()
    loads[6].wait()
    mixed_turned[...] = dot_over(merge_ref[...], middle_ref[...].astype(jnp.bfloat16), 1, 1).astype(jnp.bfloat16)

    def unrotate(gradient):
        return gradient * cosine + turn_half_back(gradient * sine)

    def one_head(head, _):
        begin = pl.multiple_of(head * head_dim, 16)
        query = turned_ref[pl.ds(begin, head_dim), :]
        key = turned_ref[pl.ds(width + begin, head_dim), :]
        value = turned_ref[pl.ds(2 * width + begin, head_dim), :]
        upstream = mixed_turned[pl.ds(begin, head_dim), :]
        logsum = logsum_ref[pl.ds(head, 1), :]
        query_parts, key_parts, value_parts = [], [], []
        for at in range(rows // block):
            span = slice(at * block, (at + 1) * block)
            query_in, key_in, value_in, up = query[:, span], key[:, span], value[:, span], upstream[:, span]
            scores = dot_over(key_in, query_in, 0, 0) * scale
            scores = jnp.where(allowed_ref[span, :] > 0.5, scores, masked_value)
            probs = jnp.exp(scores - logsum[:, span])
            value_parts.append(dot_over(up, probs.astype(jnp.bfloat16), 1, 1))
            probs_back = dot_over(value_in, up, 0, 0)
            inner = jnp.sum(probs * probs_back, axis=0, keepdims=True)
            scores_back = (probs * (probs_back - inner) * scale).astype(jnp.bfloat16)
            query_parts.append(dot_plain(key_in, scores_back))
            key_parts.append(dot_over(query_in, scores_back, 1, 1))
        for at, parts in enumerate((query_parts, key_parts, value_parts)):
            result = jnp.concatenate(parts, axis=1)
            if at < 2:
                result = unrotate(result)
            result = result.astype(jnp.bfloat16)
            joint_turned[pl.ds(at * width + begin, head_dim), :] = result
            joint_pack[pl.ds(at * width + begin, head_dim), :] = result.astype(jnp.float32)
        return 0

    loads[7].wait()
    lax.fori_loop(0, heads, one_head, 0, unroll=8)
    store(joint_pack, joint_hbm_out)
    loads[1].wait()
    tile = rows
    for part in range(width // tile):
        span = slice(part * tile, (part + 1) * tile)
        first_ref[:, span] = dot_plain(joint_ref[span, :], joint_turned[...]).T
    loads[2].wait()
    embedded = embedded_ref[...]
    first_back = first_ref[...]
    scale_one = lax.rsqrt(jnp.mean(embedded * embedded, axis=1, keepdims=True) + epsilon)
    first_sum = jnp.sum(first_back * embedded * scale_one, axis=0, keepdims=True)
    through = first_back * gain_first_ref[...][None, :]
    inner = jnp.mean(through * embedded, axis=1, keepdims=True)
    embed_low = (
        middle_ref[...] + scale_one * through - embedded * (scale_one * scale_one * scale_one * inner)
    ).astype(jnp.bfloat16)
    put_tiles(last, places["embed_tiles"], embed_low)
    flip_ref[...] = embed_low.T
    split_rows(place_ref, flip_ref, last, own.at[pl.ds(0, half_rows)], places["embed"], UNITS)
    store(last, last_hbm, places["embed_tiles"], width + half_rows)
    tokens = tokens_ref[...]
    loads[4].wait()
    hidden_pre = dot_plain(tokens, lift_ref[...])
    gate = logistic(hidden_pre)
    slope = gate * (1.0 + hidden_pre * (1.0 - gate))
    loads[3].wait()
    pre_back = (dot_over(embed_low, mix_ref[...], 1, 1) * slope).astype(jnp.bfloat16)
    flip_ref[...] = pre_back.T
    split_rows(place_ref, flip_ref, last, own.at[pl.ds(half_rows, half_rows)], places["pre"], UNITS)
    store(own, own_hbm)
    last[places["tokens"] : places["sums"], :] = tokens.astype(jnp.float32).T
    row = iota((8, width), 0)
    sums = jnp.where(row == 0, second_ref[...], jnp.where(row == 1, first_sum, 0.0))
    for at in range(width // rows):
        first = places["sums"] + 8 * at
        last[first : first + 8, :] = sums[:, at * rows : (at + 1) * rows]
    store(last, last_hbm, places["pre"])

    loads[5].wait()
    token_back = dot_over(pre_back, lift_ref[...], 1, 1) + dot_over(embed_low, skip_ref[...], 1, 1)
    lane = remainder(iota((2 * patch_len, points), 1), patch_len)
    unfold = (lane == iota((2 * patch_len, points), 0)).astype(jnp.float32)
    inside = own_patch(rows, points, patches, patch_len)
    spread_back_rows = jnp.where(inside, dot_exact(token_back, unfold), 0.0)
    scaled_back = dot_exact(belongs_back(rows, count, patches, jnp.float32), spread_back_rows)
    kept_back = scaled_back * kept
    point_back = kept_back / sigma
    sigma_back = jnp.sum(sigma_sum_ref[...], axis=1, keepdims=True)
    center_back = jnp.sum(center_sum_ref[...], axis=1, keepdims=True)
    center_total = center_back - jnp.sum(point_back, axis=1, keepdims=True)
    sigma_total = sigma_back - jnp.sum(kept_back * shifted, axis=1, keepdims=True) / (sigma * sigma)
    spread_grad = jnp.where(spread > 1.0, sigma_total * 0.5 / sigma, 0.0)
    offset_sum = jnp.sum(hot_kept * 2.0 * shifted, axis=1, keepdims=True)
    center_all = center_total - spread_grad * offset_sum / kept_count
    series_grad_ref[...] = point_back + hot_kept * (center_all + 2.0 * shifted * spread_grad) / kept_count
    for copy in stores:
        copy.wait()


def back(token, place, lengths, series, flags, tables, weights, kept_values, heads, cost):
    lift, mix, skip, gain_first, joint, merge = weights
    tokens, logsum, sigma_sum, center_sum, second_sum, embedded, middle, turned = kept_values
    rows, width = embedded.shape
    half = width // 2
    f32, bf16 = jnp.float32, jnp.bfloat16
    vmem = pl.BlockSpec(memory_space=pltpu.VMEM)
    smem = pl.BlockSpec(memory_space=pltpu.SMEM)
    hbm = pl.BlockSpec(memory_space=pl.ANY)
    shape = jax.ShapeDtypeStruct
    packs = [(3 * width, rows), (last_rows(width, lift.shape[0] // 2, rows)["end"], rows), (2 * half, rows)]
    scratch = [
        pltpu.VMEM(lift.shape, bf16),
        pltpu.VMEM(mix.shape, bf16),
        pltpu.VMEM(skip.shape, bf16),
        pltpu.VMEM(joint.shape, bf16),
        pltpu.VMEM(merge.shape, bf16),
        pltpu.VMEM((rows, width), f32),
        pltpu.VMEM((rows, width), f32),
        pltpu.VMEM((3 * width, rows), bf16),
        pltpu.VMEM((width, rows), bf16),
        pltpu.VMEM((3 * width, rows), bf16),
        pltpu.VMEM((rows, width), f32),
        pltpu.VMEM((rows, BLOCK), f32),
        pltpu.VMEM((width, rows), bf16),
    ] + [pltpu.VMEM(pack, f32) for pack in packs]
    scratch += [pltpu.SemaphoreType.DMA((8,)), pltpu.SemaphoreType.DMA((4,))]
    return pl.pallas_call(
        functools.partial(back_kernel, heads),
        out_shape=[TOKEN, shape(series.shape, f32)] + [shape(pack, f32) for pack in packs],
        in_specs=[smem, smem] + [vmem] * 10 + [hbm] * 9,
        out_specs=[hbm, vmem] + [hbm] * 3,
        scratch_shapes=scratch,
        compiler_params=pltpu.CompilerParams(vmem_limit_bytes=62 * 1024 * 1024),
        cost_estimate=expect(cost),
    )(
        lengths,
        place,
        series,
        flags,
        gain_first,
        *tables,
        tokens,
        logsum,
        sigma_sum,
        center_sum,
        second_sum,
        middle,
        turned,
        embedded,
        lift,
        mix,
        skip,
        joint,
        merge,
        token,
    )


def gradient_kernel(place_ref, *refs, pieces, arrays, unit):
    sources = refs[:arrays]
    token_ref, outputs = refs[arrays + 1], refs[arrays + 2 : arrays + 2 + 2 * len(pieces)]
    result_ref, left_raw, left_ref, right_raw, load_sem, store_sem = refs[arrays + 2 + 2 * len(pieces) :]
    del token_ref
    total = 4 * unit
    rows = left_raw.shape[2]
    loads, stores, lefts, rights = [], [], {}, []

    def load(source, first, target):
        copy = pltpu.make_async_copy(sources[source].at[pl.ds(first, target.shape[0])], target, load_sem.at[len(loads)])
        copy.start()
        loads.append(copy)
        return copy

    place = 0
    for _, terms in pieces:
        for own, own_row, other, other_row, near, far, row, kind, width in terms:
            key = (own, own_row, other, other_row)
            if kind != "sum" and key not in lefts:
                at = len(lefts)
                copies = [load(own, own_row, left_raw.at[2 * at]), load(other, other_row, left_raw.at[2 * at + 1])]
                lefts[key] = (at, copies)
            tiles = []
            for tile in range(0, width, rows):
                size = min(rows, width - tile)
                spots = [right_raw.at[pl.ds(place + side * size, size)] for side in (0, 1)]
                place += 2 * size
                tiles.append((size, spots, [load(side, row + tile, spot) for side, spot in zip((near, far), spots)]))
            rights.append(tiles)
    waited = set()
    number = 0
    tile_at = 0
    for order, (axis, terms) in enumerate(pieces):
        core = place_ref[0]
        stride, across = 1 + core, 2 - core
        if axis == "z":
            height, mine = unit // 2, place_ref[3] & 1
            groups = [stride * a + across * b for b in (0, 1) for a in (0, 1)]
            starts = [group * unit + half * height for half in (1 - mine, mine) for group in groups]
        else:
            height, mine = unit, place_ref[1]
            starts = [(stride * side + across * other) * unit for side in (1 - mine, mine) for other in (0, 1)]
        out_tile = 0

        def store(count):
            for half in (0, 1):
                copy = pltpu.make_async_copy(
                    result_ref.at[pl.ds(tile_at, count), pl.ds(half * total // 2, total // 2)],
                    outputs[2 * order + half].at[pl.ds(out_tile, count)],
                    store_sem.at[len(stores)],
                )
                copy.start()
                stores.append(copy)

        held = None
        for own, own_row, other, other_row, _, _, _, kind, width in terms:
            tiles = rights[number]
            number += 1
            if kind == "sum":
                for _, spots, copies in tiles:
                    for copy in copies:
                        copy.wait()
                both = tiles[0][1][0][...] + tiles[0][1][1][...]
                lanes = jnp.concatenate([both[part : part + 8, :] for part in range(0, width, 8)], axis=1)
                tall = jnp.concatenate([lanes, jnp.zeros((BLOCK - 8, lanes.shape[1]), jnp.float32)], axis=0).T
                unit_rows = tall.reshape(UNITS // 2, 2, unit, BLOCK)
                spare = left_raw.at[left_raw.shape[0] - 1]
                spare[:, :BLOCK] = jnp.where(place_ref[0] == 0, unit_rows[:, 0], unit_rows[:, 1]).reshape(total, BLOCK)
                for slot, first in enumerate(starts):
                    result_ref[tile_at, slot * height : (slot + 1) * height, :] = spare[
                        pl.ds(pl.multiple_of(first, 16), height), :BLOCK
                    ]
                store(1)
                tile_at += 1
                out_tile += 1
                continue
            at, copies = lefts[(own, own_row, other, other_row)]
            if at not in waited:
                waited.add(at)
                for copy in copies:
                    copy.wait()
            if held != at:
                held = at
                for slot, first in enumerate(starts):
                    first = pl.multiple_of(first, 16)
                    span = slice(slot * height, (slot + 1) * height)
                    for side in (0, 1):
                        left_ref[order % 2, span, side * rows : (side + 1) * rows] = left_raw[
                            2 * at + side, pl.ds(first, height), :
                        ].astype(jnp.bfloat16)
            left = left_ref[order % 2]
            for size, spots, copies in tiles:
                for copy in copies:
                    copy.wait()
                near, far = (spot[...].astype(jnp.bfloat16) for spot in spots)
                if kind == "tiles":
                    result = dot_plain(left, jnp.concatenate([near, far], axis=0))
                else:
                    right = jnp.concatenate([near, far], axis=1)
                    if kind != "turned":
                        blank = jnp.zeros_like(right)
                        right = jnp.concatenate((right, blank) if kind == "low" else (blank, right), axis=0)
                    result = dot_over(left, right, 1, 1)
                count = result.shape[1] // BLOCK
                for part in range(count):
                    piece = result[:, part * BLOCK : (part + 1) * BLOCK]
                    if kind == "high":
                        result_ref[tile_at + part] += piece
                    else:
                        result_ref[tile_at + part] = piece
                if kind != "low":
                    store(count)
                    tile_at += count
                    out_tile += count
    for copy in stores:
        copy.wait()


def tiles_of(terms):
    widths = {"low": 0, "high": BLOCK, "sum": BLOCK}
    return sum(widths.get(term[7], term[8]) for term in terms) // BLOCK


def weight_gradient(token, place, arrays, pieces, unit, cost):
    rows = arrays[0].shape[1]
    total = 4 * unit
    hbm = pl.BlockSpec(memory_space=pl.ANY)
    vmem = pl.BlockSpec(memory_space=pltpu.VMEM)
    counts = [tiles_of(terms) for _, terms in pieces]
    every = [term for _, terms in pieces for term in terms]
    lefts = len({term[:4] for term in every if term[7] != "sum"})
    copies = 2 * lefts + sum(2 * (-(-term[8] // rows)) for term in every)
    shapes = [jax.ShapeDtypeStruct((count, total // 2, BLOCK), jnp.float32) for count in counts for _ in (0, 1)]
    results = pl.pallas_call(
        functools.partial(gradient_kernel, pieces=pieces, arrays=len(arrays), unit=unit),
        in_specs=[pl.BlockSpec(memory_space=pltpu.SMEM)] + [hbm] * (len(arrays) + 1),
        out_specs=[hbm] * (1 + len(shapes)),
        scratch_shapes=[
            pltpu.VMEM((sum(counts), total, BLOCK), jnp.float32),
            pltpu.VMEM((2 * lefts + 1, total, rows), jnp.float32),
            pltpu.VMEM((2, total, 2 * rows), jnp.bfloat16),
            pltpu.VMEM((2 * sum(term[8] for term in every), rows), jnp.float32),
            pltpu.SemaphoreType.DMA((copies,)),
            pltpu.SemaphoreType.DMA((copies,)),
        ],
        out_shape=[TOKEN] + shapes,
        compiler_params=pltpu.CompilerParams(vmem_limit_bytes=VMEM_GRADIENT * 1024 * 1024),
        cost_estimate=expect(cost),
    )(place, *arrays, token)
    return results[0], [results[1 + 2 * at : 3 + 2 * at] for at in range(len(pieces))]


def combine_kernel(place_ref, *refs, inputs, parts, which, last, spread, passed):
    total = sum(inputs)
    sources = refs[:total]
    token_ref = refs[total + 1]
    results = refs[total + 2 : total + 2 + (len(inputs) if last else 1 if spread else parts)]
    scratch = refs[total + 2 + len(results) :]
    raws, sums, load_sem, store_sem = scratch[:total], scratch[total], scratch[total + 1], scratch[total + 2]
    del token_ref
    mine = place_ref[which] & (parts - 1)
    chosen = [step if spread else mine ^ ((step + 1) & (parts - 1)) for step in range(parts)]
    loads, stores = {}, []
    for step in range(parts):
        for at in range(total):
            copy = pltpu.make_async_copy(
                sources[at].at[:, :, chosen[step]], raws[at].at[step], load_sem.at[step * total + at]
            )
            copy.start()
            loads[step, at] = copy
    for step in range(parts):
        first = 0
        begin = 0
        for group, count in enumerate(inputs):
            for at in range(first, first + count):
                loads[step, at].wait()
            value = raws[first][step]
            for at in range(first + 1, first + count):
                if passed:
                    outside = jnp.logical_or(place_ref[3] == 0, place_ref[3] == 3)
                    value = jnp.where(outside, value, raws[at][step])
                else:
                    value = value + raws[at][step]
            tiles = value.shape[0]
            if last:
                fold = tiles // (results[group].shape[1] // BLOCK)
                tiles //= fold
                for tile in range(tiles):
                    piece = value[tile, 0]
                    for part in range(1, fold):
                        piece = piece + value[part * tiles + tile, 0]
                    results[group][:, tile * BLOCK : (tile + 1) * BLOCK] = piece
            else:
                sums[step, begin : begin + tiles] = value
                copy = pltpu.make_async_copy(
                    sums.at[step, pl.ds(begin, tiles)],
                    results[0].at[step, pl.ds(begin, tiles)] if spread else results[step].at[pl.ds(begin, tiles)],
                    store_sem.at[len(stores)],
                )
                copy.start()
                stores.append(copy)
            begin += tiles
            first += count
    for copy in stores:
        copy.wait()


def combine(token, place, groups, before, parts, which, cost, last=False, spread=False, fold=1, passed=False):
    rows = groups[0][0].shape[1]
    after = rows // (before * parts)
    flat = [array.reshape(array.shape[0], before, parts, after, BLOCK) for group in groups for array in group]
    tiles = [group[0].shape[0] for group in groups]
    hbm = pl.BlockSpec(memory_space=pl.ANY)
    vmem = pl.BlockSpec(memory_space=pltpu.VMEM)
    shape = jax.ShapeDtypeStruct
    if last:
        shapes = [shape((rows, count // fold * BLOCK), jnp.float32) for count in tiles]
    elif spread:
        shapes = [shape((parts, sum(tiles), before, after, BLOCK), jnp.float32)]
    else:
        shapes = [shape((sum(tiles), before, after, BLOCK), jnp.float32)] * parts
    results = pl.pallas_call(
        functools.partial(
            combine_kernel, inputs=tuple(len(group) for group in groups), parts=parts, which=which, last=last, spread=spread, passed=passed
        ),
        in_specs=[pl.BlockSpec(memory_space=pltpu.SMEM)] + [hbm] * (len(flat) + 1),
        out_specs=[hbm] + [vmem if last else hbm] * len(shapes),
        scratch_shapes=[pltpu.VMEM((parts, array.shape[0], before, after, BLOCK), jnp.float32) for array in flat]
        + [
            pltpu.VMEM((1,) * 5 if last else (parts, sum(tiles), before, after, BLOCK), jnp.float32),
            pltpu.SemaphoreType.DMA((parts * len(flat),)),
            pltpu.SemaphoreType.DMA((parts * len(groups),)),
        ],
        out_shape=[TOKEN] + shapes,
        compiler_params=pltpu.CompilerParams(vmem_limit_bytes=VMEM_COMBINE * 1024 * 1024),
        cost_estimate=expect(cost),
    )(place, *flat, token)
    if last or spread:
        return results[0], results[1:]
    return results[0], [result.reshape(sum(tiles), before * after, BLOCK) for result in results[1:]]


class Layout:
    def __init__(self, mesh_shape):
        self.wide = mesh_shape["wide"]
        self.narrow = mesh_shape["narrow"]
        self.total = self.wide * self.narrow
        self.paired = self.wide == 8 and self.narrow == 4

    def flip(self, bit):
        return [(i, i ^ bit) for i in range(self.total)]

    def middle(self):
        swapped = {1: 2, 2: 1}
        return [(i, (i & ~3) | swapped[i & 3] if i & 3 in swapped else i ^ 4) for i in range(self.total)]

    def across(self, first):
        return [(i, i ^ (8 if (i & 4 == 0) == first else 16)) for i in range(self.total)]

    def position(self):
        wide = lax.axis_index("wide")
        core, x, y = wide % 2, wide // 2 % 2, wide // 4 % 2
        places = (core, jnp.where(core == 0, x, y), jnp.where(core == 0, y, x), lax.axis_index("narrow"))
        if not self.paired:
            places = tuple(jnp.zeros_like(place) for place in places)
        return jnp.stack(places).astype(jnp.int32)


class Bundle:
    def __init__(self, names, plan, axes, groups, fold=1, passed=False):
        self.names, self.plan, self.axes, self.groups = names, plan, axes, groups
        self.fold, self.passed = fold, passed


def steps_of(order):
    plan = []
    for axis in order:
        plan += ["half", "middle", "part"] if axis == "z" else [axis]
    return plan


def move(layout, array, step):
    if step == "middle":
        pairs = layout.middle()
    else:
        pairs = layout.across(step == "a") if step in ("a", "b") else layout.flip(1)
    return lax.ppermute(array, AXES, pairs)


def start_bundles(layout, token, place, arrays, names, terms, unit, cost):
    plans = [steps_of(ORDERS[name]) for name in names]
    token, results = weight_gradient(
        token, place, arrays, tuple((ORDERS[name][0], terms[name]) for name in names), unit, cost
    )
    bundles = {}
    for name, plan, (send, keep) in zip(names, plans, results):
        step = plan.pop(0)
        axes = [axis for axis in ("b", "a", "half", "part") if axis != step]
        bundles[name] = Bundle([name], plan, axes, [[keep, move(layout, send, step)]])
    return token, bundles


def advance(layout, token, place, bundles, rows, cost, finished):
    plan, axes = bundles[0].plan, bundles[0].axes
    groups = [group for bundle in bundles for group in bundle.groups]
    names = [name for bundle in bundles for name in bundle.names]
    sizes = [group[0].shape[0] for group in groups]
    if not plan:
        token, results = combine(token, place, groups, 1, 1, 0, cost, last=True, fold=bundles[0].fold)
        wide = results[0] if len(results) == 1 else jnp.concatenate(results, axis=1)
        finished.append((names, wide))
        return token, None
    step, plan = plan[0], plan[1:]
    if step == "middle":
        token, (whole,) = combine(token, place, groups, 1, 1, 0, cost)
        return token, Bundle(names, plan, axes, [[whole, move(layout, whole, step)]], passed=True)
    if step == "Y":
        token, (whole,) = combine(token, place, groups, 1, 4, 0, cost, spread=True)
        got = lax.all_to_all(whole, "narrow", 0, 0, tiled=True)
        return token, Bundle(names, plan, [], [[got.reshape(4 * sum(sizes), rows, BLOCK)]], 4)
    at = axes.index(step)
    which = {"a": 1, "b": 2}.get(step, 3)
    token, (send, keep) = combine(token, place, groups, 2**at, 2, which, cost, passed=bundles[0].passed)
    return token, Bundle(names, plan, [axis for axis in axes if axis != step], [[keep, move(layout, send, step)]])


def whole_rows(own, other):
    unit = own.shape[0] // (UNITS // 2)
    pair = jnp.stack([own.reshape(-1, unit, own.shape[1]), other.reshape(-1, unit, own.shape[1])], axis=1)
    return pair.reshape(2 * own.shape[0], own.shape[1])


def whole_tiles(tiles, rows):
    return jnp.concatenate([tiles[at : at + rows] for at in range(0, tiles.shape[0], rows)], axis=1)


def per_device(
    layout,
    series,
    flags,
    lengths,
    lift_weight,
    mix_weight,
    skip_weight,
    gain_first,
    joint_weight,
    merge_weight,
    gain_second,
    grow_weight,
    shrink_weight,
    head_weight,
    cotangent,
):
    count = series.shape[0]
    patches, horizon = cotangent.shape[1:]
    width = mix_weight.shape[0]
    hidden = shrink_weight.shape[0]
    rows = count * patches
    half = width // 2
    tables = rotary_tables(patches, width // HEADS, count)
    place = layout.position()
    weights = (
        lift_weight,
        mix_weight,
        skip_weight,
        gain_first,
        joint_weight,
        merge_weight,
        gain_second,
        grow_weight,
        shrink_weight,
        head_weight,
    )
    (
        token,
        predictions,
        tokens,
        logsum,
        sigma_sum,
        center_sum,
        second_sum,
        embedded,
        middle,
        turned,
        own,
        soon,
        later,
        rest,
    ) = front(place, lengths, series, flags, cotangent.reshape(rows, horizon), tables, weights, HEADS, PROGRAM[0][2])
    across = lift_weight.shape[0]
    joint_width = joint_weight.shape[1]

    def run_back(token, cost):
        return back(
            token,
            place,
            lengths,
            series,
            flags,
            tables,
            (lift_weight, mix_weight, skip_weight, gain_first, joint_weight, merge_weight),
            (tokens, logsum, sigma_sum, center_sum, second_sum, embedded, middle, turned),
            HEADS,
            cost,
        )

    at_own = {name: place * half for place, name in enumerate(OWN)}
    at_later = later_rows(width, horizon)
    at_rest = rest_rows(width)
    at_last = last_rows(width, across // 2, rows)
    if layout.paired:
        swap = lambda array: lax.ppermute(array, AXES, layout.flip(4))
        unit = width // UNITS
        soon_got, later_got, rest_got = swap(soon), swap(later), swap(rest)
        terms = {
            "A": ((0, at_own["branch"], 2, 0, 1, 2, half, "tiles", hidden),),
            "B": (
                (0, at_own["normed_two"], 4, at_later["normed_two"], 3, 4, at_later["upper"], "tiles", hidden),
                (0, at_own["resid"], 4, at_later["resid"], 3, 4, at_later["head"], "turned", horizon),
            ),
            "C": ((0, at_own["mixed"], 6, at_rest["mixed"], 5, 6, at_rest["middle"], "tiles", width),),
            "E": (
                (0, at_own["hidden"], 6, at_rest["hidden"], 9, 10, at_last["embed_tiles"], "tiles", width),
                (11, half, 10, at_last["pre"], 9, 10, at_last["tokens"], "low", across),
                (11, 0, 10, at_last["embed"], 9, 10, at_last["tokens"], "high", across),
                (0, 0, 0, 0, 9, 10, at_last["sums"], "sum", 8 * width // rows),
            ),
        }
        joint_names = [name for name in ORDERS if name.startswith("D")]
        first = 0
        for name in joint_names:
            span = JOINT_TILES[name] * BLOCK
            terms[name] = ((0, at_own["normed_one"], 6, at_rest["normed_one"], 7, 8, first, "turned", span),)
            first += span
        arrays = [own, soon, soon_got, later, later_got, rest, rest_got]
        bundles, finished = {}, []
        for kind, names, cost in PROGRAM[1:]:
            if kind == "K":
                token, series_grad, joint, last, last_own = run_back(token, cost)
                arrays += [joint, swap(joint), last, swap(last), last_own]
            elif kind == "G":
                used = sorted({index for name in names for term in terms[name] for index in (term[0], *term[2:3], *term[4:6])})
                local = {
                    name: tuple(
                        (used.index(t[0]), t[1], used.index(t[2]), t[3], used.index(t[4]), used.index(t[5]), *t[6:])
                        for t in terms[name]
                    )
                    for name in names
                }
                token, fresh = start_bundles(
                    layout, token, place, [arrays[index] for index in used], names, local, unit, cost
                )
                bundles.update(fresh)
            else:
                token, joined = advance(
                    layout, token, place, [bundles.pop(name) for name in names], unit // 4, cost, finished
                )
                bundles["".join(names)] = joined
        columns = {}
        for names, wide in finished:
            begin = 0
            for name in names:
                span = tiles_of(terms[name]) * BLOCK
                columns[name] = wide[:, begin : begin + span]
                begin += span
        shrink_rows, merge_grad = columns["A"], columns["C"]
        grow_grad, head_grad = columns["B"][:, :hidden], columns["B"][:, hidden:]
        joint_grad = jnp.concatenate([columns[name] for name in joint_names], axis=1)
        mix_small = columns["E"]
        mix_grad = mix_small[:, :width]
        lift_rows = mix_small[:, width : width + across]
        skip_rows = mix_small[:, width + across : width + 2 * across]
        second_grad = mix_small[:, width + 2 * across]
        first_grad = mix_small[:, width + 2 * across + 1]
    else:
        _, series_grad, joint, last, last_own = run_back(token, 1.0)
        scatter = lambda left, right: lax.psum_scatter(
            dot_plain(left.astype(jnp.bfloat16), right.astype(jnp.bfloat16)), AXES, scatter_dimension=0, tiled=True
        )
        mine = lambda name: own[at_own[name] : at_own[name] + half]
        theirs = lambda name: (
            later[at_later[name] : at_later[name] + half]
            if name in at_later
            else rest[at_rest[name] : at_rest[name] + half]
        )
        tiles = lambda pack, first: whole_tiles(pack[first : first + width], rows)
        shrink_rows = scatter(whole_rows(mine("branch"), soon[:half]), tiles(soon, half))
        grow_grad = scatter(whole_rows(mine("normed_two"), theirs("normed_two")), tiles(later, at_later["upper"]))
        head_grad = scatter(
            whole_rows(mine("resid"), theirs("resid")), later[at_later["head"] : at_later["head"] + horizon].T
        )
        merge_grad = scatter(whole_rows(mine("mixed"), theirs("mixed")), tiles(rest, at_rest["middle"]))
        joint_grad = scatter(whole_rows(mine("normed_one"), theirs("normed_one")), joint.T)
        mix_grad = scatter(whole_rows(mine("hidden"), theirs("hidden")), tiles(last, at_last["embed_tiles"]))
        lift_rows = scatter(whole_rows(last_own[half:], last[at_last["pre"] : at_last["pre"] + half]), tokens)
        skip_rows = scatter(whole_rows(last_own[:half], last[at_last["embed"] : at_last["embed"] + half]), tokens)
        sums = whole_tiles(last[at_last["sums"] : at_last["end"]].reshape(-1, rows), 8)
        sums = lax.psum_scatter(sums[:2].T, AXES, scatter_dimension=0, tiled=True)
        second_grad, first_grad = sums[:, 0], sums[:, 1]
    return (
        predictions.reshape(count, patches, horizon),
        series_grad,
        lift_rows.T,
        mix_grad,
        skip_rows.T,
        first_grad,
        joint_grad,
        merge_grad,
        second_grad,
        grow_grad,
        shrink_rows.T,
        head_grad,
    )


def solution(mesh):
    both = P(AXES)
    in_specs = (both, both, both) + (P(),) * 10 + (both,)
    out_specs = (
        P(AXES, None, None),
        P(AXES, None),
        P(None, AXES),
        P(AXES, None),
        P(None, AXES),
        P(AXES),
        P(AXES, None),
        P(AXES, None),
        P(AXES),
        P(AXES, None),
        P(None, AXES),
        P(AXES, None),
    )
    return jax.shard_map(
        functools.partial(per_device, Layout(mesh.shape)),
        mesh=mesh,
        in_specs=in_specs,
        out_specs=out_specs,
        check_vma=False,
    )
```

```python
import functools

import jax
import jax.numpy as jnp
import numpy as np
from jax import lax
from jax.experimental import pallas as pl
from jax.experimental.pallas import tpu as pltpu
from jax.sharding import PartitionSpec as P

HEADS = 16
BLOCK = 128

epsilon = 1e-06
masked_value = -1000000000.0
AXES = ("wide", "narrow")


def rotary_tables(patches, head_dim, count):
    exponent = np.arange(head_dim // 2, dtype=np.float32) * np.float32(2.0 / head_dim)
    frequency = np.float32(10000.0) ** (-exponent)
    angles = frequency[:, None] * np.arange(patches, dtype=np.float32)[None, :]
    angles = np.tile(np.concatenate([angles, angles], axis=0), (1, count))
    return jnp.asarray(np.cos(angles)), jnp.asarray(np.sin(angles))


VMEM_GRADIENT = 60
VMEM_COMBINE = 32
ORDERS = {"A": "abY", "B": "zab", "C": "azb", "E": "abz", "D1": "abz", "D2": "azb"}
JOINT_TILES = {"D1": 15, "D2": 15}
PROGRAM = (
    ("F", (), 5),
    ("G", ("A", ), 25),
    ("G", ("B", ), 18),
    ("G", ("C", ), 2),
    ("K", (), 5),
    ("+", ("A", ), 40),
    ("+", ("C", ), 0.3),
    ("G", ("D2", ), 1),
    ("+", ("B", ), 3),
    ("+", ("A", ), 18),
    ("G", ("D1", ), 1),
    ("G", ("E", ), 3),
    ("+", ("D2", ), 12),
    ("+", ("B", ), 8),
    ("+", ("C", ), 0),
    ("+", ("A", ), 2),
    ("+", ("D1", ), 8),
    ("+", ("D2", ), 1),
    ("+", ("E", ), 18),
    ("+", ("C", ), 3),
    ("+", ("B", ), 0),
    ("+", ("D1", ), 1),
    ("+", ("C", ), 1),
    ("+", ("E", ), 1),
    ("+", ("B", ), 2),
    ("+", ("D1", ), 3),
    ("+", ("D2", ), 0),
    ("+", ("B", ), 0),
    ("+", ("E", ), 2),
    ("+", ("C", ), 1),
    ("+", ("D1", ), 0),
    ("+", ("D2", ), 2),
    ("+", ("E", ), 2),
    ("+", ("D1", ), 1),
    ("+", ("D2", ), 2),
    ("+", ("E", ), 3),
)


def dot_plain(left_side, right_side):
    return jnp.dot(left_side, right_side, preferred_element_type=jnp.float32)


def dot_over(left_side, right_side, left_axis, right_axis):
    return lax.dot_general(
        left_side,
        right_side,
        (((left_axis,), (right_axis,)), ((), ())),
        preferred_element_type=jnp.float32,
    )


def dot_exact(left_side, right_side):
    return jnp.dot(
        left_side, right_side, preferred_element_type=jnp.float32, precision=lax.Precision.HIGHEST
    )


def logistic(values):
    return 1.0 / (1.0 + jnp.exp(-values))


def quotient(values, by):
    return lax.shift_right_logical(values, jnp.int32(by.bit_length() - 1))


def remainder(values, by):
    return values & (by - 1)


def iota(shape, axis):
    return lax.broadcasted_iota(jnp.int32, shape, axis)


def series_statistics(lengths_ref, series_ref, flags_ref, patch_len):
    count, points = series_ref.shape
    patches = points // patch_len
    values = series_ref[...]
    kept = 1.0 - flags_ref[...].astype(jnp.float32)
    starts = jnp.zeros((count, 1), jnp.int32)
    row = iota((count, 1), 0)
    for at in range(count):
        starts = jnp.where(row == at, patches - lengths_ref[at], starts)
    hot = (quotient(iota((count, points), 1), patch_len) == starts).astype(jnp.float32)
    hot_kept = hot * kept
    kept_count = jnp.maximum(jnp.sum(hot_kept, axis=1, keepdims=True), 1.0)
    center = jnp.sum(hot_kept * values, axis=1, keepdims=True) / kept_count
    shifted = values - center
    spread = jnp.sum(hot_kept * shifted * shifted, axis=1, keepdims=True) / kept_count
    sigma = jnp.sqrt(jnp.maximum(spread, 1.0))
    return kept, starts, hot_kept, kept_count, center, shifted, spread, sigma


def belongs(rows, count, patches, kind):
    return (quotient(iota((rows, count), 0), patches) == iota((rows, count), 1)).astype(kind)


def belongs_back(rows, count, patches, kind):
    return (quotient(iota((count, rows), 1), patches) == iota((count, rows), 0)).astype(kind)


def own_patch(rows, points, patches, patch_len):
    return quotient(iota((rows, points), 1), patch_len) == remainder(iota((rows, points), 0), patches)


def turn_half(values):
    half = values.shape[0] // 2
    return jnp.concatenate([-values[half:], values[:half]], axis=0)


def turn_half_back(values):
    half = values.shape[0] // 2
    return jnp.concatenate([values[half:], -values[:half]], axis=0)


def split_rows(place_ref, turned, other_ref, own_ref, first, units):
    core = place_ref[0]
    unit = turned.shape[0] // units
    for at in range(units // 2):
        mine = pl.multiple_of((2 * at + core) * unit, 16)
        theirs = pl.multiple_of((2 * at + 1 - core) * unit, 16)
        own_ref[at * unit : (at + 1) * unit, :] = turned[pl.ds(mine, unit), :].astype(jnp.float32)
        other_ref[first + at * unit : first + (at + 1) * unit, :] = turned[pl.ds(theirs, unit), :].astype(jnp.float32)


def put_tiles(ref, first, values):
    rows, width = values.shape
    for at in range(width // rows):
        ref[first + at * rows : first + (at + 1) * rows, :] = values[:, at * rows : (at + 1) * rows].astype(jnp.float32)


UNITS = 8
TOKEN = jax.ShapeDtypeStruct((8, 128), jnp.float32)


def expect(microseconds):
    return pl.CostEstimate(flops=int(microseconds * 1.15e9), bytes_accessed=0, transcendentals=0)


OWN = ("branch", "normed_two", "resid", "mixed", "normed_one", "hidden")


def stack_rows(*heights):
    places, at = {}, 0
    for name, height in heights:
        places[name] = at
        at += height
    places["end"] = at
    return places


def later_rows(width, horizon):
    half = width // 2
    return stack_rows(("normed_two", half), ("upper", width), ("resid", half), ("head", horizon))


def rest_rows(width):
    half = width // 2
    return stack_rows(
        ("mixed", half),
        ("middle", width),
        ("normed_one", half),
        ("hidden", half),
    )


def last_rows(width, patch_len, rows):
    half = width // 2
    return stack_rows(
        ("embed_tiles", width),
        ("embed", half),
        ("pre", half),
        ("tokens", 2 * patch_len),
        ("sums", 8 * width // rows),
    )


def front_kernel(
    heads,
    lengths_ref,
    place_ref,
    series_ref,
    flags_ref,
    cotangent_ref,
    gain_first_ref,
    gain_second_ref,
    cosine_ref,
    sine_ref,
    lift_hbm,
    mix_hbm,
    skip_hbm,
    joint_hbm,
    merge_hbm,
    grow_hbm,
    shrink_hbm,
    head_hbm,
    token_ref,
    predictions_ref,
    tokens_out,
    logsum_out,
    sigma_sum_out,
    center_sum_out,
    second_out,
    embedded_hbm,
    middle_hbm,
    turned_hbm,
    own_hbm,
    soon_hbm,
    later_hbm,
    rest_hbm,
    lift_ref,
    mix_ref,
    skip_ref,
    joint_ref,
    merge_ref,
    grow_ref,
    shrink_ref,
    head_ref,
    embedded_ref,
    middle_ref,
    joint_turned,
    turned_ref,
    mixed_turned,
    allowed_ref,
    resid_ref,
    upper_ref,
    back_ref,
    flip_ref,
    own,
    soon,
    later,
    rest,
    load_sem,
    store_sem,
):
    rows, width = embedded_ref.shape
    count, points = series_ref.shape
    patches = rows // count
    patch_len = points // patches
    head_dim = width // heads
    half_rows = width // 2
    wide = cotangent_ref.shape[1]
    del token_ref
    loads = [
        pltpu.make_async_copy(lift_hbm, lift_ref, load_sem.at[0]),
        pltpu.make_async_copy(skip_hbm, skip_ref, load_sem.at[1]),
        pltpu.make_async_copy(mix_hbm, mix_ref, load_sem.at[2]),
    ]
    for at in range(3):
        loads.append(
            pltpu.make_async_copy(joint_hbm.at[:, pl.ds(at * width, width)], joint_ref.at[at], load_sem.at[3 + at])
        )
    for at, (source, target) in enumerate(
        ((merge_hbm, merge_ref), (head_hbm, head_ref), (shrink_hbm, shrink_ref), (grow_hbm, grow_ref))
    ):
        loads.append(pltpu.make_async_copy(source, target, load_sem.at[6 + at]))
    for copy in loads:
        copy.start()
    stores = []

    def store(source, target, first=0, count=None):
        span = pl.ds(first, source.shape[0] - first if count is None else count)
        copy = pltpu.make_async_copy(source.at[span], target.at[span], store_sem.at[len(stores)])
        copy.start()
        stores.append(copy)

    def split(turned, name, pack, at):
        first = OWN.index(name) * half_rows
        split_rows(place_ref, turned, pack, own.at[pl.ds(first, half_rows)], at, UNITS)
        store(own, own_hbm, first, half_rows)

    places = later_rows(width, wide) | rest_rows(width)

    kept, starts, _, _, center, shifted, _, sigma = series_statistics(lengths_ref, series_ref, flags_ref, patch_len)
    scaled = (shifted / sigma * kept).astype(jnp.bfloat16)
    flag_values = flags_ref[...].astype(jnp.float32).astype(jnp.bfloat16)
    spread_out = belongs(rows, count, patches, jnp.bfloat16)
    inside = own_patch(rows, points, patches, patch_len)
    lane = iota((points, 2 * patch_len), 1)
    point = remainder(iota((points, 2 * patch_len), 0), patch_len)
    fold_left = (lane == point).astype(jnp.bfloat16)
    fold_right = (lane == point + patch_len).astype(jnp.bfloat16)
    left = jnp.where(inside, dot_plain(spread_out, scaled), 0.0).astype(jnp.bfloat16)
    right = jnp.where(inside, dot_plain(spread_out, flag_values), 0.0).astype(jnp.bfloat16)
    tokens = (dot_plain(left, fold_left) + dot_plain(right, fold_right)).astype(jnp.bfloat16)
    tokens_out[...] = tokens
    spread_exact = belongs(rows, count, patches, jnp.float32)
    sigma_rows = dot_exact(spread_exact, jnp.broadcast_to(sigma, (count, wide)))
    center_rows = dot_exact(spread_exact, jnp.broadcast_to(center, (count, wide)))
    starts_rows = dot_exact(spread_exact, jnp.broadcast_to(starts.astype(jnp.float32), (count, wide)))
    patch_row = remainder(iota((rows, wide), 0), patches).astype(jnp.float32)
    valid = (patch_row >= starts_rows - 0.5).astype(jnp.float32)
    block = allowed_ref.shape[1]
    key_at = remainder(iota((rows, block), 0), block)
    query_at = iota((rows, block), 1)
    key_pos, query_pos = remainder(key_at, patches), remainder(query_at, patches)
    allowed_ref[...] = (
        (quotient(key_at, patches) == quotient(query_at, patches))
        & (key_pos <= query_pos)
        & ((key_pos.astype(jnp.float32) >= starts_rows[:, :1] - 0.5) | (key_pos == query_pos))
    ).astype(jnp.float32)

    loads[0].wait()
    hidden_pre = dot_plain(tokens, lift_ref[...])
    hidden_act = (hidden_pre * logistic(hidden_pre)).astype(jnp.bfloat16)
    flip_ref[...] = hidden_act.T
    split(flip_ref, "hidden", rest, places["hidden"])
    store(rest, rest_hbm, places["hidden"], half_rows)
    loads[1].wait()
    loads[2].wait()
    embedded = dot_plain(hidden_act, mix_ref[...]) + dot_plain(tokens, skip_ref[...])
    embedded_ref[...] = embedded
    store(embedded_ref, embedded_hbm)
    scale_one = lax.rsqrt(jnp.mean(embedded * embedded, axis=1, keepdims=True) + epsilon)
    normed_one = (embedded * scale_one * gain_first_ref[...][None, :]).astype(jnp.bfloat16)
    for at in range(3):
        loads[3 + at].wait()
        tile = rows
        for part in range(width // tile):
            result = dot_plain(normed_one, joint_ref[at, :, part * tile : (part + 1) * tile])
            joint_turned[at * width + part * tile : at * width + (part + 1) * tile, :] = result.T
    flip_ref[...] = normed_one.T
    split(flip_ref, "normed_one", rest, places["normed_one"])
    store(rest, rest_hbm, places["normed_one"], half_rows)

    scale = head_dim ** (-0.5)
    cosine, sine = cosine_ref[...], sine_ref[...]

    def one_head(head, _):
        begin = pl.multiple_of(head * head_dim, 16)
        query = joint_turned[pl.ds(begin, head_dim), :]
        key = joint_turned[pl.ds(width + begin, head_dim), :]
        value = joint_turned[pl.ds(2 * width + begin, head_dim), :].astype(jnp.bfloat16)
        query = (query * cosine + turn_half(query) * sine).astype(jnp.bfloat16)
        key = (key * cosine + turn_half(key) * sine).astype(jnp.bfloat16)
        turned_ref[pl.ds(begin, head_dim), :] = query
        turned_ref[pl.ds(width + begin, head_dim), :] = key
        turned_ref[pl.ds(2 * width + begin, head_dim), :] = value
        mixed, sums = [], []
        for at in range(rows // block):
            span = slice(at * block, (at + 1) * block)
            scores = dot_over(key[:, span], query[:, span], 0, 0) * scale
            scores = jnp.where(allowed_ref[span, :] > 0.5, scores, masked_value)
            top = jnp.max(scores, axis=0, keepdims=True)
            raised = jnp.exp(scores - top)
            total = jnp.sum(raised, axis=0, keepdims=True)
            sums.append(top + jnp.log(total))
            probs = (raised / total).astype(jnp.bfloat16)
            mixed.append(dot_plain(value[:, span], probs))
        logsum_out[pl.ds(head, 1), :] = jnp.concatenate(sums, axis=1)
        mixed_turned[pl.ds(begin, head_dim), :] = jnp.concatenate(mixed, axis=1).astype(jnp.bfloat16)
        return 0

    lax.fori_loop(0, heads, one_head, 0, unroll=2)
    store(turned_ref, turned_hbm)
    split(mixed_turned, "mixed", rest, places["mixed"])
    store(rest, rest_hbm, places["mixed"], half_rows)
    mixed = mixed_turned[...].T
    loads[6].wait()
    resid_one = embedded_ref[...] + dot_plain(mixed, merge_ref[...])
    resid_ref[...] = resid_one
    scale_two = lax.rsqrt(jnp.mean(resid_one * resid_one, axis=1, keepdims=True) + epsilon)
    normed_two = (resid_one * scale_two * gain_second_ref[...][None, :]).astype(jnp.bfloat16)
    flip_ref[...] = normed_two.T
    split(flip_ref, "normed_two", later, places["normed_two"])
    store(later, later_hbm, places["normed_two"], half_rows)

    outer = cotangent_ref[...] * valid
    head_back = (outer * sigma_rows).astype(jnp.bfloat16)
    loads[7].wait()
    resid_back = dot_over(head_back, head_ref[...], 1, 1)
    back_ref[...] = resid_back
    branch_back = resid_back.astype(jnp.bfloat16)
    flip_ref[...] = branch_back.T
    split(flip_ref, "branch", soon, 0)

    loads[9].wait()
    upper_pre = dot_plain(normed_two, grow_ref[...])
    upper_ref[...] = upper_pre
    active = (upper_pre * logistic(upper_pre)).astype(jnp.bfloat16)
    put_tiles(soon, half_rows, active)
    store(soon, soon_hbm)
    loads[8].wait()
    upper_pre = upper_ref[...]
    gate = logistic(upper_pre)
    slope = gate * (1.0 + upper_pre * (1.0 - gate))
    upper_back = (dot_over(branch_back, shrink_ref[...], 1, 1) * slope).astype(jnp.bfloat16)
    put_tiles(later, places["upper"], upper_back)
    store(later, later_hbm, places["upper"], width)
    resid_low = (resid_ref[...] + dot_plain(active, shrink_ref[...])).astype(jnp.bfloat16)
    flip_ref[...] = resid_low.T
    split(flip_ref, "resid", later, places["resid"])
    store(later, later_hbm, places["resid"], half_rows)
    later[places["head"] : places["head"] + wide, :] = head_back.astype(jnp.float32).T
    store(later, later_hbm, places["head"], wide)

    normed_back = dot_over(upper_back, grow_ref[...], 1, 1)
    resid_one = resid_ref[...]
    second_out[...] = jnp.sum(normed_back * resid_one * scale_two, axis=0, keepdims=True)
    through = normed_back * gain_second_ref[...][None, :]
    inner = jnp.mean(through * resid_one, axis=1, keepdims=True)
    middle = back_ref[...] + scale_two * through - resid_one * (scale_two * scale_two * scale_two * inner)
    middle_ref[...] = middle
    store(middle_ref, middle_hbm)
    put_tiles(rest, places["middle"], middle.astype(jnp.bfloat16))
    store(rest, rest_hbm, places["middle"], width)

    head_out = dot_plain(resid_low, head_ref[...])
    predictions_ref[...] = valid * (head_out * sigma_rows + center_rows)
    gather = belongs_back(rows, count, patches, jnp.float32)
    sigma_sum_out[...] = dot_exact(gather, outer * head_out)
    center_sum_out[...] = dot_exact(gather, outer)
    for copy in stores:
        copy.wait()


def front(place, lengths, series, flags, cotangent, tables, weights, heads, cost):
    lift, mix, skip, gain_first, joint, merge, gain_second, grow, shrink, head = weights
    rows, horizon = cotangent.shape
    width = mix.shape[0]
    half = width // 2
    count = series.shape[0]
    f32, bf16 = jnp.float32, jnp.bfloat16
    vmem = pl.BlockSpec(memory_space=pltpu.VMEM)
    smem = pl.BlockSpec(memory_space=pltpu.SMEM)
    hbm = pl.BlockSpec(memory_space=pl.ANY)
    shape = jax.ShapeDtypeStruct
    packs = [
        (len(OWN) * half, rows),
        (half + width, rows),
        (later_rows(width, horizon)["end"], rows),
        (rest_rows(width)["end"], rows),
    ]
    outs = [
        TOKEN,
        shape((rows, horizon), f32),
        shape((rows, lift.shape[0]), bf16),
        shape((heads, rows), f32),
        shape((count, horizon), f32),
        shape((count, horizon), f32),
        shape((1, width), f32),
        shape((rows, width), f32),
        shape((rows, width), f32),
        shape((3 * width, rows), bf16),
    ] + [shape(pack, f32) for pack in packs]
    scratch = [
        pltpu.VMEM(lift.shape, bf16),
        pltpu.VMEM(mix.shape, bf16),
        pltpu.VMEM(skip.shape, bf16),
        pltpu.VMEM((3, width, width), bf16),
        pltpu.VMEM(merge.shape, bf16),
        pltpu.VMEM(grow.shape, bf16),
        pltpu.VMEM(shrink.shape, bf16),
        pltpu.VMEM(head.shape, bf16),
        pltpu.VMEM((rows, width), f32),
        pltpu.VMEM((rows, width), f32),
        pltpu.VMEM((3 * width, rows), f32),
        pltpu.VMEM((3 * width, rows), bf16),
        pltpu.VMEM((width, rows), bf16),
        pltpu.VMEM((rows, BLOCK), f32),
        pltpu.VMEM((rows, width), f32),
        pltpu.VMEM((rows, width), f32),
        pltpu.VMEM((rows, width), f32),
        pltpu.VMEM((width, rows), bf16),
    ] + [pltpu.VMEM(pack, f32) for pack in packs]
    scratch += [pltpu.SemaphoreType.DMA((10,)), pltpu.SemaphoreType.DMA((18,))]
    return pl.pallas_call(
        functools.partial(front_kernel, heads),
        out_shape=outs,
        in_specs=[smem, smem] + [vmem] * 7 + [hbm] * 8,
        out_specs=[hbm] + [vmem] * 6 + [hbm] * 7,
        scratch_shapes=scratch,
        compiler_params=pltpu.CompilerParams(vmem_limit_bytes=62 * 1024 * 1024),
        cost_estimate=expect(cost),
    )(
        lengths,
        place,
        series,
        flags,
        cotangent,
        gain_first,
        gain_second,
        *tables,
        lift,
        mix,
        skip,
        joint,
        merge,
        grow,
        shrink,
        head,
    )


def back_kernel(
    heads,
    lengths_ref,
    place_ref,
    series_ref,
    flags_ref,
    gain_first_ref,
    cosine_ref,
    sine_ref,
    tokens_ref,
    logsum_ref,
    sigma_sum_ref,
    center_sum_ref,
    second_ref,
    middle_hbm,
    turned_hbm,
    embedded_hbm,
    lift_hbm,
    mix_hbm,
    skip_hbm,
    joint_hbm,
    merge_hbm,
    token_in,
    token_ref,
    series_grad_ref,
    joint_hbm_out,
    last_hbm,
    own_hbm,
    lift_ref,
    mix_ref,
    skip_ref,
    joint_ref,
    merge_ref,
    embedded_ref,
    middle_ref,
    turned_ref,
    mixed_turned,
    joint_turned,
    first_ref,
    allowed_ref,
    flip_ref,
    joint_pack,
    last,
    own,
    load_sem,
    store_sem,
):
    rows, width = embedded_ref.shape
    count, points = series_ref.shape
    patches = rows // count
    patch_len = points // patches
    head_dim = width // heads
    half_rows = width // 2
    del token_in, token_ref
    loads = [
        pltpu.make_async_copy(source, target, load_sem.at[at])
        for at, (source, target) in enumerate(
            (
                (merge_hbm, merge_ref),
                (joint_hbm, joint_ref),
                (embedded_hbm, embedded_ref),
                (mix_hbm, mix_ref),
                (lift_hbm, lift_ref),
                (skip_hbm, skip_ref),
                (middle_hbm, middle_ref),
                (turned_hbm, turned_ref),
            )
        )
    ]
    for at in (6, 0, 7, 1, 2, 3, 4, 5):
        loads[at].start()
    stores = []

    def store(source, target, first=0, count=None):
        span = pl.ds(first, source.shape[0] - first if count is None else count)
        copy = pltpu.make_async_copy(source.at[span], target.at[span], store_sem.at[len(stores)])
        copy.start()
        stores.append(copy)

    places = last_rows(width, patch_len, rows)

    kept, starts, hot_kept, kept_count, center, shifted, spread, sigma = series_statistics(
        lengths_ref, series_ref, flags_ref, patch_len
    )
    block = allowed_ref.shape[1]
    spread_exact = belongs(rows, count, patches, jnp.float32)
    starts_rows = dot_exact(spread_exact, jnp.broadcast_to(starts.astype(jnp.float32), (count, block)))
    key_at = remainder(iota((rows, block), 0), block)
    query_at = iota((rows, block), 1)
    key_pos, query_pos = remainder(key_at, patches), remainder(query_at, patches)
    allowed_ref[...] = (
        (quotient(key_at, patches) == quotient(query_at, patches))
        & (key_pos <= query_pos)
        & ((key_pos.astype(jnp.float32) >= starts_rows - 0.5) | (key_pos == query_pos))
    ).astype(jnp.float32)
    scale = head_dim ** (-0.5)
    cosine, sine = cosine_ref[...], sine_ref[...]
    loads[0].wait()
    loads[6].wait()
    mixed_turned[...] = dot_over(merge_ref[...], middle_ref[...].astype(jnp.bfloat16), 1, 1).astype(jnp.bfloat16)

    def unrotate(gradient):
        return gradient * cosine + turn_half_back(gradient * sine)

    def one_head(head, _):
        begin = pl.multiple_of(head * head_dim, 16)
        query = turned_ref[pl.ds(begin, head_dim), :]
        key = turned_ref[pl.ds(width + begin, head_dim), :]
        value = turned_ref[pl.ds(2 * width + begin, head_dim), :]
        upstream = mixed_turned[pl.ds(begin, head_dim), :]
        logsum = logsum_ref[pl.ds(head, 1), :]
        query_parts, key_parts, value_parts = [], [], []
        for at in range(rows // block):
            span = slice(at * block, (at + 1) * block)
            query_in, key_in, value_in, up = query[:, span], key[:, span], value[:, span], upstream[:, span]
            scores = dot_over(key_in, query_in, 0, 0) * scale
            scores = jnp.where(allowed_ref[span, :] > 0.5, scores, masked_value)
            probs = jnp.exp(scores - logsum[:, span])
            value_parts.append(dot_over(up, probs.astype(jnp.bfloat16), 1, 1))
            probs_back = dot_over(value_in, up, 0, 0)
            inner = jnp.sum(probs * probs_back, axis=0, keepdims=True)
            scores_back = (probs * (probs_back - inner) * scale).astype(jnp.bfloat16)
            query_parts.append(dot_plain(key_in, scores_back))
            key_parts.append(dot_over(query_in, scores_back, 1, 1))
        for at, parts in enumerate((query_parts, key_parts, value_parts)):
            result = jnp.concatenate(parts, axis=1)
            if at < 2:
                result = unrotate(result)
            result = result.astype(jnp.bfloat16)
            joint_turned[pl.ds(at * width + begin, head_dim), :] = result
            joint_pack[pl.ds(at * width + begin, head_dim), :] = result.astype(jnp.float32)
        return 0

    loads[7].wait()
    lax.fori_loop(0, heads, one_head, 0, unroll=8)
    store(joint_pack, joint_hbm_out)
    loads[1].wait()
    tile = rows
    for part in range(width // tile):
        span = slice(part * tile, (part + 1) * tile)
        first_ref[:, span] = dot_plain(joint_ref[span, :], joint_turned[...]).T
    loads[2].wait()
    embedded = embedded_ref[...]
    first_back = first_ref[...]
    scale_one = lax.rsqrt(jnp.mean(embedded * embedded, axis=1, keepdims=True) + epsilon)
    first_sum = jnp.sum(first_back * embedded * scale_one, axis=0, keepdims=True)
    through = first_back * gain_first_ref[...][None, :]
    inner = jnp.mean(through * embedded, axis=1, keepdims=True)
    embed_low = (
        middle_ref[...] + scale_one * through - embedded * (scale_one * scale_one * scale_one * inner)
    ).astype(jnp.bfloat16)
    put_tiles(last, places["embed_tiles"], embed_low)
    flip_ref[...] = embed_low.T
    split_rows(place_ref, flip_ref, last, own.at[pl.ds(0, half_rows)], places["embed"], UNITS)
    store(last, last_hbm, places["embed_tiles"], width + half_rows)
    tokens = tokens_ref[...]
    loads[4].wait()
    hidden_pre = dot_plain(tokens, lift_ref[...])
    gate = logistic(hidden_pre)
    slope = gate * (1.0 + hidden_pre * (1.0 - gate))
    loads[3].wait()
    pre_back = (dot_over(embed_low, mix_ref[...], 1, 1) * slope).astype(jnp.bfloat16)
    flip_ref[...] = pre_back.T
    split_rows(place_ref, flip_ref, last, own.at[pl.ds(half_rows, half_rows)], places["pre"], UNITS)
    store(own, own_hbm)
    last[places["tokens"] : places["sums"], :] = tokens.astype(jnp.float32).T
    row = iota((8, width), 0)
    sums = jnp.where(row == 0, second_ref[...], jnp.where(row == 1, first_sum, 0.0))
    for at in range(width // rows):
        first = places["sums"] + 8 * at
        last[first : first + 8, :] = sums[:, at * rows : (at + 1) * rows]
    store(last, last_hbm, places["pre"])

    loads[5].wait()
    token_back = dot_over(pre_back, lift_ref[...], 1, 1) + dot_over(embed_low, skip_ref[...], 1, 1)
    lane = remainder(iota((2 * patch_len, points), 1), patch_len)
    unfold = (lane == iota((2 * patch_len, points), 0)).astype(jnp.float32)
    inside = own_patch(rows, points, patches, patch_len)
    spread_back_rows = jnp.where(inside, dot_exact(token_back, unfold), 0.0)
    scaled_back = dot_exact(belongs_back(rows, count, patches, jnp.float32), spread_back_rows)
    kept_back = scaled_back * kept
    point_back = kept_back / sigma
    sigma_back = jnp.sum(sigma_sum_ref[...], axis=1, keepdims=True)
    center_back = jnp.sum(center_sum_ref[...], axis=1, keepdims=True)
    center_total = center_back - jnp.sum(point_back, axis=1, keepdims=True)
    sigma_total = sigma_back - jnp.sum(kept_back * shifted, axis=1, keepdims=True) / (sigma * sigma)
    spread_grad = jnp.where(spread > 1.0, sigma_total * 0.5 / sigma, 0.0)
    offset_sum = jnp.sum(hot_kept * 2.0 * shifted, axis=1, keepdims=True)
    center_all = center_total - spread_grad * offset_sum / kept_count
    series_grad_ref[...] = point_back + hot_kept * (center_all + 2.0 * shifted * spread_grad) / kept_count
    for copy in stores:
        copy.wait()


def back(token, place, lengths, series, flags, tables, weights, kept_values, heads, cost):
    lift, mix, skip, gain_first, joint, merge = weights
    tokens, logsum, sigma_sum, center_sum, second_sum, embedded, middle, turned = kept_values
    rows, width = embedded.shape
    half = width // 2
    f32, bf16 = jnp.float32, jnp.bfloat16
    vmem = pl.BlockSpec(memory_space=pltpu.VMEM)
    smem = pl.BlockSpec(memory_space=pltpu.SMEM)
    hbm = pl.BlockSpec(memory_space=pl.ANY)
    shape = jax.ShapeDtypeStruct
    packs = [(3 * width, rows), (last_rows(width, lift.shape[0] // 2, rows)["end"], rows), (2 * half, rows)]
    scratch = [
        pltpu.VMEM(lift.shape, bf16),
        pltpu.VMEM(mix.shape, bf16),
        pltpu.VMEM(skip.shape, bf16),
        pltpu.VMEM(joint.shape, bf16),
        pltpu.VMEM(merge.shape, bf16),
        pltpu.VMEM((rows, width), f32),
        pltpu.VMEM((rows, width), f32),
        pltpu.VMEM((3 * width, rows), bf16),
        pltpu.VMEM((width, rows), bf16),
        pltpu.VMEM((3 * width, rows), bf16),
        pltpu.VMEM((rows, width), f32),
        pltpu.VMEM((rows, BLOCK), f32),
        pltpu.VMEM((width, rows), bf16),
    ] + [pltpu.VMEM(pack, f32) for pack in packs]
    scratch += [pltpu.SemaphoreType.DMA((8,)), pltpu.SemaphoreType.DMA((4,))]
    return pl.pallas_call(
        functools.partial(back_kernel, heads),
        out_shape=[TOKEN, shape(series.shape, f32)] + [shape(pack, f32) for pack in packs],
        in_specs=[smem, smem] + [vmem] * 10 + [hbm] * 9,
        out_specs=[hbm, vmem] + [hbm] * 3,
        scratch_shapes=scratch,
        compiler_params=pltpu.CompilerParams(vmem_limit_bytes=62 * 1024 * 1024),
        cost_estimate=expect(cost),
    )(
        lengths,
        place,
        series,
        flags,
        gain_first,
        *tables,
        tokens,
        logsum,
        sigma_sum,
        center_sum,
        second_sum,
        middle,
        turned,
        embedded,
        lift,
        mix,
        skip,
        joint,
        merge,
        token,
    )


def gradient_kernel(place_ref, *refs, pieces, arrays, unit):
    sources = refs[:arrays]
    token_ref, outputs = refs[arrays + 1], refs[arrays + 2 : arrays + 2 + 2 * len(pieces)]
    result_ref, left_raw, left_ref, right_raw, load_sem, store_sem = refs[arrays + 2 + 2 * len(pieces) :]
    del token_ref
    total = 4 * unit
    rows = left_raw.shape[2]
    loads, stores, lefts, rights = [], [], {}, []

    def load(source, first, target):
        copy = pltpu.make_async_copy(sources[source].at[pl.ds(first, target.shape[0])], target, load_sem.at[len(loads)])
        copy.start()
        loads.append(copy)
        return copy

    place = 0
    for _, terms in pieces:
        for own, own_row, other, other_row, near, far, row, kind, width in terms:
            key = (own, own_row, other, other_row)
            if kind != "sum" and key not in lefts:
                at = len(lefts)
                copies = [load(own, own_row, left_raw.at[2 * at]), load(other, other_row, left_raw.at[2 * at + 1])]
                lefts[key] = (at, copies)
            tiles = []
            for tile in range(0, width, rows):
                size = min(rows, width - tile)
                spots = [right_raw.at[pl.ds(place + side * size, size)] for side in (0, 1)]
                place += 2 * size
                tiles.append((size, spots, [load(side, row + tile, spot) for side, spot in zip((near, far), spots)]))
            rights.append(tiles)
    waited = set()
    number = 0
    tile_at = 0
    for order, (axis, terms) in enumerate(pieces):
        core = place_ref[0]
        stride, across = 1 + core, 2 - core
        if axis == "z":
            height, mine = unit // 2, place_ref[3] & 1
            groups = [stride * a + across * b for b in (0, 1) for a in (0, 1)]
            starts = [group * unit + half * height for half in (1 - mine, mine) for group in groups]
        else:
            height, mine = unit, place_ref[1]
            starts = [(stride * side + across * other) * unit for side in (1 - mine, mine) for other in (0, 1)]
        out_tile = 0

        def store(count):
            for half in (0, 1):
                copy = pltpu.make_async_copy(
                    result_ref.at[pl.ds(tile_at, count), pl.ds(half * total // 2, total // 2)],
                    outputs[2 * order + half].at[pl.ds(out_tile, count)],
                    store_sem.at[len(stores)],
                )
                copy.start()
                stores.append(copy)

        held = None
        for own, own_row, other, other_row, _, _, _, kind, width in terms:
            tiles = rights[number]
            number += 1
            if kind == "sum":
                for _, spots, copies in tiles:
                    for copy in copies:
                        copy.wait()
                both = tiles[0][1][0][...] + tiles[0][1][1][...]
                lanes = jnp.concatenate([both[part : part + 8, :] for part in range(0, width, 8)], axis=1)
                tall = jnp.concatenate([lanes, jnp.zeros((BLOCK - 8, lanes.shape[1]), jnp.float32)], axis=0).T
                unit_rows = tall.reshape(UNITS // 2, 2, unit, BLOCK)
                spare = left_raw.at[left_raw.shape[0] - 1]
                spare[:, :BLOCK] = jnp.where(place_ref[0] == 0, unit_rows[:, 0], unit_rows[:, 1]).reshape(total, BLOCK)
                for slot, first in enumerate(starts):
                    result_ref[tile_at, slot * height : (slot + 1) * height, :] = spare[
                        pl.ds(pl.multiple_of(first, 16), height), :BLOCK
                    ]
                store(1)
                tile_at += 1
                out_tile += 1
                continue
            at, copies = lefts[(own, own_row, other, other_row)]
            if at not in waited:
                waited.add(at)
                for copy in copies:
                    copy.wait()
            if held != at:
                held = at
                for slot, first in enumerate(starts):
                    first = pl.multiple_of(first, 16)
                    span = slice(slot * height, (slot + 1) * height)
                    for side in (0, 1):
                        left_ref[order % 2, span, side * rows : (side + 1) * rows] = left_raw[
                            2 * at + side, pl.ds(first, height), :
                        ].astype(jnp.bfloat16)
            left = left_ref[order % 2]
            for size, spots, copies in tiles:
                for copy in copies:
                    copy.wait()
                near, far = (spot[...].astype(jnp.bfloat16) for spot in spots)
                if kind == "tiles":
                    result = dot_plain(left, jnp.concatenate([near, far], axis=0))
                else:
                    right = jnp.concatenate([near, far], axis=1)
                    if kind != "turned":
                        blank = jnp.zeros_like(right)
                        right = jnp.concatenate((right, blank) if kind == "low" else (blank, right), axis=0)
                    result = dot_over(left, right, 1, 1)
                count = result.shape[1] // BLOCK
                for part in range(count):
                    piece = result[:, part * BLOCK : (part + 1) * BLOCK]
                    if kind == "high":
                        result_ref[tile_at + part] += piece
                    else:
                        result_ref[tile_at + part] = piece
                if kind != "low":
                    store(count)
                    tile_at += count
                    out_tile += count
    for copy in stores:
        copy.wait()


def tiles_of(terms):
    widths = {"low": 0, "high": BLOCK, "sum": BLOCK}
    return sum(widths.get(term[7], term[8]) for term in terms) // BLOCK


def weight_gradient(token, place, arrays, pieces, unit, cost):
    rows = arrays[0].shape[1]
    total = 4 * unit
    hbm = pl.BlockSpec(memory_space=pl.ANY)
    vmem = pl.BlockSpec(memory_space=pltpu.VMEM)
    counts = [tiles_of(terms) for _, terms in pieces]
    every = [term for _, terms in pieces for term in terms]
    lefts = len({term[:4] for term in every if term[7] != "sum"})
    copies = 2 * lefts + sum(2 * (-(-term[8] // rows)) for term in every)
    shapes = [jax.ShapeDtypeStruct((count, total // 2, BLOCK), jnp.float32) for count in counts for _ in (0, 1)]
    results = pl.pallas_call(
        functools.partial(gradient_kernel, pieces=pieces, arrays=len(arrays), unit=unit),
        in_specs=[pl.BlockSpec(memory_space=pltpu.SMEM)] + [hbm] * (len(arrays) + 1),
        out_specs=[hbm] * (1 + len(shapes)),
        scratch_shapes=[
            pltpu.VMEM((sum(counts), total, BLOCK), jnp.float32),
            pltpu.VMEM((2 * lefts + 1, total, rows), jnp.float32),
            pltpu.VMEM((2, total, 2 * rows), jnp.bfloat16),
            pltpu.VMEM((2 * sum(term[8] for term in every), rows), jnp.float32),
            pltpu.SemaphoreType.DMA((copies,)),
            pltpu.SemaphoreType.DMA((copies,)),
        ],
        out_shape=[TOKEN] + shapes,
        compiler_params=pltpu.CompilerParams(vmem_limit_bytes=VMEM_GRADIENT * 1024 * 1024),
        cost_estimate=expect(cost),
    )(place, *arrays, token)
    return results[0], [results[1 + 2 * at : 3 + 2 * at] for at in range(len(pieces))]


def combine_kernel(place_ref, *refs, inputs, parts, which, last, spread, passed):
    total = sum(inputs)
    sources = refs[:total]
    token_ref = refs[total + 1]
    results = refs[total + 2 : total + 2 + (len(inputs) if last else 1 if spread else parts)]
    scratch = refs[total + 2 + len(results) :]
    raws, sums, load_sem, store_sem = scratch[:total], scratch[total], scratch[total + 1], scratch[total + 2]
    del token_ref
    mine = place_ref[which] & (parts - 1)
    chosen = [step if spread else mine ^ ((step + 1) & (parts - 1)) for step in range(parts)]
    loads, stores = {}, []
    for step in range(parts):
        for at in range(total):
            copy = pltpu.make_async_copy(
                sources[at].at[:, :, chosen[step]], raws[at].at[step], load_sem.at[step * total + at]
            )
            copy.start()
            loads[step, at] = copy
    for step in range(parts):
        first = 0
        begin = 0
        for group, count in enumerate(inputs):
            for at in range(first, first + count):
                loads[step, at].wait()
            value = raws[first][step]
            for at in range(first + 1, first + count):
                if passed:
                    outside = jnp.logical_or(place_ref[3] == 0, place_ref[3] == 3)
                    value = jnp.where(outside, value, raws[at][step])
                else:
                    value = value + raws[at][step]
            tiles = value.shape[0]
            if last:
                fold = tiles // (results[group].shape[1] // BLOCK)
                tiles //= fold
                for tile in range(tiles):
                    piece = value[tile, 0]
                    for part in range(1, fold):
                        piece = piece + value[part * tiles + tile, 0]
                    results[group][:, tile * BLOCK : (tile + 1) * BLOCK] = piece
            else:
                sums[step, begin : begin + tiles] = value
                copy = pltpu.make_async_copy(
                    sums.at[step, pl.ds(begin, tiles)],
                    results[0].at[step, pl.ds(begin, tiles)] if spread else results[step].at[pl.ds(begin, tiles)],
                    store_sem.at[len(stores)],
                )
                copy.start()
                stores.append(copy)
            begin += tiles
            first += count
    for copy in stores:
        copy.wait()


def combine(token, place, groups, before, parts, which, cost, last=False, spread=False, fold=1, passed=False):
    rows = groups[0][0].shape[1]
    after = rows // (before * parts)
    flat = [array.reshape(array.shape[0], before, parts, after, BLOCK) for group in groups for array in group]
    tiles = [group[0].shape[0] for group in groups]
    hbm = pl.BlockSpec(memory_space=pl.ANY)
    vmem = pl.BlockSpec(memory_space=pltpu.VMEM)
    shape = jax.ShapeDtypeStruct
    if last:
        shapes = [shape((rows, count // fold * BLOCK), jnp.float32) for count in tiles]
    elif spread:
        shapes = [shape((parts, sum(tiles), before, after, BLOCK), jnp.float32)]
    else:
        shapes = [shape((sum(tiles), before, after, BLOCK), jnp.float32)] * parts
    results = pl.pallas_call(
        functools.partial(
            combine_kernel, inputs=tuple(len(group) for group in groups), parts=parts, which=which, last=last, spread=spread, passed=passed
        ),
        in_specs=[pl.BlockSpec(memory_space=pltpu.SMEM)] + [hbm] * (len(flat) + 1),
        out_specs=[hbm] + [vmem if last else hbm] * len(shapes),
        scratch_shapes=[pltpu.VMEM((parts, array.shape[0], before, after, BLOCK), jnp.float32) for array in flat]
        + [
            pltpu.VMEM((1,) * 5 if last else (parts, sum(tiles), before, after, BLOCK), jnp.float32),
            pltpu.SemaphoreType.DMA((parts * len(flat),)),
            pltpu.SemaphoreType.DMA((parts * len(groups),)),
        ],
        out_shape=[TOKEN] + shapes,
        compiler_params=pltpu.CompilerParams(vmem_limit_bytes=VMEM_COMBINE * 1024 * 1024),
        cost_estimate=expect(cost),
    )(place, *flat, token)
    if last or spread:
        return results[0], results[1:]
    return results[0], [result.reshape(sum(tiles), before * after, BLOCK) for result in results[1:]]


class Layout:
    def __init__(self, mesh_shape):
        self.wide = mesh_shape["wide"]
        self.narrow = mesh_shape["narrow"]
        self.total = self.wide * self.narrow
        self.paired = self.wide == 8 and self.narrow == 4

    def flip(self, bit):
        return [(i, i ^ bit) for i in range(self.total)]

    def middle(self):
        swapped = {1: 2, 2: 1}
        return [(i, (i & ~3) | swapped[i & 3] if i & 3 in swapped else i ^ 4) for i in range(self.total)]

    def across(self, first):
        return [(i, i ^ (8 if (i & 4 == 0) == first else 16)) for i in range(self.total)]

    def position(self):
        wide = lax.axis_index("wide")
        core, x, y = wide % 2, wide // 2 % 2, wide // 4 % 2
        places = (core, jnp.where(core == 0, x, y), jnp.where(core == 0, y, x), lax.axis_index("narrow"))
        if not self.paired:
            places = tuple(jnp.zeros_like(place) for place in places)
        return jnp.stack(places).astype(jnp.int32)


class Bundle:
    def __init__(self, names, plan, axes, groups, fold=1, passed=False):
        self.names, self.plan, self.axes, self.groups = names, plan, axes, groups
        self.fold, self.passed = fold, passed


def steps_of(order):
    plan = []
    for axis in order:
        plan += ["half", "middle", "part"] if axis == "z" else [axis]
    return plan


def move(layout, array, step):
    if step == "middle":
        pairs = layout.middle()
    else:
        pairs = layout.across(step == "a") if step in ("a", "b") else layout.flip(1)
    return lax.ppermute(array, AXES, pairs)


def start_bundles(layout, token, place, arrays, names, terms, unit, cost):
    plans = [steps_of(ORDERS[name]) for name in names]
    token, results = weight_gradient(
        token, place, arrays, tuple((ORDERS[name][0], terms[name]) for name in names), unit, cost
    )
    bundles = {}
    for name, plan, (send, keep) in zip(names, plans, results):
        step = plan.pop(0)
        axes = [axis for axis in ("b", "a", "half", "part") if axis != step]
        bundles[name] = Bundle([name], plan, axes, [[keep, move(layout, send, step)]])
    return token, bundles


def advance(layout, token, place, bundles, rows, cost, finished):
    plan, axes = bundles[0].plan, bundles[0].axes
    groups = [group for bundle in bundles for group in bundle.groups]
    names = [name for bundle in bundles for name in bundle.names]
    sizes = [group[0].shape[0] for group in groups]
    if not plan:
        token, results = combine(token, place, groups, 1, 1, 0, cost, last=True, fold=bundles[0].fold)
        wide = results[0] if len(results) == 1 else jnp.concatenate(results, axis=1)
        finished.append((names, wide))
        return token, None
    step, plan = plan[0], plan[1:]
    if step == "middle":
        token, (whole,) = combine(token, place, groups, 1, 1, 0, cost)
        return token, Bundle(names, plan, axes, [[whole, move(layout, whole, step)]], passed=True)
    if step == "Y":
        token, (whole,) = combine(token, place, groups, 1, 4, 0, cost, spread=True)
        got = lax.all_to_all(whole, "narrow", 0, 0, tiled=True)
        return token, Bundle(names, plan, [], [[got.reshape(4 * sum(sizes), rows, BLOCK)]], 4)
    at = axes.index(step)
    which = {"a": 1, "b": 2}.get(step, 3)
    token, (send, keep) = combine(token, place, groups, 2**at, 2, which, cost, passed=bundles[0].passed)
    return token, Bundle(names, plan, [axis for axis in axes if axis != step], [[keep, move(layout, send, step)]])


def whole_rows(own, other):
    unit = own.shape[0] // (UNITS // 2)
    pair = jnp.stack([own.reshape(-1, unit, own.shape[1]), other.reshape(-1, unit, own.shape[1])], axis=1)
    return pair.reshape(2 * own.shape[0], own.shape[1])


def whole_tiles(tiles, rows):
    return jnp.concatenate([tiles[at : at + rows] for at in range(0, tiles.shape[0], rows)], axis=1)


def per_device(
    layout,
    series,
    flags,
    lengths,
    lift_weight,
    mix_weight,
    skip_weight,
    gain_first,
    joint_weight,
    merge_weight,
    gain_second,
    grow_weight,
    shrink_weight,
    head_weight,
    cotangent,
):
    count = series.shape[0]
    patches, horizon = cotangent.shape[1:]
    width = mix_weight.shape[0]
    hidden = shrink_weight.shape[0]
    rows = count * patches
    half = width // 2
    tables = rotary_tables(patches, width // HEADS, count)
    place = layout.position()
    weights = (
        lift_weight,
        mix_weight,
        skip_weight,
        gain_first,
        joint_weight,
        merge_weight,
        gain_second,
        grow_weight,
        shrink_weight,
        head_weight,
    )
    (
        token,
        predictions,
        tokens,
        logsum,
        sigma_sum,
        center_sum,
        second_sum,
        embedded,
        middle,
        turned,
        own,
        soon,
        later,
        rest,
    ) = front(place, lengths, series, flags, cotangent.reshape(rows, horizon), tables, weights, HEADS, PROGRAM[0][2])
    across = lift_weight.shape[0]
    joint_width = joint_weight.shape[1]

    def run_back(token, cost):
        return back(
            token,
            place,
            lengths,
            series,
            flags,
            tables,
            (lift_weight, mix_weight, skip_weight, gain_first, joint_weight, merge_weight),
            (tokens, logsum, sigma_sum, center_sum, second_sum, embedded, middle, turned),
            HEADS,
            cost,
        )

    at_own = {name: place * half for place, name in enumerate(OWN)}
    at_later = later_rows(width, horizon)
    at_rest = rest_rows(width)
    at_last = last_rows(width, across // 2, rows)
    if layout.paired:
        swap = lambda array: lax.ppermute(array, AXES, layout.flip(4))
        unit = width // UNITS
        soon_got, later_got, rest_got = swap(soon), swap(later), swap(rest)
        terms = {
            "A": ((0, at_own["branch"], 2, 0, 1, 2, half, "tiles", hidden),),
            "B": (
                (0, at_own["normed_two"], 4, at_later["normed_two"], 3, 4, at_later["upper"], "tiles", hidden),
                (0, at_own["resid"], 4, at_later["resid"], 3, 4, at_later["head"], "turned", horizon),
            ),
            "C": ((0, at_own["mixed"], 6, at_rest["mixed"], 5, 6, at_rest["middle"], "tiles", width),),
            "E": (
                (0, at_own["hidden"], 6, at_rest["hidden"], 9, 10, at_last["embed_tiles"], "tiles", width),
                (11, half, 10, at_last["pre"], 9, 10, at_last["tokens"], "low", across),
                (11, 0, 10, at_last["embed"], 9, 10, at_last["tokens"], "high", across),
                (0, 0, 0, 0, 9, 10, at_last["sums"], "sum", 8 * width // rows),
            ),
        }
        joint_names = [name for name in ORDERS if name.startswith("D")]
        first = 0
        for name in joint_names:
            span = JOINT_TILES[name] * BLOCK
            terms[name] = ((0, at_own["normed_one"], 6, at_rest["normed_one"], 7, 8, first, "turned", span),)
            first += span
        arrays = [own, soon, soon_got, later, later_got, rest, rest_got]
        bundles, finished = {}, []
        for kind, names, cost in PROGRAM[1:]:
            if kind == "K":
                token, series_grad, joint, last, last_own = run_back(token, cost)
                arrays += [joint, swap(joint), last, swap(last), last_own]
            elif kind == "G":
                used = sorted({index for name in names for term in terms[name] for index in (term[0], *term[2:3], *term[4:6])})
                local = {
                    name: tuple(
                        (used.index(t[0]), t[1], used.index(t[2]), t[3], used.index(t[4]), used.index(t[5]), *t[6:])
                        for t in terms[name]
                    )
                    for name in names
                }
                token, fresh = start_bundles(
                    layout, token, place, [arrays[index] for index in used], names, local, unit, cost
                )
                bundles.update(fresh)
            else:
                token, joined = advance(
                    layout, token, place, [bundles.pop(name) for name in names], unit // 4, cost, finished
                )
                bundles["".join(names)] = joined
        columns = {}
        for names, wide in finished:
            begin = 0
            for name in names:
                span = tiles_of(terms[name]) * BLOCK
                columns[name] = wide[:, begin : begin + span]
                begin += span
        shrink_rows, merge_grad = columns["A"], columns["C"]
        grow_grad, head_grad = columns["B"][:, :hidden], columns["B"][:, hidden:]
        joint_grad = jnp.concatenate([columns[name] for name in joint_names], axis=1)
        mix_small = columns["E"]
        mix_grad = mix_small[:, :width]
        lift_rows = mix_small[:, width : width + across]
        skip_rows = mix_small[:, width + across : width + 2 * across]
        second_grad = mix_small[:, width + 2 * across]
        first_grad = mix_small[:, width + 2 * across + 1]
    else:
        _, series_grad, joint, last, last_own = run_back(token, 1.0)
        scatter = lambda left, right: lax.psum_scatter(
            dot_plain(left.astype(jnp.bfloat16), right.astype(jnp.bfloat16)), AXES, scatter_dimension=0, tiled=True
        )
        mine = lambda name: own[at_own[name] : at_own[name] + half]
        theirs = lambda name: (
            later[at_later[name] : at_later[name] + half]
            if name in at_later
            else rest[at_rest[name] : at_rest[name] + half]
        )
        tiles = lambda pack, first: whole_tiles(pack[first : first + width], rows)
        shrink_rows = scatter(whole_rows(mine("branch"), soon[:half]), tiles(soon, half))
        grow_grad = scatter(whole_rows(mine("normed_two"), theirs("normed_two")), tiles(later, at_later["upper"]))
        head_grad = scatter(
            whole_rows(mine("resid"), theirs("resid")), later[at_later["head"] : at_later["head"] + horizon].T
        )
        merge_grad = scatter(whole_rows(mine("mixed"), theirs("mixed")), tiles(rest, at_rest["middle"]))
        joint_grad = scatter(whole_rows(mine("normed_one"), theirs("normed_one")), joint.T)
        mix_grad = scatter(whole_rows(mine("hidden"), theirs("hidden")), tiles(last, at_last["embed_tiles"]))
        lift_rows = scatter(whole_rows(last_own[half:], last[at_last["pre"] : at_last["pre"] + half]), tokens)
        skip_rows = scatter(whole_rows(last_own[:half], last[at_last["embed"] : at_last["embed"] + half]), tokens)
        sums = whole_tiles(last[at_last["sums"] : at_last["end"]].reshape(-1, rows), 8)
        sums = lax.psum_scatter(sums[:2].T, AXES, scatter_dimension=0, tiled=True)
        second_grad, first_grad = sums[:, 0], sums[:, 1]
    return (
        predictions.reshape(count, patches, horizon),
        series_grad,
        lift_rows.T,
        mix_grad,
        skip_rows.T,
        first_grad,
        joint_grad,
        merge_grad,
        second_grad,
        grow_grad,
        shrink_rows.T,
        head_grad,
    )


def solution(mesh):
    both = P(AXES)
    in_specs = (both, both, both) + (P(),) * 10 + (both,)
    out_specs = (
        P(AXES, None, None),
        P(AXES, None),
        P(None, AXES),
        P(AXES, None),
        P(None, AXES),
        P(AXES),
        P(AXES, None),
        P(AXES, None),
        P(AXES),
        P(AXES, None),
        P(None, AXES),
        P(AXES, None),
    )
    return jax.shard_map(
        functools.partial(per_device, Layout(mesh.shape)),
        mesh=mesh,
        in_specs=in_specs,
        out_specs=out_specs,
        check_vma=False,
    )
```
